512 devices in a mesh: ctx: 64 (over z, y_hi, core), head: 8 (over y_lo, x).
Axes of the slice: x: 4, y: 8 (y_hi: 4, y_lo: 2; y = y_hi * 2 + y_lo), z: 8, core: 2. Of those that a mesh axis runs over, the one named last changes fastest.
Arguments:
- queries: bfloat16 [8192, 2048], P('ctx', 'head'), may hold values from -100 to 100
- keys: bfloat16 [8192, 2048], P('ctx', 'head'), may hold values from -50 to 50
- values: bfloat16 [8192, 2048], P('ctx', 'head'), may hold values from -6 to 6
- out_weight: bfloat16 [2048, 4096], P('head'), may hold values from -0.125 to 0.125
- mixed_grad: bfloat16 [8192, 4096], P('ctx', 'head'), may hold values from -6 to 6
- lengths: int32 [64], replicated, may hold values from 1 to 384, 8192 in all
- dilation: int32 [16], P('head'), may hold values from 1 to 8
Outputs:
- mixed: bfloat16 [8192, 4096], P('ctx', 'head')
- grad_queries: bfloat16 [8192, 2048], P('ctx', 'head')
- grad_keys: bfloat16 [8192, 2048], P('ctx', 'head')
- grad_values: bfloat16 [8192, 2048], P('ctx', 'head')
The draws below stay inside these ranges and needn't reach their ends.
Inputs may be any that keep to these rules, and one draw needn't show every extreme that they name: The lengths sum to 8192, and the longest document has exactly 384 tokens.
All inputs are finite; a program needn't handle non-finite values.
Results may differ from the reference program's by a relative error of at most 0.029.
Values may be sent and summed in bfloat16 or wider, within the bound.
No kernel may reach another device: no remote copies, remote signals or barrier semaphores. Data moves between devices by JAX's collectives and lax.ppermute only.
A program may use at most 64 MiB of HBM per device.

```python
import math
import jax
import jax.numpy as jnp
import numpy as np
from jax import lax

D = 4096
HEADS = 16
HD = 128
HALF = 32
MAXD = 8
TOK_DEV = 128
TOKENS = 8192
DOCS = 64


def draw_queries(key, part):
    drawn = jax.random.normal(jax.random.fold_in(key, 11), (TOKENS, HEADS * HD), jnp.float32)
    return drawn.astype(jnp.bfloat16)


def draw_keys(key, part):
    drawn = jax.random.normal(jax.random.fold_in(key, 23), (TOKENS, HEADS * HD), jnp.float32)
    return drawn.astype(jnp.bfloat16)


def plant(entries, stream_key, smallest, high):
    shape = entries.shape
    spot = [jax.random.randint(jax.random.fold_in(stream_key, axis), (), 0, shape[axis]) for axis in range(len(shape))]
    entries = entries.at[tuple(spot)].set(smallest)
    longest = shape.index(max(shape))
    spot[longest] = (spot[longest] + 1) % shape[longest]
    return entries.at[tuple(spot)].set(high)


def block_scale(own_key, dims, shards, smallest, high):
    def one(axis_at, blocks):
        draws = jax.random.uniform(jax.random.fold_in(jax.random.fold_in(own_key, 6), axis_at), (blocks,), jnp.float32, smallest / len(shards), high / len(shards))
        return jnp.repeat(jnp.exp(draws), dims[axis_at] // blocks).reshape((-1,) + (1,) * (len(dims) - axis_at - 1))

    factor_of = one(*shards[0])
    for cut in shards[1:]:
        factor_of = factor_of * one(*cut)
    return factor_of


def split_up(amount, total, most, slope):
    portions = [(1 << 20) // math.isqrt(rank ** slope) + 1 for rank in range(2, amount + 1)]
    spare, given = total - most - (amount - 1), [1] * (amount - 1)
    while spare > 0:
        free = [i for i in range(amount - 1) if given[i] < most]
        pool, budget = sum([portions[i] for i in free]), spare
        for i in free:
            extra = min(most - given[i], max(1, budget * portions[i] // pool), spare)
            given[i] = given[i] + extra
            spare = spare - extra
    return np.array([most] + given)


def ragged(stream_key, amount, total, most, skew):
    if amount == 2:
        one = jax.random.randint(stream_key, (), max(1, total - most), min(most, total - 1) + 1)
        return jnp.stack([one, total - one])
    sizes = jnp.asarray(split_up(amount, total, most, skew), jnp.int32)
    twos = (amount - 1) // 2
    source_of, taker = sizes[1:1 + 2 * twos:2], sizes[2:2 + 2 * twos:2]
    room = jnp.minimum(source_of - 1, most - taker)
    moved = jax.random.randint(jax.random.fold_in(stream_key, 1), (twos,), 0, 1 << 20) % (room + 1)
    sizes = sizes.at[1:1 + 2 * twos:2].set(source_of - moved).at[2:2 + 2 * twos:2].set(taker + moved)
    return sizes[jax.random.permutation(jax.random.fold_in(stream_key, 2), amount)]


def noise(key, shape, spread, bound, shards=(), kind=jnp.bfloat16):
    values = jax.random.normal(key, shape, jnp.float32) * spread
    if len(shards) > 0:
        values = block_scale(key, shape, shards, -0.22, 0.18) * values
    return jnp.clip(values, min=-bound, max=bound).astype(kind)


def setup_inputs(seed: int = 0) -> dict:
    key_of = jax.random.split(jax.random.key(seed), 8)
    return {
        "queries": draw_queries(jax.random.fold_in(key_of[7], 71), 0),
        "keys": draw_keys(jax.random.fold_in(key_of[7], 71), 0),
        "values": noise(key_of[2], (TOKENS, HEADS * HD), 1.0, 6.0, ((0, 64), (1, 8))),
        "out_weight": noise(key_of[3], (HEADS * HD, D), (HEADS * HD) ** -0.5, 0.125, ((0, 8),)),
        "mixed_grad": noise(key_of[4], (TOKENS, D), 1.0, 6.0, ((0, 64), (1, 8))),
        "lengths": ragged(key_of[5], DOCS, TOKENS, HALF * MAXD + TOK_DEV, 2).astype(jnp.int32),
        "dilation": plant(jax.random.randint(key_of[6], (HEADS,), 1, MAXD + 1), jax.random.fold_in(key_of[6], 1), 1, MAXD).astype(jnp.int32),
    }


def segment_of(positions, lengths):
    boundary = jnp.cumsum(lengths).astype(jnp.int32)
    return jnp.sum((positions[:, None] >= boundary[None, :]).astype(jnp.int32), axis=1)


def allowed(query_pos, key_pos, query_seg, key_seg, dilation, reach, total):
    offset_grid = query_pos[:, None] - key_pos[None, :]
    common = (query_seg[:, None] == key_seg[None, :]) & (key_pos[None, :] >= 0) & (key_pos[None, :] < total)
    common = common & (query_pos[:, None] >= 0) & (query_pos[:, None] < total)
    stride = dilation[:, None, None]
    within = (jnp.abs(offset_grid)[None] <= reach * stride) & (jnp.remainder(offset_grid[None], stride) == 0)
    return within & common[None]


def reference(queries, keys, values, out_weight, mixed_grad, lengths, dilation):
    total = queries.shape[0]
    margin = HALF * MAXD
    factor = HD ** -0.5
    window = TOK_DEV + 2 * margin
    blocks = total // TOK_DEV
    grad_attention = jnp.dot(mixed_grad, out_weight.T, preferred_element_type=jnp.float32).astype(jnp.bfloat16)

    def by_head(array):
        return array.reshape(total, HEADS, HD).transpose(1, 0, 2)

    def one_head(item):
        query_rows, key_rows, value_rows, grad_rows, spacing = item
        padding = ((margin, margin), (0, 0))
        key_padded = jnp.pad(key_rows, padding)
        value_padded = jnp.pad(value_rows, padding)
        zeros_pad = jnp.zeros((total + 2 * margin, HD), jnp.float32)

        def step(carry, block):
            key_acc, value_acc = carry
            start = (block * TOK_DEV).astype(jnp.int32)
            query_block = lax.dynamic_slice_in_dim(query_rows, start, TOK_DEV, 0)
            grad_block = lax.dynamic_slice_in_dim(grad_rows, start, TOK_DEV, 0)
            key_window = lax.dynamic_slice_in_dim(key_padded, start, window, 0)
            value_window = lax.dynamic_slice_in_dim(value_padded, start, window, 0)
            query_pos = start + jnp.arange(TOK_DEV, dtype=jnp.int32)
            key_pos = start - margin + jnp.arange(window, dtype=jnp.int32)
            mask = allowed(query_pos, key_pos, segment_of(query_pos, lengths), segment_of(key_pos, lengths), spacing[None], HALF, total)[0]
            scores = jnp.dot(query_block, key_window.T, preferred_element_type=jnp.float32) * factor
            top = jnp.max(jnp.where(mask, scores, -jnp.inf), axis=1)
            log_total = top + jnp.log(jnp.sum(jnp.where(mask, jnp.exp(scores - top[:, None]), 0.0), axis=1))
            weights = jnp.where(mask, jnp.exp(scores - log_total[:, None]), 0.0)
            probs = weights.astype(jnp.bfloat16)
            attention = jnp.dot(probs, value_window, preferred_element_type=jnp.float32).astype(jnp.bfloat16)
            delta = jnp.sum(grad_block.astype(jnp.float32) * attention.astype(jnp.float32), axis=1)
            grad_prob = jnp.dot(grad_block, value_window.T, preferred_element_type=jnp.float32)
            slopes = (weights * (grad_prob - delta[:, None])).astype(jnp.bfloat16)
            grad_query = (jnp.dot(slopes, key_window, preferred_element_type=jnp.float32) * factor).astype(jnp.bfloat16)
            key_term = jnp.dot(slopes.T, query_block, preferred_element_type=jnp.float32) * factor
            value_term = jnp.dot(probs.T, grad_block, preferred_element_type=jnp.float32)
            key_acc = lax.dynamic_update_slice_in_dim(key_acc, lax.dynamic_slice_in_dim(key_acc, start, window, 0) + key_term, start, 0)
            value_acc = lax.dynamic_update_slice_in_dim(value_acc, lax.dynamic_slice_in_dim(value_acc, start, window, 0) + value_term, start, 0)
            return (key_acc, value_acc), (attention, grad_query)

        (key_acc, value_acc), (attention, grad_query) = lax.scan(step, (zeros_pad, zeros_pad), jnp.arange(blocks, dtype=jnp.int32))
        grad_key = key_acc[margin:margin + total].astype(jnp.bfloat16)
        grad_value = value_acc[margin:margin + total].astype(jnp.bfloat16)
        return attention.reshape(total, HD), grad_query.reshape(total, HD), grad_key, grad_value

    results = lax.map(one_head, (by_head(queries), by_head(keys), by_head(values), by_head(grad_attention), dilation))

    def flat(array):
        return array.transpose(1, 0, 2).reshape(total, HEADS * HD)

    attention = flat(results[0])
    mixed = jnp.dot(attention, out_weight, preferred_element_type=jnp.float32).astype(jnp.bfloat16)
    return mixed, flat(results[1]), flat(results[2]), flat(results[3])
```

```python
import functools

import jax
import jax.numpy as jnp
from jax import lax
from jax.experimental import pallas as pl
from jax.experimental.pallas import tpu as pltpu
from jax.sharding import PartitionSpec as P

HALF = 32
BF = jnp.bfloat16
F32 = jnp.float32
VMEM = pl.BlockSpec(memory_space=pltpu.VMEM)
SMEM = pl.BlockSpec(memory_space=pltpu.SMEM)


def dot(a, b, dims):
    return lax.dot_general(a, b, (dims, ((), ())), preferred_element_type=F32)


def call(body, outs, ins, name, flops=0, scratch=()):
    moved = sum(x.size * x.dtype.itemsize for x in (*ins, *outs))
    return pl.pallas_call(
        body,
        out_shape=outs,
        in_specs=[SMEM if x.ndim == 1 else VMEM for x in ins],
        out_specs=[VMEM] * len(outs),
        scratch_shapes=scratch,
        compiler_params=pltpu.CompilerParams(vmem_limit_bytes=24 << 20),
        cost_estimate=pl.CostEstimate(flops=flops, bytes_accessed=moved, transcendentals=0),
        name=name,
    )(*ins)


def shape(dims, dtype):
    return jax.ShapeDtypeStruct(dims, dtype)


def pack_kernel(k_ref, v_ref, mg_ref, kv_ref, all_ref):
    w = k_ref.shape[1]
    kv_ref[:, :w] = k_ref[...]
    kv_ref[:, w:] = v_ref[...]
    for b in range(all_ref.shape[0]):
        all_ref[b] = mg_ref[...]


def document_codes(lens, row_pos, col_pos):
    n = lens.shape[1]
    down = lax.broadcasted_iota(jnp.int32, (n, n), 0)
    across = lax.broadcasted_iota(jnp.int32, (n, n), 1)
    wide = jnp.broadcast_to(lens, (n, n))
    ends_col = jnp.sum(jnp.where(across <= down, wide, 0.0), axis=1, keepdims=True)
    lens_col = jnp.sum(jnp.where(across == down, wide, 0.0), axis=1, keepdims=True)
    ends_row = jnp.sum(jnp.where(down <= across, lens_col, 0.0), axis=0, keepdims=True)
    row_doc = jnp.sum(jnp.where(row_pos >= ends_col, 1.0, 0.0), axis=0, keepdims=True)
    col_doc = jnp.sum(jnp.where(col_pos >= ends_row, 1.0, 0.0), axis=1, keepdims=True)
    return row_doc, col_doc


def forward_kernel(
    heads, total, where_ref, dil_ref, lens_ref, q_ref, prev_ref, own_ref, next_ref, w_ref,
    part_ref, weight_ref, attn_ref, win_ref,
):
    rows = q_ref.shape[0]
    width = q_ref.shape[1]
    hd = width // heads
    keys = win_ref.shape[0]
    slab = where_ref[0]
    core = lax.rem(slab, 2)
    six = [prev_ref, prev_ref, own_ref, own_ref, next_ref, next_ref]

    @pl.when(core == 0)
    def _():
        for i in range(5):
            win_ref[i * rows : (i + 1) * rows, :] = six[i][i % 2]

    @pl.when(core == 1)
    def _():
        for i in range(5):
            win_ref[i * rows : (i + 1) * rows, :] = six[i + 1][(i + 1) % 2]

    first = slab * rows
    row_idx = lax.broadcasted_iota(jnp.int32, (1, keys), 1) + (first - 2 * rows)
    col_idx = lax.broadcasted_iota(jnp.int32, (rows, 1), 0) + first
    row_pos, col_pos = row_idx.astype(F32), col_idx.astype(F32)
    row_doc, col_doc = document_codes(lens_ref[...].astype(F32), row_pos, col_pos)
    inside = (row_pos >= 0.0) & (row_pos < float(total))
    distance = jnp.abs(col_pos - row_pos)
    for h in range(heads):
        stride = dil_ref[h].astype(F32)

        def residue(pos, doc):
            steps = jnp.floor((pos + 0.5) / jnp.full(pos.shape, stride))
            return doc * 8.0 + (pos - steps * stride)

        row_code = jnp.where(inside, residue(row_pos, row_doc), -1.0)
        col_code = residue(col_pos, col_doc)
        mask = (row_code == col_code) & (distance <= stride * float(HALF))
        q = q_ref[:, h * hd : (h + 1) * hd]
        k = win_ref[:, h * hd : (h + 1) * hd]
        v = win_ref[:, width + h * hd : width + (h + 1) * hd]
        s = dot(q, k, ((1,), (1,))) * (hd**-0.5)
        s = jnp.where(mask, s, -jnp.inf)
        top = jnp.max(s, axis=1, keepdims=True)
        e = jnp.exp(s - top)
        weight = e / jnp.sum(e, axis=1, keepdims=True)
        weight_ref[h] = weight
        attn_ref[:, h * hd : (h + 1) * hd] = dot(weight.astype(BF), v, ((1,), (0,))).astype(BF)
    attn = attn_ref[...]
    span = part_ref.shape[2]
    for b in range(part_ref.shape[0]):
        part_ref[b] = dot(attn, w_ref[:, b * span : (b + 1) * span], ((1,), (0,))).astype(BF)


def backward_kernel(
    heads, q_ref, win_ref, weight_ref, attn_ref, mg_ref, w_ref, dq_ref, keep_ref, give_ref, ga_ref
):
    rows = q_ref.shape[0]
    width = q_ref.shape[1]
    hd = width // heads
    factor = hd**-0.5
    span = mg_ref.shape[2]
    total = jnp.zeros((rows, width), F32)
    for b in range(mg_ref.shape[0]):
        total = total + dot(mg_ref[b], w_ref[:, b * span : (b + 1) * span], ((1,), (1,)))
    ga_ref[...] = total.astype(BF)
    for h in range(heads):
        cols = slice(h * hd, (h + 1) * hd)
        vcols = slice(width + h * hd, width + (h + 1) * hd)
        ga = ga_ref[:, cols]
        q = q_ref[:, cols]
        delta = jnp.sum(ga.astype(F32) * attn_ref[:, cols].astype(F32), axis=1, keepdims=True)
        grad_prob = dot(ga, win_ref[:, vcols], ((1,), (1,)))
        weight = weight_ref[h]
        slopes = (weight * (grad_prob - delta)).astype(BF)
        probs = weight.astype(BF)
        dq_ref[:, cols] = (dot(slopes, win_ref[:, cols], ((1,), (0,))) * factor).astype(BF)
        dk = dot(slopes, q, ((0,), (0,))) * factor
        dv = dot(probs, ga, ((0,), (0,)))
        for i in range(5):
            part = slice(i * rows, (i + 1) * rows)
            if i % 2 == 0:
                keep_ref[i // 2, :, cols] = dk[part]
                keep_ref[i // 2, :, vcols] = dv[part]
            else:
                give_ref[i // 2, :, cols] = dk[part].astype(BF)
                give_ref[i // 2, :, vcols] = dv[part].astype(BF)


def share_kernel(where_ref, keep_ref, got_ref, down_ref, up_ref, own_ref):
    core = lax.rem(where_ref[0], 2)

    @pl.when(core == 0)
    def _():
        down_ref[...] = keep_ref[0].astype(BF)
        own_ref[...] = keep_ref[1] + got_ref[1, 0].astype(F32)
        up_ref[...] = (keep_ref[2] + got_ref[1, 1].astype(F32)).astype(BF)

    @pl.when(core == 1)
    def _():
        down_ref[...] = (keep_ref[0] + got_ref[0, 0].astype(F32)).astype(BF)
        own_ref[...] = keep_ref[1] + got_ref[0, 1].astype(F32)
        up_ref[...] = keep_ref[2].astype(BF)


def finish_kernel(own_ref, a_ref, b_ref, dk_ref, dv_ref):
    w = dk_ref.shape[1]
    total = own_ref[...] + a_ref[...].astype(F32) + b_ref[...].astype(F32)
    dk_ref[...] = total[:, :w].astype(BF)
    dv_ref[...] = total[:, w:].astype(BF)


def mixed_kernel(x_ref, o_ref):
    total = x_ref[0].astype(F32)
    for b in range(1, x_ref.shape[0]):
        total = total + x_ref[b].astype(F32)
    o_ref[...] = total.astype(BF)


def shifted(x, steps):
    count = lax.axis_size("ctx")
    first, last = max(0, -steps), min(count, count - steps)
    return lax.ppermute(x, "ctx", [(i, i + steps) for i in range(first, last)])


def in_chip(x):
    pairs = [[i, i + 1] for i in range(0, lax.axis_size("ctx"), 2)]
    return lax.all_gather(x, "ctx", axis=0, axis_index_groups=pairs)


def per_device(queries, keys, values, out_weight, mixed_grad, lengths, dilation):
    rows, width = queries.shape
    heads = dilation.shape[0]
    groups = lax.axis_size("head")
    span = mixed_grad.shape[1]
    total = rows * lax.axis_size("ctx")
    where = lax.axis_index("ctx").astype(jnp.int32).reshape(1)
    lens = lengths.reshape(1, -1)

    kv, spread = call(
        pack_kernel,
        [shape((rows, 2 * width), BF), shape((groups, rows, span), BF)],
        [keys, values, mixed_grad],
        "pack",
    )
    prev = shifted(kv, 2)
    follow = shifted(kv, -2)
    gathered = lax.all_to_all(spread, "head", 0, 0, tiled=True)
    own2, prev2, next2 = in_chip(kv), in_chip(prev), in_chip(follow)
    part, weight, attn, window = call(
        functools.partial(forward_kernel, heads, total),
        [
            shape((groups, rows, span), BF),
            shape((heads, rows, 5 * rows), F32),
            shape((rows, width), BF),
            shape((5 * rows, 2 * width), BF),
        ],
        [where, dilation, lens, queries, prev2, own2, next2, out_weight],
        "forward",
        flops=2 * rows * width * (groups * span + 10 * rows),
    )
    summed = lax.all_to_all(part, "head", 0, 0, tiled=True)
    dq, keep, give = call(
        functools.partial(backward_kernel, heads),
        [
            shape((rows, width), BF),
            shape((3, rows, 2 * width), F32),
            shape((2, rows, 2 * width), BF),
        ],
        [queries, window, weight, attn, gathered, out_weight],
        "backward",
        flops=2 * rows * width * (groups * span + 20 * rows),
        scratch=[pltpu.VMEM((rows, width), BF)],
    )
    got = in_chip(give)
    down, up, own = call(
        share_kernel,
        [shape((rows, 2 * width), BF), shape((rows, 2 * width), BF), shape((rows, 2 * width), F32)],
        [where, keep, got],
        "share",
    )
    from_next = shifted(down, -2)
    from_prev = shifted(up, 2)
    dk, dv = call(
        finish_kernel,
        [shape((rows, width), BF), shape((rows, width), BF)],
        [own, from_prev, from_next],
        "finish",
    )
    (mixed,) = call(mixed_kernel, [shape((rows, span), BF)], [summed], "mixed")
    return mixed, dq, dk, dv


def solution(mesh):
    placed = (
        P("ctx", "head"),
        P("ctx", "head"),
        P("ctx", "head"),
        P("head", None),
        P("ctx", "head"),
        P(),
        P("head"),
    )
    return jax.shard_map(
        per_device,
        mesh=mesh,
        in_specs=placed,
        out_specs=(P("ctx", "head"), P("ctx", "head"), P("ctx", "head"), P("ctx", "head")),
        check_vma=False,
    )
```

```python
import functools

import jax
import jax.numpy as jnp
from jax import lax
from jax.experimental import pallas as pl
from jax.experimental.pallas import tpu as pltpu
from jax.sharding import PartitionSpec as P

HALF = 32
BF = jnp.bfloat16
F32 = jnp.float32
VMEM = pl.BlockSpec(memory_space=pltpu.VMEM)
SMEM = pl.BlockSpec(memory_space=pltpu.SMEM)
HBM = pl.BlockSpec(memory_space=pltpu.HBM)


def dot(a, b, dims):
    return lax.dot_general(a, b, (dims, ((), ())), preferred_element_type=F32)


def call(body, outs, ins, name, flops=0, scratch=(), hbm_in=(), hbm_out=()):
    moved = sum(x.size * x.dtype.itemsize for x in (*ins, *outs))
    held = [
        pltpu.with_memory_space_constraint(x, pltpu.HBM) if i in hbm_in else x
        for i, x in enumerate(ins)
    ]
    return pl.pallas_call(
        body,
        out_shape=[pltpu.HBM(x.shape, x.dtype) if i in hbm_out else x for i, x in enumerate(outs)],
        in_specs=[SMEM if x.ndim == 1 else HBM if i in hbm_in else VMEM for i, x in enumerate(ins)],
        out_specs=[HBM if i in hbm_out else VMEM for i in range(len(outs))],
        scratch_shapes=scratch,
        compiler_params=pltpu.CompilerParams(vmem_limit_bytes=24 << 20),
        cost_estimate=pl.CostEstimate(flops=flops, bytes_accessed=moved, transcendentals=0),
        name=name,
    )(*held)


def shape(dims, dtype):
    return jax.ShapeDtypeStruct(dims, dtype)


def pack_kernel(k_ref, v_ref, mg_ref, kv_ref, all_ref, sems):
    w = k_ref.shape[1]
    copies = [
        pltpu.make_async_copy(k_ref, kv_ref.at[:, :w], sems.at[0]),
        pltpu.make_async_copy(v_ref, kv_ref.at[:, w:], sems.at[1]),
    ]
    for b in range(all_ref.shape[0]):
        copies.append(pltpu.make_async_copy(mg_ref, all_ref.at[b], sems.at[2 + b]))
    for c in copies:
        c.start()
    for c in copies:
        c.wait()


def document_codes(lens, row_pos, col_pos):
    n = lens.shape[1]
    down = lax.broadcasted_iota(jnp.int32, (n, n), 0)
    across = lax.broadcasted_iota(jnp.int32, (n, n), 1)
    wide = jnp.broadcast_to(lens, (n, n))
    ends_col = jnp.sum(jnp.where(across <= down, wide, 0.0), axis=1, keepdims=True)
    lens_col = jnp.sum(jnp.where(across == down, wide, 0.0), axis=1, keepdims=True)
    ends_row = jnp.sum(jnp.where(down <= across, lens_col, 0.0), axis=0, keepdims=True)
    row_doc = jnp.sum(jnp.where(row_pos >= ends_col, 1.0, 0.0), axis=0, keepdims=True)
    col_doc = jnp.sum(jnp.where(col_pos >= ends_row, 1.0, 0.0), axis=1, keepdims=True)
    return row_doc, col_doc


def forward_kernel(
    heads, total, where_ref, dil_ref, lens_ref, q_ref, own_ref, far_ref, w_ref,
    part_ref, out_probs_ref, out_attn_ref, out_win_ref,
    hold_ref, win_ref, probs_ref, attn_ref, sems,
):
    rows = q_ref.shape[0]
    width = q_ref.shape[1]
    hd = width // heads
    keys = win_ref.shape[0]
    slab = where_ref[0]
    core = lax.rem(slab, 2)
    prev, follow = far_ref.at[0], far_ref.at[1]
    six = [prev.at[0], prev.at[1], own_ref.at[0], own_ref.at[1], follow.at[0], follow.at[1]]

    @pl.when(core == 0)
    def _():
        for i in range(5):
            win_ref[i * rows : (i + 1) * rows, :] = six[i][...]

    @pl.when(core == 1)
    def _():
        for i in range(5):
            win_ref[i * rows : (i + 1) * rows, :] = six[i + 1][...]

    copies = [pltpu.make_async_copy(win_ref, out_win_ref, sems.at[part_ref.shape[0]])]
    copies[0].start()

    first = slab * rows
    row_idx = lax.broadcasted_iota(jnp.int32, (1, keys), 1) + (first - 2 * rows)
    col_idx = lax.broadcasted_iota(jnp.int32, (rows, 1), 0) + first
    row_pos, col_pos = row_idx.astype(F32), col_idx.astype(F32)
    row_doc, col_doc = document_codes(lens_ref[...].astype(F32), row_pos, col_pos)
    inside = (row_pos >= 0.0) & (row_pos < float(total))
    distance = jnp.abs(col_pos - row_pos)
    for h in range(heads):
        stride = dil_ref[h].astype(F32)

        def residue(pos, doc):
            steps = jnp.floor((pos + 0.5) / jnp.full(pos.shape, stride))
            return doc * 8.0 + (pos - steps * stride)

        row_code = jnp.where(inside, residue(row_pos, row_doc), -1.0)
        col_code = residue(col_pos, col_doc)
        mask = (row_code == col_code) & (distance <= stride * float(HALF))
        q = q_ref[:, h * hd : (h + 1) * hd]
        k = win_ref[:, h * hd : (h + 1) * hd]
        v = win_ref[:, width + h * hd : width + (h + 1) * hd]
        s = dot(q, k, ((1,), (1,))) * (hd**-0.5)
        s = jnp.where(mask, s, -jnp.inf)
        top = jnp.max(s, axis=1, keepdims=True)
        e = jnp.exp(s - top)
        probs = (e * (1.0 / jnp.sum(e, axis=1, keepdims=True))).astype(BF)
        probs_ref[h] = probs
        attn_ref[:, h * hd : (h + 1) * hd] = dot(probs, v, ((1,), (0,))).astype(BF)
    for i, (a, b) in enumerate(((probs_ref, out_probs_ref), (attn_ref, out_attn_ref))):
        copies.append(pltpu.make_async_copy(a, b, sems.at[part_ref.shape[0] + 1 + i]))
        copies[-1].start()
    attn = attn_ref[...]
    span = part_ref.shape[2]
    for b in range(part_ref.shape[0]):
        hold_ref[b] = dot(attn, w_ref[:, b * span : (b + 1) * span], ((1,), (0,))).astype(BF)
        copies.append(pltpu.make_async_copy(hold_ref.at[b], part_ref.at[b], sems.at[b]))
        copies[-1].start()
    for c in copies:
        c.wait()


def backward_kernel(
    heads, where_ref, q_hbm, win_hbm, probs_hbm, attn_hbm, mg_ref, w_ref,
    dq_ref, own_ref, pass_ref, give_ref,
    mgv_ref, ga_ref, terms_ref, q_ref, win_ref, probs_ref, attn_ref, sems,
):
    rows = q_ref.shape[0]
    width = q_ref.shape[1]
    hd = width // heads
    factor = hd**-0.5
    span = mg_ref.shape[2]
    groups = mg_ref.shape[0]
    copies = [pltpu.make_async_copy(mg_ref.at[b], mgv_ref.at[b], sems.at[b]) for b in range(groups)]
    held = ((q_hbm, q_ref), (attn_hbm, attn_ref), (win_hbm, win_ref), (probs_hbm, probs_ref))
    for i, (a, b) in enumerate(held):
        copies.append(pltpu.make_async_copy(a, b, sems.at[groups + i]))
    for c in copies:
        c.start()
    total = jnp.zeros((rows, width), F32)
    for b in range(groups):
        copies[b].wait()
        total = total + dot(mgv_ref[b], w_ref[:, b * span : (b + 1) * span], ((1,), (1,)))
    ga_ref[...] = total.astype(BF)
    for c in copies[groups:]:
        c.wait()
    for h in range(heads):
        cols = slice(h * hd, (h + 1) * hd)
        vcols = slice(width + h * hd, width + (h + 1) * hd)
        ga = ga_ref[:, cols]
        q = q_ref[:, cols]
        delta = jnp.sum(ga.astype(F32) * attn_ref[:, cols].astype(F32), axis=1, keepdims=True)
        grad_prob = dot(ga, win_ref[:, vcols], ((1,), (1,)))
        probs = probs_ref[h]
        slopes = (probs.astype(F32) * (grad_prob - delta)).astype(BF)
        dq_ref[:, cols] = (dot(slopes, win_ref[:, cols], ((1,), (0,))) * factor).astype(BF)
        dk = dot(slopes, q, ((0,), (0,))) * factor
        dv = dot(probs, ga, ((0,), (0,)))
        for i in range(5):
            part = slice(i * rows, (i + 1) * rows)
            if i == 2:
                own_ref[:, cols] = dk[part]
                own_ref[:, vcols] = dv[part]
            else:
                terms_ref[i, :, cols] = dk[part].astype(BF)
                terms_ref[i, :, vcols] = dv[part].astype(BF)
    core = lax.rem(where_ref[0], 2)
    for value, given, kept in ((0, (0, 1, 3), 4), (1, (1, 3, 4), 0)):

        @pl.when(core == value)
        def _(given=given, kept=kept):
            pass_ref[...] = terms_ref[kept]
            for i, slab in enumerate(given):
                give_ref[i] = terms_ref[slab]


def share_kernel(where_ref, own_ref, pass_ref, got_ref, send_ref, sum_ref):
    core = lax.rem(where_ref[0], 2)
    mine = pass_ref[...].astype(F32)

    @pl.when(core == 0)
    def _():
        sum_ref[...] = own_ref[...] + got_ref[1, 0].astype(F32)
        send_ref[0] = (mine + got_ref[1, 1].astype(F32)).astype(BF)
        send_ref[1] = got_ref[1, 2]

    @pl.when(core == 1)
    def _():
        sum_ref[...] = own_ref[...] + got_ref[0, 2].astype(F32)
        send_ref[0] = got_ref[0, 0]
        send_ref[1] = (mine + got_ref[0, 1].astype(F32)).astype(BF)


def finish_kernel(where_ref, own_ref, far_ref, dk_ref, dv_ref):
    w = dk_ref.shape[1]
    core = lax.rem(where_ref[0], 2)
    total = own_ref[...] + far_ref[0, core].astype(F32) + far_ref[1, core].astype(F32)
    dk_ref[...] = total[:, :w].astype(BF)
    dv_ref[...] = total[:, w:].astype(BF)


def mixed_kernel(x_ref, o_ref):
    total = x_ref[0].astype(F32)
    for b in range(1, x_ref.shape[0]):
        total = total + x_ref[b].astype(F32)
    o_ref[...] = total.astype(BF)


def to_neighbours(x):
    count = lax.axis_size("ctx")
    ahead = [(i, i + 2) for i in range(0, count - 2, 2)]
    back = [(i, i - 2) for i in range(3, count, 2)]
    return lax.ppermute(x, "ctx", ahead + back)


def in_chip(x):
    pairs = [[i, i + 1] for i in range(0, lax.axis_size("ctx"), 2)]
    return lax.all_gather(x, "ctx", axis=0, axis_index_groups=pairs)


def per_device(queries, keys, values, out_weight, mixed_grad, lengths, dilation):
    rows, width = queries.shape
    heads = dilation.shape[0]
    groups = lax.axis_size("head")
    span = mixed_grad.shape[1]
    total = rows * lax.axis_size("ctx")
    where = lax.axis_index("ctx").astype(jnp.int32).reshape(1)
    lens = lengths.reshape(1, -1)

    kv, spread = call(
        pack_kernel,
        [shape((rows, 2 * width), BF), shape((groups, rows, span), BF)],
        [keys, values, mixed_grad],
        "pack",
        scratch=[pltpu.SemaphoreType.DMA((2 + groups,))],
        hbm_in=(0, 1, 2),
        hbm_out=(1,),
    )
    own2, spread = lax.optimization_barrier((in_chip(kv), spread))
    far = in_chip(to_neighbours(own2))
    gathered = lax.all_to_all(spread, "head", 0, 0, tiled=True)
    part, probs, attn, window = call(
        functools.partial(forward_kernel, heads, total),
        [
            shape((groups, rows, span), BF),
            shape((heads, rows, 5 * rows), BF),
            shape((rows, width), BF),
            shape((5 * rows, 2 * width), BF),
        ],
        [where, dilation, lens, queries, own2, far, out_weight],
        "forward",
        flops=2 * rows * width * (groups * span + 10 * rows),
        scratch=[
            pltpu.VMEM((groups, rows, span), BF),
            pltpu.VMEM((5 * rows, 2 * width), BF),
            pltpu.VMEM((heads, rows, 5 * rows), BF),
            pltpu.VMEM((rows, width), BF),
            pltpu.SemaphoreType.DMA((groups + 3,)),
        ],
        hbm_out=(0, 1, 2, 3),
    )
    summed = lax.all_to_all(part, "head", 0, 0, tiled=True)
    dq, own, passed, give = call(
        functools.partial(backward_kernel, heads),
        [
            shape((rows, width), BF),
            shape((rows, 2 * width), F32),
            shape((rows, 2 * width), BF),
            shape((3, rows, 2 * width), BF),
        ],
        [where, queries, window, probs, attn, gathered, out_weight],
        "backward",
        flops=2 * rows * width * (groups * span + 20 * rows),
        scratch=[
            pltpu.VMEM((groups, rows, span), BF),
            pltpu.VMEM((rows, width), BF),
            pltpu.VMEM((5, rows, 2 * width), BF),
            pltpu.VMEM((rows, width), BF),
            pltpu.VMEM((5 * rows, 2 * width), BF),
            pltpu.VMEM((heads, rows, 5 * rows), BF),
            pltpu.VMEM((rows, width), BF),
            pltpu.SemaphoreType.DMA((groups + 4,)),
        ],
        hbm_in=(1, 2, 3, 4, 5),
    )
    send, own = call(
        share_kernel,
        [shape((2, rows, 2 * width), BF), shape((rows, 2 * width), F32)],
        [where, own, passed, in_chip(give)],
        "share",
    )
    dk, dv = call(
        finish_kernel,
        [shape((rows, width), BF), shape((rows, width), BF)],
        [where, own, in_chip(to_neighbours(send))],
        "finish",
    )
    (mixed,) = call(mixed_kernel, [shape((rows, span), BF)], [summed], "mixed")
    return mixed, dq, dk, dv


def solution(mesh):
    placed = (
        P("ctx", "head"),
        P("ctx", "head"),
        P("ctx", "head"),
        P("head", None),
        P("ctx", "head"),
        P(),
        P("head"),
    )
    return jax.shard_map(
        per_device,
        mesh=mesh,
        in_specs=placed,
        out_specs=(P("ctx", "head"), P("ctx", "head"), P("ctx", "head"), P("ctx", "head")),
        check_vma=False,
    )
```

```python
import functools

import jax
import jax.numpy as jnp
from jax import lax
from jax.experimental import pallas as pl
from jax.experimental.pallas import tpu as pltpu
from jax.sharding import PartitionSpec as P

HALF = 32
BF = jnp.bfloat16
F32 = jnp.float32
VMEM = pl.BlockSpec(memory_space=pltpu.VMEM)
SMEM = pl.BlockSpec(memory_space=pltpu.SMEM)
HBM = pl.BlockSpec(memory_space=pltpu.HBM)


def dot(a, b, dims):
    return lax.dot_general(a, b, (dims, ((), ())), preferred_element_type=F32)


def call(body, outs, ins, name, flops=0, scratch=(), hbm_in=(), hbm_out=()):
    moved = sum(x.size * x.dtype.itemsize for x in (*ins, *outs))
    held = [
        pltpu.with_memory_space_constraint(x, pltpu.HBM) if i in hbm_in else x
        for i, x in enumerate(ins)
    ]
    return pl.pallas_call(
        body,
        out_shape=[pltpu.HBM(x.shape, x.dtype) if i in hbm_out else x for i, x in enumerate(outs)],
        in_specs=[SMEM if x.ndim == 1 else HBM if i in hbm_in else VMEM for i, x in enumerate(ins)],
        out_specs=[HBM if i in hbm_out else VMEM for i in range(len(outs))],
        scratch_shapes=scratch,
        compiler_params=pltpu.CompilerParams(vmem_limit_bytes=24 << 20),
        cost_estimate=pl.CostEstimate(flops=flops, bytes_accessed=moved, transcendentals=0),
        name=name,
    )(*held)


def shape(dims, dtype):
    return jax.ShapeDtypeStruct(dims, dtype)


def pack_kernel(k_ref, v_ref, kv_ref, sems):
    w = k_ref.shape[1]
    copies = [
        pltpu.make_async_copy(k_ref, kv_ref.at[:, :w], sems.at[0]),
        pltpu.make_async_copy(v_ref, kv_ref.at[:, w:], sems.at[1]),
    ]
    for c in copies:
        c.start()
    for c in copies:
        c.wait()


def spread_kernel(mg_ref, after_ref, all_ref, sems):
    copies = [
        pltpu.make_async_copy(mg_ref, all_ref.at[b], sems.at[b]) for b in range(all_ref.shape[0])
    ]
    for c in copies:
        c.start()
    for c in copies:
        c.wait()


def document_codes(lens, row_pos, col_pos):
    n = lens.shape[1]
    down = lax.broadcasted_iota(jnp.int32, (n, n), 0)
    across = lax.broadcasted_iota(jnp.int32, (n, n), 1)
    wide = jnp.broadcast_to(lens, (n, n))
    ends_col = jnp.sum(jnp.where(across <= down, wide, 0.0), axis=1, keepdims=True)
    lens_col = jnp.sum(jnp.where(across == down, wide, 0.0), axis=1, keepdims=True)
    ends_row = jnp.sum(jnp.where(down <= across, lens_col, 0.0), axis=0, keepdims=True)
    row_doc = jnp.sum(jnp.where(row_pos >= ends_col, 1.0, 0.0), axis=0, keepdims=True)
    col_doc = jnp.sum(jnp.where(col_pos >= ends_row, 1.0, 0.0), axis=1, keepdims=True)
    return row_doc, col_doc


def forward_kernel(
    heads, total, where_ref, dil_ref, lens_ref, q_ref, own_ref, far_ref, w_ref,
    part_ref, out_probs_ref, out_attn_ref, out_win_ref,
    hold_ref, win_ref, probs_ref, attn_ref, sems,
):
    rows = q_ref.shape[0]
    width = q_ref.shape[1]
    hd = width // heads
    keys = win_ref.shape[0]
    slab = where_ref[0]
    core = lax.rem(slab, 2)
    prev, follow = far_ref.at[0], far_ref.at[1]
    six = [prev.at[0], prev.at[1], own_ref.at[0], own_ref.at[1], follow.at[0], follow.at[1]]

    @pl.when(core == 0)
    def _():
        for i in range(5):
            win_ref[i * rows : (i + 1) * rows, :] = six[i][...]

    @pl.when(core == 1)
    def _():
        for i in range(5):
            win_ref[i * rows : (i + 1) * rows, :] = six[i + 1][...]

    copies = [pltpu.make_async_copy(win_ref, out_win_ref, sems.at[part_ref.shape[0]])]
    copies[0].start()

    first = slab * rows
    row_idx = lax.broadcasted_iota(jnp.int32, (1, keys), 1) + (first - 2 * rows)
    col_idx = lax.broadcasted_iota(jnp.int32, (rows, 1), 0) + first
    row_pos, col_pos = row_idx.astype(F32), col_idx.astype(F32)
    row_doc, col_doc = document_codes(lens_ref[...].astype(F32), row_pos, col_pos)
    inside = (row_pos >= 0.0) & (row_pos < float(total))
    distance = jnp.abs(col_pos - row_pos)
    for h in range(heads):
        stride = dil_ref[h].astype(F32)

        def residue(pos, doc):
            steps = jnp.floor((pos + 0.5) / jnp.full(pos.shape, stride))
            return doc * 8.0 + (pos - steps * stride)

        row_code = jnp.where(inside, residue(row_pos, row_doc), -1.0)
        col_code = residue(col_pos, col_doc)
        mask = (row_code == col_code) & (distance <= stride * float(HALF))
        q = q_ref[:, h * hd : (h + 1) * hd]
        k = win_ref[:, h * hd : (h + 1) * hd]
        v = win_ref[:, width + h * hd : width + (h + 1) * hd]
        s = dot(q, k, ((1,), (1,))) * (hd**-0.5)
        s = jnp.where(mask, s, -jnp.inf)
        top = jnp.max(s, axis=1, keepdims=True)
        e = jnp.exp(s - top)
        probs = (e * (1.0 / jnp.sum(e, axis=1, keepdims=True))).astype(BF)
        probs_ref[h] = probs
        attn_ref[:, h * hd : (h + 1) * hd] = dot(probs, v, ((1,), (0,))).astype(BF)
    for i, (a, b) in enumerate(((probs_ref, out_probs_ref), (attn_ref, out_attn_ref))):
        copies.append(pltpu.make_async_copy(a, b, sems.at[part_ref.shape[0] + 1 + i]))
        copies[-1].start()
    attn = attn_ref[...]
    span = part_ref.shape[2]
    for b in range(part_ref.shape[0]):
        hold_ref[b] = dot(attn, w_ref[:, b * span : (b + 1) * span], ((1,), (0,))).astype(BF)
        copies.append(pltpu.make_async_copy(hold_ref.at[b], part_ref.at[b], sems.at[b]))
        copies[-1].start()
    for c in copies:
        c.wait()


def backward_kernel(
    heads, where_ref, q_hbm, win_hbm, probs_hbm, attn_hbm, mg_ref, w_ref,
    dq_ref, own_ref, pass_ref, give_ref,
    mgv_ref, ga_ref, terms_ref, q_ref, win_ref, probs_ref, attn_ref, sems,
):
    rows = q_ref.shape[0]
    width = q_ref.shape[1]
    hd = width // heads
    factor = hd**-0.5
    span = mg_ref.shape[2]
    groups = mg_ref.shape[0]
    copies = [pltpu.make_async_copy(mg_ref.at[b], mgv_ref.at[b], sems.at[b]) for b in range(groups)]
    held = ((q_hbm, q_ref), (attn_hbm, attn_ref), (win_hbm, win_ref), (probs_hbm, probs_ref))
    for i, (a, b) in enumerate(held):
        copies.append(pltpu.make_async_copy(a, b, sems.at[groups + i]))
    for c in copies:
        c.start()
    total = jnp.zeros((rows, width), F32)
    for b in range(groups):
        copies[b].wait()
        total = total + dot(mgv_ref[b], w_ref[:, b * span : (b + 1) * span], ((1,), (1,)))
    ga_ref[...] = total.astype(BF)
    for c in copies[groups:]:
        c.wait()
    for h in range(heads):
        cols = slice(h * hd, (h + 1) * hd)
        vcols = slice(width + h * hd, width + (h + 1) * hd)
        ga = ga_ref[:, cols]
        q = q_ref[:, cols]
        delta = jnp.sum(ga.astype(F32) * attn_ref[:, cols].astype(F32), axis=1, keepdims=True)
        grad_prob = dot(ga, win_ref[:, vcols], ((1,), (1,)))
        probs = probs_ref[h]
        slopes = (probs.astype(F32) * (grad_prob - delta)).astype(BF)
        dq_ref[:, cols] = (dot(slopes, win_ref[:, cols], ((1,), (0,))) * factor).astype(BF)
        dk = dot(slopes, q, ((0,), (0,))) * factor
        dv = dot(probs, ga, ((0,), (0,)))
        for i in range(5):
            part = slice(i * rows, (i + 1) * rows)
            if i == 2:
                own_ref[:, cols] = dk[part]
                own_ref[:, vcols] = dv[part]
            else:
                terms_ref[i, :, cols] = dk[part].astype(BF)
                terms_ref[i, :, vcols] = dv[part].astype(BF)
    core = lax.rem(where_ref[0], 2)
    for value, given, kept in ((0, (0, 1, 3), 4), (1, (1, 3, 4), 0)):

        @pl.when(core == value)
        def _(given=given, kept=kept):
            pass_ref[...] = terms_ref[kept]
            for i, slab in enumerate(given):
                give_ref[i] = terms_ref[slab]


def share_kernel(where_ref, own_ref, pass_ref, got_ref, send_ref, sum_ref):
    core = lax.rem(where_ref[0], 2)
    mine = pass_ref[...].astype(F32)

    @pl.when(core == 0)
    def _():
        sum_ref[...] = own_ref[...] + got_ref[1, 0].astype(F32)
        send_ref[0] = (mine + got_ref[1, 1].astype(F32)).astype(BF)
        send_ref[1] = got_ref[1, 2]

    @pl.when(core == 1)
    def _():
        sum_ref[...] = own_ref[...] + got_ref[0, 2].astype(F32)
        send_ref[0] = got_ref[0, 0]
        send_ref[1] = (mine + got_ref[0, 1].astype(F32)).astype(BF)


def finish_kernel(where_ref, own_ref, far_ref, dk_ref, dv_ref):
    w = dk_ref.shape[1]
    core = lax.rem(where_ref[0], 2)
    total = own_ref[...] + far_ref[0, core].astype(F32) + far_ref[1, core].astype(F32)
    dk_ref[...] = total[:, :w].astype(BF)
    dv_ref[...] = total[:, w:].astype(BF)


def mixed_kernel(x_ref, o_ref):
    total = x_ref[0].astype(F32)
    for b in range(1, x_ref.shape[0]):
        total = total + x_ref[b].astype(F32)
    o_ref[...] = total.astype(BF)


def to_neighbours(x):
    count = lax.axis_size("ctx")
    ahead = [(i, i + 2) for i in range(0, count - 2, 2)]
    back = [(i, i - 2) for i in range(3, count, 2)]
    return lax.ppermute(x, "ctx", ahead + back)


def in_chip(x):
    pairs = [[i, i + 1] for i in range(0, lax.axis_size("ctx"), 2)]
    return lax.all_gather(x, "ctx", axis=0, axis_index_groups=pairs)


def per_device(queries, keys, values, out_weight, mixed_grad, lengths, dilation):
    rows, width = queries.shape
    heads = dilation.shape[0]
    groups = lax.axis_size("head")
    span = mixed_grad.shape[1]
    total = rows * lax.axis_size("ctx")
    where = lax.axis_index("ctx").astype(jnp.int32).reshape(1)
    lens = lengths.reshape(1, -1)

    (kv,) = call(
        pack_kernel,
        [shape((rows, 2 * width), BF)],
        [keys, values],
        "pack",
        scratch=[pltpu.SemaphoreType.DMA((2,))],
        hbm_in=(0, 1),
    )
    own2 = in_chip(kv)
    near = to_neighbours(own2)
    (spread,) = call(
        spread_kernel,
        [shape((groups, rows, span), BF)],
        [mixed_grad, own2],
        "spread",
        scratch=[pltpu.SemaphoreType.DMA((groups,))],
        hbm_out=(0,),
    )
    gathered = lax.all_to_all(spread, "head", 0, 0, tiled=True)
    far = in_chip(near)
    part, probs, attn, window = call(
        functools.partial(forward_kernel, heads, total),
        [
            shape((groups, rows, span), BF),
            shape((heads, rows, 5 * rows), BF),
            shape((rows, width), BF),
            shape((5 * rows, 2 * width), BF),
        ],
        [where, dilation, lens, queries, own2, far, out_weight],
        "forward",
        flops=80 * 2 * rows * width * (groups * span + 10 * rows),
        scratch=[
            pltpu.VMEM((groups, rows, span), BF),
            pltpu.VMEM((5 * rows, 2 * width), BF),
            pltpu.VMEM((heads, rows, 5 * rows), BF),
            pltpu.VMEM((rows, width), BF),
            pltpu.SemaphoreType.DMA((groups + 3,)),
        ],
        hbm_out=(0, 1, 2, 3),
    )
    summed = lax.all_to_all(part, "head", 0, 0, tiled=True)
    dq, own, passed, give = call(
        functools.partial(backward_kernel, heads),
        [
            shape((rows, width), BF),
            shape((rows, 2 * width), F32),
            shape((rows, 2 * width), BF),
            shape((3, rows, 2 * width), BF),
        ],
        [where, queries, window, probs, attn, gathered, out_weight],
        "backward",
        flops=2 * rows * width * (groups * span + 20 * rows),
        scratch=[
            pltpu.VMEM((groups, rows, span), BF),
            pltpu.VMEM((rows, width), BF),
            pltpu.VMEM((5, rows, 2 * width), BF),
            pltpu.VMEM((rows, width), BF),
            pltpu.VMEM((5 * rows, 2 * width), BF),
            pltpu.VMEM((heads, rows, 5 * rows), BF),
            pltpu.VMEM((rows, width), BF),
            pltpu.SemaphoreType.DMA((groups + 4,)),
        ],
        hbm_in=(1, 2, 3, 4, 5),
    )
    send, own = call(
        share_kernel,
        [shape((2, rows, 2 * width), BF), shape((rows, 2 * width), F32)],
        [where, own, passed, in_chip(give)],
        "share",
    )
    dk, dv = call(
        finish_kernel,
        [shape((rows, width), BF), shape((rows, width), BF)],
        [where, own, in_chip(to_neighbours(send))],
        "finish",
    )
    (mixed,) = call(mixed_kernel, [shape((rows, span), BF)], [summed], "mixed")
    return mixed, dq, dk, dv


def solution(mesh):
    placed = (
        P("ctx", "head"),
        P("ctx", "head"),
        P("ctx", "head"),
        P("head", None),
        P("ctx", "head"),
        P(),
        P("head"),
    )
    return jax.shard_map(
        per_device,
        mesh=mesh,
        in_specs=placed,
        out_specs=(P("ctx", "head"), P("ctx", "head"), P("ctx", "head"), P("ctx", "head")),
        check_vma=False,
    )
```

```python
import functools

import jax
import jax.numpy as jnp
from jax import lax
from jax.experimental import pallas as pl
from jax.experimental.pallas import tpu as pltpu
from jax.sharding import PartitionSpec as P

HALF = 32
BF = jnp.bfloat16
F32 = jnp.float32
VMEM = pl.BlockSpec(memory_space=pltpu.VMEM)
SMEM = pl.BlockSpec(memory_space=pltpu.SMEM)
HBM = pl.BlockSpec(memory_space=pltpu.HBM)


def dot(a, b, dims):
    return lax.dot_general(a, b, (dims, ((), ())), preferred_element_type=F32)


def call(body, outs, ins, name, flops=0, scratch=(), hbm_in=(), hbm_out=()):
    moved = sum(x.size * x.dtype.itemsize for x in (*ins, *outs))
    held = [
        pltpu.with_memory_space_constraint(x, pltpu.HBM) if i in hbm_in else x
        for i, x in enumerate(ins)
    ]
    return pl.pallas_call(
        body,
        out_shape=[pltpu.HBM(x.shape, x.dtype) if i in hbm_out else x for i, x in enumerate(outs)],
        in_specs=[SMEM if x.ndim == 1 else HBM if i in hbm_in else VMEM for i, x in enumerate(ins)],
        out_specs=[HBM if i in hbm_out else VMEM for i in range(len(outs))],
        scratch_shapes=scratch,
        compiler_params=pltpu.CompilerParams(vmem_limit_bytes=24 << 20),
        cost_estimate=pl.CostEstimate(flops=flops, bytes_accessed=moved, transcendentals=0),
        name=name,
    )(*held)


def shape(dims, dtype):
    return jax.ShapeDtypeStruct(dims, dtype)


def pack_kernel(k_ref, v_ref, mg_ref, kv_ref, mgv_ref, sems):
    w = k_ref.shape[1]
    copies = [
        pltpu.make_async_copy(mg_ref, mgv_ref, sems.at[2]),
        pltpu.make_async_copy(k_ref, kv_ref.at[:, :w], sems.at[0]),
        pltpu.make_async_copy(v_ref, kv_ref.at[:, w:], sems.at[1]),
    ]
    for c in copies:
        c.start()
    for c in copies:
        c.wait()


def spread_kernel(mg_ref, all_ref, sems):
    copies = [
        pltpu.make_async_copy(mg_ref, all_ref.at[b], sems.at[b]) for b in range(all_ref.shape[0])
    ]
    for c in copies:
        c.start()
    for c in copies:
        c.wait()


def document_codes(lens, row_pos, col_pos):
    n = lens.shape[1]
    down = lax.broadcasted_iota(jnp.int32, (n, n), 0)
    across = lax.broadcasted_iota(jnp.int32, (n, n), 1)
    wide = jnp.broadcast_to(lens, (n, n))
    ends_col = jnp.sum(jnp.where(across <= down, wide, 0.0), axis=1, keepdims=True)
    lens_col = jnp.sum(jnp.where(across == down, wide, 0.0), axis=1, keepdims=True)
    ends_row = jnp.sum(jnp.where(down <= across, lens_col, 0.0), axis=0, keepdims=True)
    row_doc = jnp.sum(jnp.where(row_pos >= ends_col, 1.0, 0.0), axis=0, keepdims=True)
    col_doc = jnp.sum(jnp.where(col_pos >= ends_row, 1.0, 0.0), axis=1, keepdims=True)
    return row_doc, col_doc


def forward_kernel(
    heads, total, where_ref, dil_ref, lens_ref, q_ref, prev_ref, own_ref, next_ref, w_ref,
    part_ref, probs_ref, attn_ref, win_ref, hold_ref, sems,
):
    rows = q_ref.shape[0]
    width = q_ref.shape[1]
    hd = width // heads
    keys = win_ref.shape[0]
    slab = where_ref[0]
    core = lax.rem(slab, 2)
    six = [x.at[i] for x in (prev_ref, own_ref, next_ref) for i in range(2)]

    @pl.when(core == 0)
    def _():
        for i in range(5):
            win_ref[i * rows : (i + 1) * rows, :] = six[i][...]

    @pl.when(core == 1)
    def _():
        for i in range(5):
            win_ref[i * rows : (i + 1) * rows, :] = six[i + 1][...]

    first = slab * rows
    row_idx = lax.broadcasted_iota(jnp.int32, (1, keys), 1) + (first - 2 * rows)
    col_idx = lax.broadcasted_iota(jnp.int32, (rows, 1), 0) + first
    row_pos, col_pos = row_idx.astype(F32), col_idx.astype(F32)
    row_doc, col_doc = document_codes(lens_ref[...].astype(F32), row_pos, col_pos)
    inside = (row_pos >= 0.0) & (row_pos < float(total))
    distance = jnp.abs(col_pos - row_pos)
    for h in range(heads):
        stride = dil_ref[h].astype(F32)

        def residue(pos, doc):
            steps = jnp.floor((pos + 0.5) / jnp.full(pos.shape, stride))
            return doc * 8.0 + (pos - steps * stride)

        row_code = jnp.where(inside, residue(row_pos, row_doc), -1.0)
        col_code = residue(col_pos, col_doc)
        mask = (row_code == col_code) & (distance <= stride * float(HALF))
        q = q_ref[:, h * hd : (h + 1) * hd]
        k = win_ref[:, h * hd : (h + 1) * hd]
        v = win_ref[:, width + h * hd : width + (h + 1) * hd]
        s = dot(q, k, ((1,), (1,))) * (hd**-0.5)
        s = jnp.where(mask, s, -jnp.inf)
        top = jnp.max(s, axis=1, keepdims=True)
        e = jnp.exp(s - top)
        probs = (e * (1.0 / jnp.sum(e, axis=1, keepdims=True))).astype(BF)
        probs_ref[h] = probs
        attn_ref[:, h * hd : (h + 1) * hd] = dot(probs, v, ((1,), (0,))).astype(BF)
    attn = attn_ref[...]
    span = part_ref.shape[2]
    copies = []
    for b in range(part_ref.shape[0]):
        hold_ref[b] = dot(attn, w_ref[:, b * span : (b + 1) * span], ((1,), (0,))).astype(BF)
        copies.append(pltpu.make_async_copy(hold_ref.at[b], part_ref.at[b], sems.at[b]))
        copies[-1].start()
    for c in copies:
        c.wait()


def backward_kernel(
    heads, where_ref, q_ref, win_ref, probs_ref, attn_ref, mg_ref, w_ref,
    dq_ref, own_ref, pass_ref, give_ref,
    mgv_ref, ga_ref, terms_ref, sems,
):
    rows = q_ref.shape[0]
    width = q_ref.shape[1]
    hd = width // heads
    factor = hd**-0.5
    span = mg_ref.shape[2]
    groups = mg_ref.shape[0]
    copies = [pltpu.make_async_copy(mg_ref.at[b], mgv_ref.at[b], sems.at[b]) for b in range(groups)]
    for c in copies:
        c.start()
    total = jnp.zeros((rows, width), F32)
    for b in range(groups):
        copies[b].wait()
        total = total + dot(mgv_ref[b], w_ref[:, b * span : (b + 1) * span], ((1,), (1,)))
    ga_ref[...] = total.astype(BF)
    for h in range(heads):
        cols = slice(h * hd, (h + 1) * hd)
        vcols = slice(width + h * hd, width + (h + 1) * hd)
        ga = ga_ref[:, cols]
        q = q_ref[:, cols]
        delta = jnp.sum(ga.astype(F32) * attn_ref[:, cols].astype(F32), axis=1, keepdims=True)
        grad_prob = dot(ga, win_ref[:, vcols], ((1,), (1,)))
        probs = probs_ref[h]
        slopes = (probs.astype(F32) * (grad_prob - delta)).astype(BF)
        dq_ref[:, cols] = (dot(slopes, win_ref[:, cols], ((1,), (0,))) * factor).astype(BF)
        dk = dot(slopes, q, ((0,), (0,))) * factor
        dv = dot(probs, ga, ((0,), (0,)))
        for i in range(5):
            part = slice(i * rows, (i + 1) * rows)
            if i == 2:
                own_ref[:, cols] = dk[part]
                own_ref[:, vcols] = dv[part]
            else:
                terms_ref[i, :, cols] = dk[part].astype(BF)
                terms_ref[i, :, vcols] = dv[part].astype(BF)
    core = lax.rem(where_ref[0], 2)
    for value, given, kept in ((0, (0, 1, 3), 4), (1, (1, 3, 4), 0)):

        @pl.when(core == value)
        def _(given=given, kept=kept):
            pass_ref[...] = terms_ref[kept]
            for i, slab in enumerate(given):
                give_ref[i] = terms_ref[slab]


def share_kernel(where_ref, own_ref, pass_ref, got_ref, send_ref, sum_ref):
    core = lax.rem(where_ref[0], 2)
    mine = pass_ref[...].astype(F32)

    @pl.when(core == 0)
    def _():
        sum_ref[...] = own_ref[...] + got_ref[1, 0].astype(F32)
        send_ref[0] = (mine + got_ref[1, 1].astype(F32)).astype(BF)
        send_ref[1] = got_ref[1, 2]

    @pl.when(core == 1)
    def _():
        sum_ref[...] = own_ref[...] + got_ref[0, 2].astype(F32)
        send_ref[0] = got_ref[0, 0]
        send_ref[1] = (mine + got_ref[0, 1].astype(F32)).astype(BF)


def finish_kernel(where_ref, own_ref, far_ref, dk_ref, dv_ref):
    w = dk_ref.shape[1]
    core = lax.rem(where_ref[0], 2)
    total = own_ref[...] + far_ref[0, core].astype(F32) + far_ref[1, core].astype(F32)
    dk_ref[...] = total[:, :w].astype(BF)
    dv_ref[...] = total[:, w:].astype(BF)


def mixed_kernel(x_ref, o_ref, hold_ref, sems):
    copies = [
        pltpu.make_async_copy(x_ref.at[b], hold_ref.at[b], sems.at[b])
        for b in range(x_ref.shape[0])
    ]
    for c in copies:
        c.start()
    total = jnp.zeros(o_ref.shape, F32)
    for b, c in enumerate(copies):
        c.wait()
        total = total + hold_ref[b].astype(F32)
    o_ref[...] = total.astype(BF)


def shifted(x, steps):
    count = lax.axis_size("ctx")
    first, last = max(0, -steps), min(count, count - steps)
    return lax.ppermute(x, "ctx", [(i, i + steps) for i in range(first, last)])


def to_neighbours(x):
    count = lax.axis_size("ctx")
    ahead = [(i, i + 2) for i in range(0, count - 2, 2)]
    back = [(i, i - 2) for i in range(3, count, 2)]
    return lax.ppermute(x, "ctx", ahead + back)


def in_chip(x):
    pairs = [[i, i + 1] for i in range(0, lax.axis_size("ctx"), 2)]
    return lax.all_gather(x, "ctx", axis=0, axis_index_groups=pairs)


def per_device(queries, keys, values, out_weight, mixed_grad, lengths, dilation):
    rows, width = queries.shape
    heads = dilation.shape[0]
    groups = lax.axis_size("head")
    span = mixed_grad.shape[1]
    total = rows * lax.axis_size("ctx")
    where = lax.axis_index("ctx").astype(jnp.int32).reshape(1)
    lens = lengths.reshape(1, -1)

    kv, mgv = call(
        pack_kernel,
        [shape((rows, 2 * width), BF), shape((rows, span), BF)],
        [keys, values, mixed_grad],
        "pack",
        scratch=[pltpu.SemaphoreType.DMA((3,))],
        hbm_in=(0, 1, 2),
    )
    prev = shifted(kv, 2)
    follow = shifted(kv, -2)
    (spread,) = call(
        spread_kernel,
        [shape((groups, rows, span), BF)],
        [mgv],
        "spread",
        scratch=[pltpu.SemaphoreType.DMA((groups,))],
        hbm_out=(0,),
    )
    gathered = lax.all_to_all(spread, "head", 0, 0, tiled=True)
    own2, prev2, next2 = in_chip(kv), in_chip(prev), in_chip(follow)
    part, probs, attn, window = call(
        functools.partial(forward_kernel, heads, total),
        [
            shape((groups, rows, span), BF),
            shape((heads, rows, 5 * rows), BF),
            shape((rows, width), BF),
            shape((5 * rows, 2 * width), BF),
        ],
        [where, dilation, lens, queries, prev2, own2, next2, out_weight],
        "forward",
        flops=80 * 2 * rows * width * (groups * span + 10 * rows),
        scratch=[
            pltpu.VMEM((groups, rows, span), BF),
            pltpu.SemaphoreType.DMA((groups,)),
        ],
        hbm_out=(0,),
    )
    summed = lax.all_to_all(part, "head", 0, 0, tiled=True)
    dq, own, passed, give = call(
        functools.partial(backward_kernel, heads),
        [
            shape((rows, width), BF),
            shape((rows, 2 * width), F32),
            shape((rows, 2 * width), BF),
            shape((3, rows, 2 * width), BF),
        ],
        [where, queries, window, probs, attn, gathered, out_weight],
        "backward",
        flops=2 * rows * width * (groups * span + 20 * rows),
        scratch=[
            pltpu.VMEM((groups, rows, span), BF),
            pltpu.VMEM((rows, width), BF),
            pltpu.VMEM((5, rows, 2 * width), BF),
            pltpu.SemaphoreType.DMA((groups,)),
        ],
        hbm_in=(5,),
    )
    send, own = call(
        share_kernel,
        [shape((2, rows, 2 * width), BF), shape((rows, 2 * width), F32)],
        [where, own, passed, in_chip(give)],
        "share",
    )
    (mixed,) = call(
        mixed_kernel,
        [shape((rows, span), BF)],
        [summed],
        "mixed",
        scratch=[pltpu.VMEM((groups, rows, span), BF), pltpu.SemaphoreType.DMA((groups,))],
        hbm_in=(0,),
    )
    dk, dv = call(
        finish_kernel,
        [shape((rows, width), BF), shape((rows, width), BF)],
        [where, own, in_chip(to_neighbours(send))],
        "finish",
    )
    return mixed, dq, dk, dv


def solution(mesh):
    placed = (
        P("ctx", "head"),
        P("ctx", "head"),
        P("ctx", "head"),
        P("head", None),
        P("ctx", "head"),
        P(),
        P("head"),
    )
    return jax.shard_map(
        per_device,
        mesh=mesh,
        in_specs=placed,
        out_specs=(P("ctx", "head"), P("ctx", "head"), P("ctx", "head"), P("ctx", "head")),
        check_vma=False,
    )
```

```python
import functools

import jax
import jax.numpy as jnp
from jax import lax
from jax.experimental import pallas as pl
from jax.experimental.pallas import tpu as pltpu
from jax.sharding import PartitionSpec as P

HALF = 32
BF = jnp.bfloat16
F32 = jnp.float32
VMEM = pl.BlockSpec(memory_space=pltpu.VMEM)
SMEM = pl.BlockSpec(memory_space=pltpu.SMEM)
HBM = pl.BlockSpec(memory_space=pltpu.HBM)


def dot(a, b, dims):
    return lax.dot_general(a, b, (dims, ((), ())), preferred_element_type=F32)


def call(body, outs, ins, name, flops=0, scratch=(), hbm_in=(), hbm_out=()):
    moved = sum(x.size * x.dtype.itemsize for x in (*ins, *outs))
    held = [
        pltpu.with_memory_space_constraint(x, pltpu.HBM) if i in hbm_in else x
        for i, x in enumerate(ins)
    ]
    return pl.pallas_call(
        body,
        out_shape=[pltpu.HBM(x.shape, x.dtype) if i in hbm_out else x for i, x in enumerate(outs)],
        in_specs=[SMEM if x.ndim == 1 else HBM if i in hbm_in else VMEM for i, x in enumerate(ins)],
        out_specs=[HBM if i in hbm_out else VMEM for i in range(len(outs))],
        scratch_shapes=scratch,
        compiler_params=pltpu.CompilerParams(vmem_limit_bytes=24 << 20),
        cost_estimate=pl.CostEstimate(flops=flops, bytes_accessed=moved, transcendentals=0),
        name=name,
    )(*held)


def shape(dims, dtype):
    return jax.ShapeDtypeStruct(dims, dtype)


def pack_kernel(k_ref, v_ref, mg_ref, kv_ref, mgv_ref, sems):
    w = k_ref.shape[1]
    copies = [
        pltpu.make_async_copy(mg_ref, mgv_ref, sems.at[2]),
        pltpu.make_async_copy(k_ref, kv_ref.at[:, :w], sems.at[0]),
        pltpu.make_async_copy(v_ref, kv_ref.at[:, w:], sems.at[1]),
    ]
    for c in copies:
        c.start()
    for c in copies:
        c.wait()


def spread_kernel(mg_ref, all_ref, sems):
    copies = [
        pltpu.make_async_copy(mg_ref, all_ref.at[b], sems.at[b]) for b in range(all_ref.shape[0])
    ]
    for c in copies:
        c.start()
    for c in copies:
        c.wait()


def document_codes(lens, row_pos, col_pos):
    n = lens.shape[1]
    down = lax.broadcasted_iota(jnp.int32, (n, n), 0)
    across = lax.broadcasted_iota(jnp.int32, (n, n), 1)
    wide = jnp.broadcast_to(lens, (n, n))
    ends_col = jnp.sum(jnp.where(across <= down, wide, 0.0), axis=1, keepdims=True)
    lens_col = jnp.sum(jnp.where(across == down, wide, 0.0), axis=1, keepdims=True)
    ends_row = jnp.sum(jnp.where(down <= across, lens_col, 0.0), axis=0, keepdims=True)
    row_doc = jnp.sum(jnp.where(row_pos >= ends_col, 1.0, 0.0), axis=0, keepdims=True)
    col_doc = jnp.sum(jnp.where(col_pos >= ends_row, 1.0, 0.0), axis=1, keepdims=True)
    return row_doc, col_doc


def forward_kernel(
    heads, total, where_ref, dil_ref, lens_ref, q_ref, prev_ref, own_ref, next_ref, w_ref,
    part_ref, probs_ref, attn_ref, win_ref, hold_ref, sems,
):
    rows = q_ref.shape[0]
    width = q_ref.shape[1]
    hd = width // heads
    keys = win_ref.shape[0]
    slab = where_ref[0]
    core = lax.rem(slab, 2)
    six = [x.at[i] for x in (prev_ref, own_ref, next_ref) for i in range(2)]

    @pl.when(core == 0)
    def _():
        for i in range(5):
            win_ref[i * rows : (i + 1) * rows, :] = six[i][...]

    @pl.when(core == 1)
    def _():
        for i in range(5):
            win_ref[i * rows : (i + 1) * rows, :] = six[i + 1][...]

    first = slab * rows
    row_idx = lax.broadcasted_iota(jnp.int32, (1, keys), 1) + (first - 2 * rows)
    col_idx = lax.broadcasted_iota(jnp.int32, (rows, 1), 0) + first
    row_pos, col_pos = row_idx.astype(F32), col_idx.astype(F32)
    row_doc, col_doc = document_codes(lens_ref[...].astype(F32), row_pos, col_pos)
    inside = (row_pos >= 0.0) & (row_pos < float(total))
    distance = jnp.abs(col_pos - row_pos)
    for h in range(heads):
        stride = dil_ref[h].astype(F32)

        def residue(pos, doc):
            steps = jnp.floor((pos + 0.5) / jnp.full(pos.shape, stride))
            return doc * 8.0 + (pos - steps * stride)

        row_code = jnp.where(inside, residue(row_pos, row_doc), -1.0)
        col_code = residue(col_pos, col_doc)
        mask = (row_code == col_code) & (distance <= stride * float(HALF))
        q = q_ref[:, h * hd : (h + 1) * hd]
        k = win_ref[:, h * hd : (h + 1) * hd]
        v = win_ref[:, width + h * hd : width + (h + 1) * hd]
        s = dot(q, k, ((1,), (1,))) * (hd**-0.5)
        s = jnp.where(mask, s, -jnp.inf)
        top = jnp.max(s, axis=1, keepdims=True)
        e = jnp.exp(s - top)
        probs = (e * (1.0 / jnp.sum(e, axis=1, keepdims=True))).astype(BF)
        probs_ref[h] = probs
        attn_ref[:, h * hd : (h + 1) * hd] = dot(probs, v, ((1,), (0,))).astype(BF)
    attn = attn_ref[...]
    span = part_ref.shape[2]
    copies = []
    for b in range(part_ref.shape[0]):
        hold_ref[b] = dot(attn, w_ref[:, b * span : (b + 1) * span], ((1,), (0,))).astype(BF)
        copies.append(pltpu.make_async_copy(hold_ref.at[b], part_ref.at[b], sems.at[b]))
        copies[-1].start()
    for c in copies:
        c.wait()


def cotangent_kernel(mg_ref, w_ref, ga_ref):
    span = mg_ref.shape[2]
    total = jnp.zeros(ga_ref.shape, F32)
    for b in range(mg_ref.shape[0]):
        total = total + dot(mg_ref[b], w_ref[:, b * span : (b + 1) * span], ((1,), (1,)))
    ga_ref[...] = total.astype(BF)


def backward_kernel(
    heads, where_ref, q_hbm, win_ref, probs_ref, attn_ref, ga_ref,
    dq_ref, own_ref, pass_ref, give_ref, terms_ref, q_ref, sem,
):
    rows = q_ref.shape[0]
    width = q_ref.shape[1]
    fetch = pltpu.make_async_copy(q_hbm, q_ref, sem)
    fetch.start()
    hd = width // heads
    factor = hd**-0.5
    for h in range(heads):
        cols = slice(h * hd, (h + 1) * hd)
        vcols = slice(width + h * hd, width + (h + 1) * hd)
        ga = ga_ref[:, cols]
        delta = jnp.sum(ga.astype(F32) * attn_ref[:, cols].astype(F32), axis=1, keepdims=True)
        grad_prob = dot(ga, win_ref[:, vcols], ((1,), (1,)))
        probs = probs_ref[h]
        slopes = (probs.astype(F32) * (grad_prob - delta)).astype(BF)
        dq_ref[:, cols] = (dot(slopes, win_ref[:, cols], ((1,), (0,))) * factor).astype(BF)
        dv = dot(probs, ga, ((0,), (0,)))
        if h == 0:
            fetch.wait()
        dk = dot(slopes, q_ref[:, cols], ((0,), (0,))) * factor
        for i in range(5):
            part = slice(i * rows, (i + 1) * rows)
            if i == 2:
                own_ref[:, cols] = dk[part]
                own_ref[:, vcols] = dv[part]
            else:
                terms_ref[i, :, cols] = dk[part].astype(BF)
                terms_ref[i, :, vcols] = dv[part].astype(BF)
    core = lax.rem(where_ref[0], 2)
    for value, given, kept in ((0, (0, 1, 3), 4), (1, (1, 3, 4), 0)):

        @pl.when(core == value)
        def _(given=given, kept=kept):
            pass_ref[...] = terms_ref[kept]
            for i, slab in enumerate(given):
                give_ref[i] = terms_ref[slab]


def share_kernel(where_ref, own_ref, pass_ref, got_ref, send_ref, sum_ref):
    core = lax.rem(where_ref[0], 2)
    mine = pass_ref[...].astype(F32)

    @pl.when(core == 0)
    def _():
        sum_ref[...] = own_ref[...] + got_ref[1, 0].astype(F32)
        send_ref[0] = (mine + got_ref[1, 1].astype(F32)).astype(BF)
        send_ref[1] = got_ref[1, 2]

    @pl.when(core == 1)
    def _():
        sum_ref[...] = own_ref[...] + got_ref[0, 2].astype(F32)
        send_ref[0] = got_ref[0, 0]
        send_ref[1] = (mine + got_ref[0, 1].astype(F32)).astype(BF)


def finish_kernel(where_ref, own_ref, far_ref, dk_ref, dv_ref):
    w = dk_ref.shape[1]
    core = lax.rem(where_ref[0], 2)
    total = own_ref[...] + far_ref[0, core].astype(F32) + far_ref[1, core].astype(F32)
    dk_ref[...] = total[:, :w].astype(BF)
    dv_ref[...] = total[:, w:].astype(BF)


def mixed_kernel(x_ref, o_ref):
    total = x_ref[0].astype(F32)
    for b in range(1, x_ref.shape[0]):
        total = total + x_ref[b].astype(F32)
    o_ref[...] = total.astype(BF)


def shifted(x, steps):
    count = lax.axis_size("ctx")
    first, last = max(0, -steps), min(count, count - steps)
    return lax.ppermute(x, "ctx", [(i, i + steps) for i in range(first, last)])


def to_neighbours(x):
    count = lax.axis_size("ctx")
    ahead = [(i, i + 2) for i in range(0, count - 2, 2)]
    back = [(i, i - 2) for i in range(3, count, 2)]
    return lax.ppermute(x, "ctx", ahead + back)


def in_chip(x):
    pairs = [[i, i + 1] for i in range(0, lax.axis_size("ctx"), 2)]
    return lax.all_gather(x, "ctx", axis=0, axis_index_groups=pairs)


def per_device(queries, keys, values, out_weight, mixed_grad, lengths, dilation):
    rows, width = queries.shape
    heads = dilation.shape[0]
    groups = lax.axis_size("head")
    span = mixed_grad.shape[1]
    total = rows * lax.axis_size("ctx")
    where = lax.axis_index("ctx").astype(jnp.int32).reshape(1)
    lens = lengths.reshape(1, -1)

    kv, mgv = call(
        pack_kernel,
        [shape((rows, 2 * width), BF), shape((rows, span), BF)],
        [keys, values, mixed_grad],
        "pack",
        scratch=[pltpu.SemaphoreType.DMA((3,))],
        hbm_in=(0, 1, 2),
    )
    prev = shifted(kv, 2)
    follow = shifted(kv, -2)
    (spread,) = call(
        spread_kernel,
        [shape((groups, rows, span), BF)],
        [mgv],
        "spread",
        scratch=[pltpu.SemaphoreType.DMA((groups,))],
        hbm_out=(0,),
    )
    gathered = lax.all_to_all(spread, "head", 0, 0, tiled=True)
    own2, prev2, next2 = in_chip(kv), in_chip(prev), in_chip(follow)
    part, probs, attn, window = call(
        functools.partial(forward_kernel, heads, total),
        [
            shape((groups, rows, span), BF),
            shape((heads, rows, 5 * rows), BF),
            shape((rows, width), BF),
            shape((5 * rows, 2 * width), BF),
        ],
        [where, dilation, lens, queries, prev2, own2, next2, out_weight],
        "forward",
        flops=80 * 2 * rows * width * (groups * span + 10 * rows),
        scratch=[
            pltpu.VMEM((groups, rows, span), BF),
            pltpu.SemaphoreType.DMA((groups,)),
        ],
        hbm_out=(0,),
    )
    (ga,) = call(
        cotangent_kernel,
        [shape((rows, width), BF)],
        [gathered, out_weight],
        "cotangent",
        flops=2 * rows * width * groups * span,
    )
    ga, part = lax.optimization_barrier((ga, part))
    summed = lax.all_to_all(part, "head", 0, 0, tiled=True)
    dq, own, passed, give = call(
        functools.partial(backward_kernel, heads),
        [
            shape((rows, width), BF),
            shape((rows, 2 * width), F32),
            shape((rows, 2 * width), BF),
            shape((3, rows, 2 * width), BF),
        ],
        [where, queries, window, probs, attn, ga],
        "backward",
        flops=2 * rows * width * 20 * rows,
        scratch=[
            pltpu.VMEM((5, rows, 2 * width), BF),
            pltpu.VMEM((rows, width), BF),
            pltpu.SemaphoreType.DMA,
        ],
        hbm_in=(1,),
    )
    send, own = call(
        share_kernel,
        [shape((2, rows, 2 * width), BF), shape((rows, 2 * width), F32)],
        [where, own, passed, in_chip(give)],
        "share",
    )
    (mixed,) = call(mixed_kernel, [shape((rows, span), BF)], [summed], "mixed")
    arrived, mixed = lax.optimization_barrier((to_neighbours(send), mixed))
    dk, dv = call(
        finish_kernel,
        [shape((rows, width), BF), shape((rows, width), BF)],
        [where, own, in_chip(arrived)],
        "finish",
    )
    return mixed, dq, dk, dv


def solution(mesh):
    placed = (
        P("ctx", "head"),
        P("ctx", "head"),
        P("ctx", "head"),
        P("head", None),
        P("ctx", "head"),
        P(),
        P("head"),
    )
    return jax.shard_map(
        per_device,
        mesh=mesh,
        in_specs=placed,
        out_specs=(P("ctx", "head"), P("ctx", "head"), P("ctx", "head"), P("ctx", "head")),
        check_vma=False,
    )
```

```python
import functools

import jax
import jax.numpy as jnp
from jax import lax
from jax.experimental import pallas as pl
from jax.experimental.pallas import tpu as pltpu
from jax.sharding import PartitionSpec as P

HALF = 32
BF = jnp.bfloat16
F32 = jnp.float32
VMEM = pl.BlockSpec(memory_space=pltpu.VMEM)
SMEM = pl.BlockSpec(memory_space=pltpu.SMEM)
HBM = pl.BlockSpec(memory_space=pltpu.HBM)


def dot(a, b, dims):
    return lax.dot_general(a, b, (dims, ((), ())), preferred_element_type=F32)


def call(body, outs, ins, name, flops=0, scratch=(), hbm_in=(), hbm_out=()):
    moved = sum(x.size * x.dtype.itemsize for x in (*ins, *outs))
    held = [
        pltpu.with_memory_space_constraint(x, pltpu.HBM) if i in hbm_in else x
        for i, x in enumerate(ins)
    ]
    return pl.pallas_call(
        body,
        out_shape=[pltpu.HBM(x.shape, x.dtype) if i in hbm_out else x for i, x in enumerate(outs)],
        in_specs=[SMEM if x.ndim == 1 else HBM if i in hbm_in else VMEM for i, x in enumerate(ins)],
        out_specs=[HBM if i in hbm_out else VMEM for i in range(len(outs))],
        scratch_shapes=scratch,
        compiler_params=pltpu.CompilerParams(vmem_limit_bytes=24 << 20),
        cost_estimate=pl.CostEstimate(flops=flops, bytes_accessed=moved, transcendentals=0),
        name=name,
    )(*held)


def shape(dims, dtype):
    return jax.ShapeDtypeStruct(dims, dtype)


def pack_kernel(k_ref, v_ref, mg_ref, kv_ref, mgv_ref, sems):
    w = k_ref.shape[1]
    copies = [
        pltpu.make_async_copy(mg_ref, mgv_ref, sems.at[2]),
        pltpu.make_async_copy(k_ref, kv_ref.at[:, :w], sems.at[0]),
        pltpu.make_async_copy(v_ref, kv_ref.at[:, w:], sems.at[1]),
    ]
    for c in copies:
        c.start()
    for c in copies:
        c.wait()


def spread_kernel(mg_ref, after_ref, all_ref, sems):
    copies = [
        pltpu.make_async_copy(mg_ref, all_ref.at[b], sems.at[b]) for b in range(all_ref.shape[0])
    ]
    for c in copies:
        c.start()
    for c in copies:
        c.wait()


def document_codes(lens, row_pos, col_pos):
    n = lens.shape[1]
    down = lax.broadcasted_iota(jnp.int32, (n, n), 0)
    across = lax.broadcasted_iota(jnp.int32, (n, n), 1)
    wide = jnp.broadcast_to(lens, (n, n))
    ends_col = jnp.sum(jnp.where(across <= down, wide, 0.0), axis=1, keepdims=True)
    lens_col = jnp.sum(jnp.where(across == down, wide, 0.0), axis=1, keepdims=True)
    ends_row = jnp.sum(jnp.where(down <= across, lens_col, 0.0), axis=0, keepdims=True)
    row_doc = jnp.sum(jnp.where(row_pos >= ends_col, 1.0, 0.0), axis=0, keepdims=True)
    col_doc = jnp.sum(jnp.where(col_pos >= ends_row, 1.0, 0.0), axis=1, keepdims=True)
    return row_doc, col_doc


def forward_kernel(
    heads, total, where_ref, dil_ref, lens_ref, q_ref, own_ref, far_ref, w_ref,
    part_ref, probs_ref, attn_ref, win_ref, hold_ref, sems,
):
    rows = q_ref.shape[0]
    width = q_ref.shape[1]
    hd = width // heads
    keys = win_ref.shape[0]
    slab = where_ref[0]
    core = lax.rem(slab, 2)
    six = [x.at[i] for x in (far_ref.at[0], own_ref, far_ref.at[1]) for i in range(2)]

    @pl.when(core == 0)
    def _():
        for i in range(5):
            win_ref[i * rows : (i + 1) * rows, :] = six[i][...]

    @pl.when(core == 1)
    def _():
        for i in range(5):
            win_ref[i * rows : (i + 1) * rows, :] = six[i + 1][...]

    first = slab * rows
    row_idx = lax.broadcasted_iota(jnp.int32, (1, keys), 1) + (first - 2 * rows)
    col_idx = lax.broadcasted_iota(jnp.int32, (rows, 1), 0) + first
    row_pos, col_pos = row_idx.astype(F32), col_idx.astype(F32)
    row_doc, col_doc = document_codes(lens_ref[...].astype(F32), row_pos, col_pos)
    inside = (row_pos >= 0.0) & (row_pos < float(total))
    distance = jnp.abs(col_pos - row_pos)
    for h in range(heads):
        stride = dil_ref[h].astype(F32)

        def residue(pos, doc):
            steps = jnp.floor((pos + 0.5) / jnp.full(pos.shape, stride))
            return doc * 8.0 + (pos - steps * stride)

        row_code = jnp.where(inside, residue(row_pos, row_doc), -1.0)
        col_code = residue(col_pos, col_doc)
        mask = (row_code == col_code) & (distance <= stride * float(HALF))
        q = q_ref[:, h * hd : (h + 1) * hd]
        k = win_ref[:, h * hd : (h + 1) * hd]
        v = win_ref[:, width + h * hd : width + (h + 1) * hd]
        s = dot(q, k, ((1,), (1,))) * (hd**-0.5)
        s = jnp.where(mask, s, -jnp.inf)
        top = jnp.max(s, axis=1, keepdims=True)
        e = jnp.exp(s - top)
        probs = (e * (1.0 / jnp.sum(e, axis=1, keepdims=True))).astype(BF)
        probs_ref[h] = probs
        attn_ref[:, h * hd : (h + 1) * hd] = dot(probs, v, ((1,), (0,))).astype(BF)
    attn = attn_ref[...]
    span = part_ref.shape[3]
    copies = []
    cols = part_ref.shape[0]
    for b in range(2 * cols):
        row, col = b // cols, b % cols
        hold_ref[b] = dot(attn, w_ref[:, b * span : (b + 1) * span], ((1,), (0,))).astype(BF)
        copies.append(pltpu.make_async_copy(hold_ref.at[b], part_ref.at[col, row], sems.at[b]))
        copies[-1].start()
    for c in copies:
        c.wait()


def cotangent_kernel(mg_ref, w_ref, ga_ref):
    span = mg_ref.shape[2]
    total = jnp.zeros(ga_ref.shape, F32)
    for b in range(mg_ref.shape[0]):
        total = total + dot(mg_ref[b], w_ref[:, b * span : (b + 1) * span], ((1,), (1,)))
    ga_ref[...] = total.astype(BF)


def backward_kernel(
    heads, where_ref, q_hbm, win_ref, probs_ref, attn_ref, ga_ref,
    dq_ref, own_ref, pass_ref, give_ref, terms_ref, q_ref, sem,
):
    rows = q_ref.shape[0]
    width = q_ref.shape[1]
    fetch = pltpu.make_async_copy(q_hbm, q_ref, sem)
    fetch.start()
    hd = width // heads
    factor = hd**-0.5
    for h in range(heads):
        cols = slice(h * hd, (h + 1) * hd)
        vcols = slice(width + h * hd, width + (h + 1) * hd)
        ga = ga_ref[:, cols]
        delta = jnp.sum(ga.astype(F32) * attn_ref[:, cols].astype(F32), axis=1, keepdims=True)
        grad_prob = dot(ga, win_ref[:, vcols], ((1,), (1,)))
        probs = probs_ref[h]
        slopes = (probs.astype(F32) * (grad_prob - delta)).astype(BF)
        dq_ref[:, cols] = (dot(slopes, win_ref[:, cols], ((1,), (0,))) * factor).astype(BF)
        dv = dot(probs, ga, ((0,), (0,)))
        if h == 0:
            fetch.wait()
        dk = dot(slopes, q_ref[:, cols], ((0,), (0,))) * factor
        for i in range(5):
            part = slice(i * rows, (i + 1) * rows)
            if i == 2:
                own_ref[:, cols] = dk[part]
                own_ref[:, vcols] = dv[part]
            else:
                terms_ref[i, :, cols] = dk[part].astype(BF)
                terms_ref[i, :, vcols] = dv[part].astype(BF)
    core = lax.rem(where_ref[0], 2)
    for value, given, kept in ((0, (0, 1, 3), 4), (1, (1, 3, 4), 0)):

        @pl.when(core == value)
        def _(given=given, kept=kept):
            pass_ref[...] = terms_ref[kept]
            for i, slab in enumerate(given):
                give_ref[i] = terms_ref[slab]


def share_kernel(where_ref, own_ref, pass_ref, got_ref, send_ref, sum_ref):
    core = lax.rem(where_ref[0], 2)
    mine = pass_ref[...].astype(F32)

    @pl.when(core == 0)
    def _():
        sum_ref[...] = own_ref[...] + got_ref[1, 0].astype(F32)
        send_ref[0] = (mine + got_ref[1, 1].astype(F32)).astype(BF)
        send_ref[1] = got_ref[1, 2]

    @pl.when(core == 1)
    def _():
        sum_ref[...] = own_ref[...] + got_ref[0, 2].astype(F32)
        send_ref[0] = got_ref[0, 0]
        send_ref[1] = (mine + got_ref[0, 1].astype(F32)).astype(BF)


def finish_kernel(where_ref, own_ref, far_ref, dk_ref, dv_ref):
    w = dk_ref.shape[1]
    core = lax.rem(where_ref[0], 2)
    total = own_ref[...] + far_ref[0, core].astype(F32) + far_ref[1, core].astype(F32)
    dk_ref[...] = total[:, :w].astype(BF)
    dv_ref[...] = total[:, w:].astype(BF)


def row_sum_kernel(where_ref, x_ref, keep_ref, give_ref):
    row = where_ref[1]
    cols = x_ref.shape[0]

    def total(r):
        acc = x_ref[0, r].astype(F32)
        for b in range(1, cols):
            acc = acc + x_ref[b, r].astype(F32)
        return acc

    keep_ref[...] = total(row)
    give_ref[...] = total(1 - row).astype(BF)


def mixed_kernel(where_ref, keep_ref, got_ref, o_ref):
    o_ref[...] = (keep_ref[...] + got_ref[1 - where_ref[1]].astype(F32)).astype(BF)


def to_neighbours(x):
    count = lax.axis_size("ctx")
    ahead = [(i, i + 2) for i in range(0, count - 2, 2)]
    back = [(i, i - 2) for i in range(3, count, 2)]
    return lax.ppermute(x, "ctx", ahead + back)


def in_chip(x):
    pairs = [[i, i + 1] for i in range(0, lax.axis_size("ctx"), 2)]
    return lax.all_gather(x, "ctx", axis=0, axis_index_groups=pairs)


def per_device(queries, keys, values, out_weight, mixed_grad, lengths, dilation):
    rows, width = queries.shape
    heads = dilation.shape[0]
    groups = lax.axis_size("head")
    span = mixed_grad.shape[1]
    total = rows * lax.axis_size("ctx")
    cols = groups // 2
    along_row = [[r * cols + c for c in range(cols)] for r in range(2)]
    across_rows = [[c, cols + c] for c in range(cols)]
    where = jnp.stack([lax.axis_index("ctx"), lax.axis_index("head") // cols]).astype(jnp.int32)
    lens = lengths.reshape(1, -1)

    kv, mgv = call(
        pack_kernel,
        [shape((rows, 2 * width), BF), shape((rows, span), BF)],
        [keys, values, mixed_grad],
        "pack",
        scratch=[pltpu.SemaphoreType.DMA((3,))],
        hbm_in=(0, 1, 2),
    )
    own2 = in_chip(kv)
    near = to_neighbours(own2)
    (spread,) = call(
        spread_kernel,
        [shape((groups, rows, span), BF)],
        [mgv, own2],
        "spread",
        scratch=[pltpu.SemaphoreType.DMA((groups,))],
        hbm_out=(0,),
    )
    gathered = lax.all_to_all(spread, "head", 0, 0, tiled=True)
    far = in_chip(near)
    part, probs, attn, window = call(
        functools.partial(forward_kernel, heads, total),
        [
            shape((groups // 2, 2, rows, span), BF),
            shape((heads, rows, 5 * rows), BF),
            shape((rows, width), BF),
            shape((5 * rows, 2 * width), BF),
        ],
        [where, dilation, lens, queries, own2, far, out_weight],
        "forward",
        flops=80 * 2 * rows * width * (groups * span + 10 * rows),
        scratch=[
            pltpu.VMEM((groups, rows, span), BF),
            pltpu.SemaphoreType.DMA((groups,)),
        ],
        hbm_out=(0,),
    )
    (ga,) = call(
        cotangent_kernel,
        [shape((rows, width), BF)],
        [gathered, out_weight],
        "cotangent",
        flops=2 * rows * width * groups * span,
    )
    ga, part = lax.optimization_barrier((ga, part))
    summed = lax.all_to_all(part, "head", 0, 0, tiled=True, axis_index_groups=along_row)
    dq, own, passed, give = call(
        functools.partial(backward_kernel, heads),
        [
            shape((rows, width), BF),
            shape((rows, 2 * width), F32),
            shape((rows, 2 * width), BF),
            shape((3, rows, 2 * width), BF),
        ],
        [where, queries, window, probs, attn, ga],
        "backward",
        flops=2 * rows * width * 20 * rows,
        scratch=[
            pltpu.VMEM((5, rows, 2 * width), BF),
            pltpu.VMEM((rows, width), BF),
            pltpu.SemaphoreType.DMA,
        ],
        hbm_in=(1,),
    )
    send, own = call(
        share_kernel,
        [shape((2, rows, 2 * width), BF), shape((rows, 2 * width), F32)],
        [where, own, passed, in_chip(give)],
        "share",
    )
    mine, yours = call(
        row_sum_kernel,
        [shape((rows, span), F32), shape((rows, span), BF)],
        [where, summed],
        "rowsum",
    )
    both = lax.all_gather(yours, "head", axis=0, axis_index_groups=across_rows)
    (mixed,) = call(mixed_kernel, [shape((rows, span), BF)], [where, mine, both], "mixed")
    arrived, mixed = lax.optimization_barrier((to_neighbours(send), mixed))
    dk, dv = call(
        finish_kernel,
        [shape((rows, width), BF), shape((rows, width), BF)],
        [where, own, in_chip(arrived)],
        "finish",
    )
    return mixed, dq, dk, dv


def solution(mesh):
    placed = (
        P("ctx", "head"),
        P("ctx", "head"),
        P("ctx", "head"),
        P("head", None),
        P("ctx", "head"),
        P(),
        P("head"),
    )
    return jax.shard_map(
        per_device,
        mesh=mesh,
        in_specs=placed,
        out_specs=(P("ctx", "head"), P("ctx", "head"), P("ctx", "head"), P("ctx", "head")),
        check_vma=False,
    )
```

```python
import functools

import jax
import jax.numpy as jnp
from jax import lax
from jax.experimental import pallas as pl
from jax.experimental.pallas import tpu as pltpu
from jax.sharding import PartitionSpec as P

HALF = 32
BF = jnp.bfloat16
F32 = jnp.float32
VMEM = pl.BlockSpec(memory_space=pltpu.VMEM)
SMEM = pl.BlockSpec(memory_space=pltpu.SMEM)
HBM = pl.BlockSpec(memory_space=pltpu.HBM)


def dot(a, b, dims):
    return lax.dot_general(a, b, (dims, ((), ())), preferred_element_type=F32)


def call(body, outs, ins, name, flops=0, scratch=(), hbm_in=(), hbm_out=()):
    moved = sum(x.size * x.dtype.itemsize for x in (*ins, *outs))
    held = [
        pltpu.with_memory_space_constraint(x, pltpu.HBM) if i in hbm_in else x
        for i, x in enumerate(ins)
    ]
    return pl.pallas_call(
        body,
        out_shape=[pltpu.HBM(x.shape, x.dtype) if i in hbm_out else x for i, x in enumerate(outs)],
        in_specs=[SMEM if x.ndim == 1 else HBM if i in hbm_in else VMEM for i, x in enumerate(ins)],
        out_specs=[HBM if i in hbm_out else VMEM for i in range(len(outs))],
        scratch_shapes=scratch,
        compiler_params=pltpu.CompilerParams(vmem_limit_bytes=24 << 20),
        cost_estimate=pl.CostEstimate(flops=flops, bytes_accessed=moved, transcendentals=0),
        name=name,
    )(*held)


def shape(dims, dtype):
    return jax.ShapeDtypeStruct(dims, dtype)


def pack_kernel(k_ref, v_ref, mg_ref, kv_ref, mgv_ref, sems):
    w = k_ref.shape[1]
    copies = [
        pltpu.make_async_copy(mg_ref, mgv_ref, sems.at[2]),
        pltpu.make_async_copy(k_ref, kv_ref.at[:, :w], sems.at[0]),
        pltpu.make_async_copy(v_ref, kv_ref.at[:, w:], sems.at[1]),
    ]
    for c in copies:
        c.start()
    for c in copies:
        c.wait()


def spread_kernel(row_ref, mine_ref, yours_ref, after_ref, all_ref, sems):
    row = row_ref[0]
    copies = []
    for c in range(all_ref.shape[0]):
        copies.append(pltpu.make_async_copy(mine_ref, all_ref.at[c, row], sems.at[2 * c]))
        copies.append(pltpu.make_async_copy(yours_ref, all_ref.at[c, 1 - row], sems.at[2 * c + 1]))
    for c in copies:
        c.start()
    for c in copies:
        c.wait()


def document_codes(lens, row_pos, col_pos):
    n = lens.shape[1]
    down = lax.broadcasted_iota(jnp.int32, (n, n), 0)
    across = lax.broadcasted_iota(jnp.int32, (n, n), 1)
    wide = jnp.broadcast_to(lens, (n, n))
    ends_col = jnp.sum(jnp.where(across <= down, wide, 0.0), axis=1, keepdims=True)
    lens_col = jnp.sum(jnp.where(across == down, wide, 0.0), axis=1, keepdims=True)
    ends_row = jnp.sum(jnp.where(down <= across, lens_col, 0.0), axis=0, keepdims=True)
    row_doc = jnp.sum(jnp.where(row_pos >= ends_col, 1.0, 0.0), axis=0, keepdims=True)
    col_doc = jnp.sum(jnp.where(col_pos >= ends_row, 1.0, 0.0), axis=1, keepdims=True)
    return row_doc, col_doc


def forward_kernel(
    heads, total, where_ref, dil_ref, lens_ref, q_ref, own_ref, far_ref, w_ref,
    part_ref, probs_ref, attn_ref, win_ref, hold_ref, sems,
):
    rows = q_ref.shape[0]
    width = q_ref.shape[1]
    hd = width // heads
    keys = win_ref.shape[0]
    slab = where_ref[0]
    core = lax.rem(slab, 2)
    six = [x.at[i] for x in (far_ref.at[0], own_ref, far_ref.at[1]) for i in range(2)]

    @pl.when(core == 0)
    def _():
        for i in range(5):
            win_ref[i * rows : (i + 1) * rows, :] = six[i][...]

    @pl.when(core == 1)
    def _():
        for i in range(5):
            win_ref[i * rows : (i + 1) * rows, :] = six[i + 1][...]

    first = slab * rows
    row_idx = lax.broadcasted_iota(jnp.int32, (1, keys), 1) + (first - 2 * rows)
    col_idx = lax.broadcasted_iota(jnp.int32, (rows, 1), 0) + first
    row_pos, col_pos = row_idx.astype(F32), col_idx.astype(F32)
    row_doc, col_doc = document_codes(lens_ref[...].astype(F32), row_pos, col_pos)
    inside = (row_pos >= 0.0) & (row_pos < float(total))
    distance = jnp.abs(col_pos - row_pos)
    for h in range(heads):
        stride = dil_ref[h].astype(F32)

        def residue(pos, doc):
            steps = jnp.floor((pos + 0.5) / jnp.full(pos.shape, stride))
            return doc * 8.0 + (pos - steps * stride)

        row_code = jnp.where(inside, residue(row_pos, row_doc), -1.0)
        col_code = residue(col_pos, col_doc)
        mask = (row_code == col_code) & (distance <= stride * float(HALF))
        q = q_ref[:, h * hd : (h + 1) * hd]
        k = win_ref[:, h * hd : (h + 1) * hd]
        v = win_ref[:, width + h * hd : width + (h + 1) * hd]
        s = dot(q, k, ((1,), (1,))) * (hd**-0.5)
        s = jnp.where(mask, s, -jnp.inf)
        top = jnp.max(s, axis=1, keepdims=True)
        e = jnp.exp(s - top)
        probs = (e * (1.0 / jnp.sum(e, axis=1, keepdims=True))).astype(BF)
        probs_ref[h] = probs
        attn_ref[:, h * hd : (h + 1) * hd] = dot(probs, v, ((1,), (0,))).astype(BF)
    attn = attn_ref[...]
    span = part_ref.shape[3]
    copies = []
    cols = part_ref.shape[0]
    for b in range(2 * cols):
        row, col = b // cols, b % cols
        hold_ref[b] = dot(attn, w_ref[:, b * span : (b + 1) * span], ((1,), (0,))).astype(BF)
        copies.append(pltpu.make_async_copy(hold_ref.at[b], part_ref.at[col, row], sems.at[b]))
        copies[-1].start()
    for c in copies:
        c.wait()


def cotangent_kernel(mg_ref, w_ref, ga_ref):
    cols, span = mg_ref.shape[0], mg_ref.shape[3]
    total = jnp.zeros(ga_ref.shape, F32)
    for b in range(2 * cols):
        block = mg_ref[b % cols, b // cols]
        total = total + dot(block, w_ref[:, b * span : (b + 1) * span], ((1,), (1,)))
    ga_ref[...] = total.astype(BF)


def backward_kernel(
    heads, where_ref, q_hbm, win_ref, probs_ref, attn_ref, ga_ref,
    dq_ref, own_ref, pass_ref, give_ref, terms_ref, q_ref, sem,
):
    rows = q_ref.shape[0]
    width = q_ref.shape[1]
    fetch = pltpu.make_async_copy(q_hbm, q_ref, sem)
    fetch.start()
    hd = width // heads
    factor = hd**-0.5
    for h in range(heads):
        cols = slice(h * hd, (h + 1) * hd)
        vcols = slice(width + h * hd, width + (h + 1) * hd)
        ga = ga_ref[:, cols]
        delta = jnp.sum(ga.astype(F32) * attn_ref[:, cols].astype(F32), axis=1, keepdims=True)
        grad_prob = dot(ga, win_ref[:, vcols], ((1,), (1,)))
        probs = probs_ref[h]
        slopes = (probs.astype(F32) * (grad_prob - delta)).astype(BF)
        dq_ref[:, cols] = (dot(slopes, win_ref[:, cols], ((1,), (0,))) * factor).astype(BF)
        dv = dot(probs, ga, ((0,), (0,)))
        if h == 0:
            fetch.wait()
        dk = dot(slopes, q_ref[:, cols], ((0,), (0,))) * factor
        for i in range(5):
            part = slice(i * rows, (i + 1) * rows)
            if i == 2:
                own_ref[:, cols] = dk[part]
                own_ref[:, vcols] = dv[part]
            else:
                terms_ref[i, :, cols] = dk[part].astype(BF)
                terms_ref[i, :, vcols] = dv[part].astype(BF)
    core = lax.rem(where_ref[0], 2)
    for value, given, kept in ((0, (0, 1, 3), 4), (1, (1, 3, 4), 0)):

        @pl.when(core == value)
        def _(given=given, kept=kept):
            pass_ref[...] = terms_ref[kept]
            for i, slab in enumerate(given):
                give_ref[i] = terms_ref[slab]


def share_kernel(where_ref, own_ref, pass_ref, got_ref, send_ref, sum_ref):
    core = lax.rem(where_ref[0], 2)
    mine = pass_ref[...].astype(F32)

    @pl.when(core == 0)
    def _():
        sum_ref[...] = own_ref[...] + got_ref[1, 0].astype(F32)
        send_ref[0] = (mine + got_ref[1, 1].astype(F32)).astype(BF)
        send_ref[1] = got_ref[1, 2]

    @pl.when(core == 1)
    def _():
        sum_ref[...] = own_ref[...] + got_ref[0, 2].astype(F32)
        send_ref[0] = got_ref[0, 0]
        send_ref[1] = (mine + got_ref[0, 1].astype(F32)).astype(BF)


def finish_kernel(where_ref, own_ref, far_ref, dk_ref, dv_ref):
    w = dk_ref.shape[1]
    core = lax.rem(where_ref[0], 2)
    total = own_ref[...] + far_ref[0, core].astype(F32) + far_ref[1, core].astype(F32)
    dk_ref[...] = total[:, :w].astype(BF)
    dv_ref[...] = total[:, w:].astype(BF)


def row_sum_kernel(row_ref, x_ref, keep_ref, give_ref):
    row = row_ref[0]
    cols = x_ref.shape[0]

    def total(r):
        acc = x_ref[0, r].astype(F32)
        for b in range(1, cols):
            acc = acc + x_ref[b, r].astype(F32)
        return acc

    keep_ref[...] = total(row)
    give_ref[...] = total(1 - row).astype(BF)


def mixed_kernel(keep_ref, got_ref, o_ref):
    o_ref[...] = (keep_ref[...] + got_ref[...].astype(F32)).astype(BF)


def to_neighbours(x):
    count = lax.axis_size("ctx")
    ahead = [(i, i + 2) for i in range(0, count - 2, 2)]
    back = [(i, i - 2) for i in range(3, count, 2)]
    return lax.ppermute(x, "ctx", ahead + back)


def in_chip(x):
    pairs = [[i, i + 1] for i in range(0, lax.axis_size("ctx"), 2)]
    return lax.all_gather(x, "ctx", axis=0, axis_index_groups=pairs)


def per_device(queries, keys, values, out_weight, mixed_grad, lengths, dilation):
    rows, width = queries.shape
    heads = dilation.shape[0]
    groups = lax.axis_size("head")
    span = mixed_grad.shape[1]
    total = rows * lax.axis_size("ctx")
    cols = groups // 2
    along_row = [[r * cols + c for c in range(cols)] for r in range(2)]
    where = lax.axis_index("ctx").astype(jnp.int32).reshape(1)
    row = (lax.axis_index("head").astype(jnp.int32) // cols).reshape(1)
    other_row = [(i, (i + cols) % groups) for i in range(groups)]
    lens = lengths.reshape(1, -1)

    kv, mgv = call(
        pack_kernel,
        [shape((rows, 2 * width), BF), shape((rows, span), BF)],
        [keys, values, mixed_grad],
        "pack",
        scratch=[pltpu.SemaphoreType.DMA((3,))],
        hbm_in=(0, 1, 2),
    )
    mg_other = lax.ppermute(mixed_grad, "head", other_row)
    own2, mg_other = lax.optimization_barrier((in_chip(kv), mg_other))
    near = to_neighbours(own2)
    (spread,) = call(
        spread_kernel,
        [shape((cols, 2, rows, span), BF)],
        [row, mgv, mg_other, own2],
        "spread",
        scratch=[pltpu.SemaphoreType.DMA((groups,))],
        hbm_out=(0,),
    )
    gathered = lax.all_to_all(spread, "head", 0, 0, tiled=True, axis_index_groups=along_row)
    far = in_chip(near)
    part, probs, attn, window = call(
        functools.partial(forward_kernel, heads, total),
        [
            shape((groups // 2, 2, rows, span), BF),
            shape((heads, rows, 5 * rows), BF),
            shape((rows, width), BF),
            shape((5 * rows, 2 * width), BF),
        ],
        [where, dilation, lens, queries, own2, far, out_weight],
        "forward",
        flops=80 * 2 * rows * width * (groups * span + 10 * rows),
        scratch=[
            pltpu.VMEM((groups, rows, span), BF),
            pltpu.SemaphoreType.DMA((groups,)),
        ],
        hbm_out=(0,),
    )
    (ga,) = call(
        cotangent_kernel,
        [shape((rows, width), BF)],
        [gathered, out_weight],
        "cotangent",
        flops=2 * rows * width * groups * span,
    )
    ga, part = lax.optimization_barrier((ga, part))
    summed = lax.all_to_all(part, "head", 0, 0, tiled=True, axis_index_groups=along_row)
    dq, own, passed, give = call(
        functools.partial(backward_kernel, heads),
        [
            shape((rows, width), BF),
            shape((rows, 2 * width), F32),
            shape((rows, 2 * width), BF),
            shape((3, rows, 2 * width), BF),
        ],
        [where, queries, window, probs, attn, ga],
        "backward",
        flops=2 * rows * width * 20 * rows,
        scratch=[
            pltpu.VMEM((5, rows, 2 * width), BF),
            pltpu.VMEM((rows, width), BF),
            pltpu.SemaphoreType.DMA,
        ],
        hbm_in=(1,),
    )
    send, own = call(
        share_kernel,
        [shape((2, rows, 2 * width), BF), shape((rows, 2 * width), F32)],
        [where, own, passed, in_chip(give)],
        "share",
    )
    mine, yours = call(
        row_sum_kernel,
        [shape((rows, span), F32), shape((rows, span), BF)],
        [row, summed],
        "rowsum",
    )
    yours = lax.ppermute(yours, "head", other_row)
    (mixed,) = call(mixed_kernel, [shape((rows, span), BF)], [mine, yours], "mixed")
    dk, dv = call(
        finish_kernel,
        [shape((rows, width), BF), shape((rows, width), BF)],
        [where, own, in_chip(to_neighbours(send))],
        "finish",
    )
    return mixed, dq, dk, dv


def solution(mesh):
    placed = (
        P("ctx", "head"),
        P("ctx", "head"),
        P("ctx", "head"),
        P("head", None),
        P("ctx", "head"),
        P(),
        P("head"),
    )
    return jax.shard_map(
        per_device,
        mesh=mesh,
        in_specs=placed,
        out_specs=(P("ctx", "head"), P("ctx", "head"), P("ctx", "head"), P("ctx", "head")),
        check_vma=False,
    )
```

```python
import functools

import jax
import jax.numpy as jnp
from jax import lax
from jax.experimental import pallas as pl
from jax.experimental.pallas import tpu as pltpu
from jax.sharding import PartitionSpec as P

HALF = 32
BF = jnp.bfloat16
F32 = jnp.float32
VMEM = pl.BlockSpec(memory_space=pltpu.VMEM)
SMEM = pl.BlockSpec(memory_space=pltpu.SMEM)
HBM = pl.BlockSpec(memory_space=pltpu.HBM)


def dot(a, b, dims):
    return lax.dot_general(a, b, (dims, ((), ())), preferred_element_type=F32)


def call(body, outs, ins, name, flops=0, scratch=(), hbm_in=(), hbm_out=()):
    moved = sum(x.size * x.dtype.itemsize for x in (*ins, *outs))
    held = [
        pltpu.with_memory_space_constraint(x, pltpu.HBM) if i in hbm_in else x
        for i, x in enumerate(ins)
    ]
    return pl.pallas_call(
        body,
        out_shape=[pltpu.HBM(x.shape, x.dtype) if i in hbm_out else x for i, x in enumerate(outs)],
        in_specs=[SMEM if x.ndim == 1 else HBM if i in hbm_in else VMEM for i, x in enumerate(ins)],
        out_specs=[HBM if i in hbm_out else VMEM for i in range(len(outs))],
        scratch_shapes=scratch,
        compiler_params=pltpu.CompilerParams(vmem_limit_bytes=24 << 20),
        cost_estimate=pl.CostEstimate(flops=flops, bytes_accessed=moved, transcendentals=0),
        name=name,
    )(*held)


def shape(dims, dtype):
    return jax.ShapeDtypeStruct(dims, dtype)


def pack_kernel(k_ref, v_ref, mg_ref, kv_ref, mgv_ref, sems):
    w = k_ref.shape[1]
    copies = [
        pltpu.make_async_copy(mg_ref, mgv_ref, sems.at[2]),
        pltpu.make_async_copy(k_ref, kv_ref.at[:, :w], sems.at[0]),
        pltpu.make_async_copy(v_ref, kv_ref.at[:, w:], sems.at[1]),
    ]
    for c in copies:
        c.start()
    for c in copies:
        c.wait()


def spread_kernel(mg_ref, after_ref, all_ref, sems):
    copies = [
        pltpu.make_async_copy(mg_ref, all_ref.at[b], sems.at[b]) for b in range(all_ref.shape[0])
    ]
    for c in copies:
        c.start()
    for c in copies:
        c.wait()


def document_codes(lens, row_pos, col_pos):
    n = lens.shape[1]
    down = lax.broadcasted_iota(jnp.int32, (n, n), 0)
    across = lax.broadcasted_iota(jnp.int32, (n, n), 1)
    wide = jnp.broadcast_to(lens, (n, n))
    ends_col = jnp.sum(jnp.where(across <= down, wide, 0.0), axis=1, keepdims=True)
    lens_col = jnp.sum(jnp.where(across == down, wide, 0.0), axis=1, keepdims=True)
    ends_row = jnp.sum(jnp.where(down <= across, lens_col, 0.0), axis=0, keepdims=True)
    row_doc = jnp.sum(jnp.where(row_pos >= ends_col, 1.0, 0.0), axis=0, keepdims=True)
    col_doc = jnp.sum(jnp.where(col_pos >= ends_row, 1.0, 0.0), axis=1, keepdims=True)
    return row_doc, col_doc


def forward_kernel(
    heads, total, where_ref, row_ref, dil_ref, lens_ref, q_ref, own_ref, far_ref, w_ref,
    keep_ref, give_ref, probs_ref, attn_ref, win_ref,
):
    rows = q_ref.shape[0]
    width = q_ref.shape[1]
    hd = width // heads
    keys = win_ref.shape[0]
    slab = where_ref[0]
    core = lax.rem(slab, 2)
    six = [x.at[i] for x in (far_ref.at[0], own_ref, far_ref.at[1]) for i in range(2)]

    @pl.when(core == 0)
    def _():
        for i in range(5):
            win_ref[i * rows : (i + 1) * rows, :] = six[i][...]

    @pl.when(core == 1)
    def _():
        for i in range(5):
            win_ref[i * rows : (i + 1) * rows, :] = six[i + 1][...]

    first = slab * rows
    row_idx = lax.broadcasted_iota(jnp.int32, (1, keys), 1) + (first - 2 * rows)
    col_idx = lax.broadcasted_iota(jnp.int32, (rows, 1), 0) + first
    row_pos, col_pos = row_idx.astype(F32), col_idx.astype(F32)
    row_doc, col_doc = document_codes(lens_ref[...].astype(F32), row_pos, col_pos)
    inside = (row_pos >= 0.0) & (row_pos < float(total))
    distance = jnp.abs(col_pos - row_pos)
    for h in range(heads):
        stride = dil_ref[h].astype(F32)

        def residue(pos, doc):
            steps = jnp.floor((pos + 0.5) / jnp.full(pos.shape, stride))
            return doc * 8.0 + (pos - steps * stride)

        row_code = jnp.where(inside, residue(row_pos, row_doc), -1.0)
        col_code = residue(col_pos, col_doc)
        mask = (row_code == col_code) & (distance <= stride * float(HALF))
        q = q_ref[:, h * hd : (h + 1) * hd]
        k = win_ref[:, h * hd : (h + 1) * hd]
        v = win_ref[:, width + h * hd : width + (h + 1) * hd]
        s = dot(q, k, ((1,), (1,))) * (hd**-0.5)
        s = jnp.where(mask, s, -jnp.inf)
        top = jnp.max(s, axis=1, keepdims=True)
        e = jnp.exp(s - top)
        probs = (e * (1.0 / jnp.sum(e, axis=1, keepdims=True))).astype(BF)
        probs_ref[h] = probs
        attn_ref[:, h * hd : (h + 1) * hd] = dot(probs, v, ((1,), (0,))).astype(BF)
    attn = attn_ref[...]
    cols, span = keep_ref.shape[0], keep_ref.shape[2]
    row = row_ref[0]
    for r, half_ref in ((1 - row, give_ref), (row, keep_ref)):
        for c in range(cols):
            block = pl.ds(pl.multiple_of((r * cols + c) * span, span), span)
            half_ref[c] = dot(attn, w_ref[:, block], ((1,), (0,))).astype(BF)


def cotangent_kernel(mg_ref, w_ref, ga_ref):
    span = mg_ref.shape[2]
    total = jnp.zeros(ga_ref.shape, F32)
    for b in range(mg_ref.shape[0]):
        total = total + dot(mg_ref[b], w_ref[:, b * span : (b + 1) * span], ((1,), (1,)))
    ga_ref[...] = total.astype(BF)


def backward_kernel(
    heads, where_ref, q_hbm, win_ref, probs_ref, attn_ref, ga_ref,
    dq_ref, own_ref, pass_ref, give_ref, terms_ref, q_ref, sem,
):
    rows = q_ref.shape[0]
    width = q_ref.shape[1]
    fetch = pltpu.make_async_copy(q_hbm, q_ref, sem)
    fetch.start()
    hd = width // heads
    factor = hd**-0.5
    for h in range(heads):
        cols = slice(h * hd, (h + 1) * hd)
        vcols = slice(width + h * hd, width + (h + 1) * hd)
        ga = ga_ref[:, cols]
        delta = jnp.sum(ga.astype(F32) * attn_ref[:, cols].astype(F32), axis=1, keepdims=True)
        grad_prob = dot(ga, win_ref[:, vcols], ((1,), (1,)))
        probs = probs_ref[h]
        slopes = (probs.astype(F32) * (grad_prob - delta)).astype(BF)
        dq_ref[:, cols] = (dot(slopes, win_ref[:, cols], ((1,), (0,))) * factor).astype(BF)
        dv = dot(probs, ga, ((0,), (0,)))
        if h == 0:
            fetch.wait()
        dk = dot(slopes, q_ref[:, cols], ((0,), (0,))) * factor
        for i in range(5):
            part = slice(i * rows, (i + 1) * rows)
            if i == 2:
                own_ref[:, cols] = dk[part]
                own_ref[:, vcols] = dv[part]
            else:
                terms_ref[i, :, cols] = dk[part].astype(BF)
                terms_ref[i, :, vcols] = dv[part].astype(BF)
    core = lax.rem(where_ref[0], 2)
    for value, given, kept in ((0, (0, 1, 3), 4), (1, (1, 3, 4), 0)):

        @pl.when(core == value)
        def _(given=given, kept=kept):
            pass_ref[...] = terms_ref[kept]
            for i, slab in enumerate(given):
                give_ref[i] = terms_ref[slab]


def share_kernel(where_ref, own_ref, pass_ref, got_ref, send_ref, sum_ref):
    core = lax.rem(where_ref[0], 2)
    mine = pass_ref[...].astype(F32)

    @pl.when(core == 0)
    def _():
        sum_ref[...] = own_ref[...] + got_ref[1, 0].astype(F32)
        send_ref[0] = (mine + got_ref[1, 1].astype(F32)).astype(BF)
        send_ref[1] = got_ref[1, 2]

    @pl.when(core == 1)
    def _():
        sum_ref[...] = own_ref[...] + got_ref[0, 2].astype(F32)
        send_ref[0] = got_ref[0, 0]
        send_ref[1] = (mine + got_ref[0, 1].astype(F32)).astype(BF)


def finish_kernel(where_ref, own_ref, far_ref, dk_ref, dv_ref):
    w = dk_ref.shape[1]
    core = lax.rem(where_ref[0], 2)
    total = own_ref[...] + far_ref[0, core].astype(F32) + far_ref[1, core].astype(F32)
    dk_ref[...] = total[:, :w].astype(BF)
    dv_ref[...] = total[:, w:].astype(BF)


def rows_kernel(keep_ref, got_ref, after_ref, out_ref, hold_ref, sems):
    copies = []
    for c in range(keep_ref.shape[0]):
        hold_ref[c] = (keep_ref[c].astype(F32) + got_ref[c].astype(F32)).astype(BF)
        copies.append(pltpu.make_async_copy(hold_ref.at[c], out_ref.at[c], sems.at[c]))
        copies[-1].start()
    for c in copies:
        c.wait()


def mixed_kernel(x_ref, o_ref):
    total = x_ref[0].astype(F32)
    for c in range(1, x_ref.shape[0]):
        total = total + x_ref[c].astype(F32)
    o_ref[...] = total.astype(BF)


def to_neighbours(x):
    count = lax.axis_size("ctx")
    ahead = [(i, i + 2) for i in range(0, count - 2, 2)]
    back = [(i, i - 2) for i in range(3, count, 2)]
    return lax.ppermute(x, "ctx", ahead + back)


def in_chip(x):
    pairs = [[i, i + 1] for i in range(0, lax.axis_size("ctx"), 2)]
    return lax.all_gather(x, "ctx", axis=0, axis_index_groups=pairs)


def per_device(queries, keys, values, out_weight, mixed_grad, lengths, dilation):
    rows, width = queries.shape
    heads = dilation.shape[0]
    groups = lax.axis_size("head")
    span = mixed_grad.shape[1]
    total = rows * lax.axis_size("ctx")
    cols = groups // 2
    along_row = [[r * cols + c for c in range(cols)] for r in range(2)]
    where = lax.axis_index("ctx").astype(jnp.int32).reshape(1)
    row = (lax.axis_index("head").astype(jnp.int32) // cols).reshape(1)
    other_row = [(i, (i + cols) % groups) for i in range(groups)]
    lens = lengths.reshape(1, -1)

    kv, mgv = call(
        pack_kernel,
        [shape((rows, 2 * width), BF), shape((rows, span), BF)],
        [keys, values, mixed_grad],
        "pack",
        scratch=[pltpu.SemaphoreType.DMA((3,))],
        hbm_in=(0, 1, 2),
    )
    own2 = in_chip(kv)
    near = to_neighbours(own2)
    (spread,) = call(
        spread_kernel,
        [shape((groups, rows, span), BF)],
        [mgv, own2],
        "spread",
        scratch=[pltpu.SemaphoreType.DMA((groups,))],
        hbm_out=(0,),
    )
    gathered = lax.all_to_all(spread, "head", 0, 0, tiled=True)
    far = in_chip(near)
    keep, give, probs, attn, window = call(
        functools.partial(forward_kernel, heads, total),
        [
            shape((cols, rows, span), BF),
            shape((cols, rows, span), BF),
            shape((heads, rows, 5 * rows), BF),
            shape((rows, width), BF),
            shape((5 * rows, 2 * width), BF),
        ],
        [where, row, dilation, lens, queries, own2, far, out_weight],
        "forward",
        flops=80 * 2 * rows * width * (groups * span + 10 * rows),
    )
    got_half = lax.ppermute(give, "head", other_row)
    (ga,) = call(
        cotangent_kernel,
        [shape((rows, width), BF)],
        [gathered, out_weight],
        "cotangent",
        flops=2 * rows * width * groups * span,
    )
    dq, own, passed, terms = call(
        functools.partial(backward_kernel, heads),
        [
            shape((rows, width), BF),
            shape((rows, 2 * width), F32),
            shape((rows, 2 * width), BF),
            shape((3, rows, 2 * width), BF),
        ],
        [where, queries, window, probs, attn, ga],
        "backward",
        flops=2 * rows * width * 20 * rows,
        scratch=[
            pltpu.VMEM((5, rows, 2 * width), BF),
            pltpu.VMEM((rows, width), BF),
            pltpu.SemaphoreType.DMA,
        ],
        hbm_in=(1,),
    )
    send, own = call(
        share_kernel,
        [shape((2, rows, 2 * width), BF), shape((rows, 2 * width), F32)],
        [where, own, passed, in_chip(terms)],
        "share",
    )
    (half,) = call(
        rows_kernel,
        [shape((cols, rows, span), BF)],
        [keep, got_half, send],
        "rows",
        scratch=[pltpu.VMEM((cols, rows, span), BF), pltpu.SemaphoreType.DMA((cols,))],
        hbm_out=(0,),
    )
    summed = lax.all_to_all(half, "head", 0, 0, tiled=True, axis_index_groups=along_row)
    (mixed,) = call(mixed_kernel, [shape((rows, span), BF)], [summed], "mixed")
    dk, dv = call(
        finish_kernel,
        [shape((rows, width), BF), shape((rows, width), BF)],
        [where, own, in_chip(to_neighbours(send))],
        "finish",
    )
    return mixed, dq, dk, dv


def solution(mesh):
    placed = (
        P("ctx", "head"),
        P("ctx", "head"),
        P("ctx", "head"),
        P("head", None),
        P("ctx", "head"),
        P(),
        P("head"),
    )
    return jax.shard_map(
        per_device,
        mesh=mesh,
        in_specs=placed,
        out_specs=(P("ctx", "head"), P("ctx", "head"), P("ctx", "head"), P("ctx", "head")),
        check_vma=False,
    )
```

```python
import functools

import jax
import jax.numpy as jnp
from jax import lax
from jax.experimental import pallas as pl
from jax.experimental.pallas import tpu as pltpu
from jax.sharding import PartitionSpec as P

HALF = 32
BF = jnp.bfloat16
F32 = jnp.float32
VMEM = pl.BlockSpec(memory_space=pltpu.VMEM)
SMEM = pl.BlockSpec(memory_space=pltpu.SMEM)
HBM = pl.BlockSpec(memory_space=pltpu.HBM)


def dot(a, b, dims):
    return lax.dot_general(a, b, (dims, ((), ())), preferred_element_type=F32)


def call(body, outs, ins, name, flops=0, scratch=(), hbm_in=(), hbm_out=()):
    moved = sum(x.size * x.dtype.itemsize for x in (*ins, *outs))
    held = [
        pltpu.with_memory_space_constraint(x, pltpu.HBM) if i in hbm_in else x
        for i, x in enumerate(ins)
    ]
    return pl.pallas_call(
        body,
        out_shape=[pltpu.HBM(x.shape, x.dtype) if i in hbm_out else x for i, x in enumerate(outs)],
        in_specs=[SMEM if x.ndim == 1 else HBM if i in hbm_in else VMEM for i, x in enumerate(ins)],
        out_specs=[HBM if i in hbm_out else VMEM for i in range(len(outs))],
        scratch_shapes=scratch,
        compiler_params=pltpu.CompilerParams(vmem_limit_bytes=24 << 20),
        cost_estimate=pl.CostEstimate(flops=flops, bytes_accessed=moved, transcendentals=0),
        name=name,
    )(*held)


def shape(dims, dtype):
    return jax.ShapeDtypeStruct(dims, dtype)


def pack_kernel(k_ref, v_ref, q_ref, mg_ref, kvq_ref, mgv_ref, sems):
    w = k_ref.shape[1]
    copies = [pltpu.make_async_copy(mg_ref, mgv_ref, sems.at[3])]
    for i, x_ref in enumerate((k_ref, v_ref, q_ref)):
        part = kvq_ref.at[:, i * w : (i + 1) * w]
        copies.append(pltpu.make_async_copy(x_ref, part, sems.at[i]))
    for c in copies:
        c.start()
    for c in copies:
        c.wait()


def spread_kernel(mg_ref, after_ref, all_ref, sems):
    copies = [
        pltpu.make_async_copy(mg_ref, all_ref.at[b], sems.at[b]) for b in range(all_ref.shape[0])
    ]
    for c in copies:
        c.start()
    for c in copies:
        c.wait()


def as_row(col):
    n = col.shape[0]
    down = lax.broadcasted_iota(jnp.int32, (n, n), 0)
    across = lax.broadcasted_iota(jnp.int32, (n, n), 1)
    return jnp.sum(jnp.where(down == across, col, 0.0), axis=0, keepdims=True)


def in_pieces(x):
    pieces = []
    for _ in range(3):
        piece = x.astype(BF).astype(F32)
        pieces.append(piece)
        x = x - piece
    return pieces


def document_codes(lens, row_pos, col_pos):
    n = lens.shape[1]
    down = lax.broadcasted_iota(jnp.int32, (n, n), 0)
    across = lax.broadcasted_iota(jnp.int32, (n, n), 1)
    wide = jnp.broadcast_to(lens, (n, n))
    ends_col = jnp.sum(jnp.where(across <= down, wide, 0.0), axis=1, keepdims=True)
    lens_col = jnp.sum(jnp.where(across == down, wide, 0.0), axis=1, keepdims=True)
    ends_row = jnp.sum(jnp.where(down <= across, lens_col, 0.0), axis=0, keepdims=True)
    row_doc = jnp.sum(jnp.where(row_pos >= ends_col, 1.0, 0.0), axis=0, keepdims=True)
    col_doc = jnp.sum(jnp.where(col_pos >= ends_row, 1.0, 0.0), axis=1, keepdims=True)
    return row_doc, col_doc


def take_window(core, own_ref, far_ref, rows, window_ref):
    six = [x.at[i] for x in (far_ref.at[0], own_ref, far_ref.at[1]) for i in range(2)]
    for value in range(2):

        @pl.when(core == value)
        def _(value=value):
            for i in range(5):
                window_ref[i * rows : (i + 1) * rows, :] = six[i + value][:rows, :]


def forward_kernel(
    heads, total, where_ref, dil_ref, lens_ref, own_ref, far_ref, w_hbm,
    part_ref, probs_out, attn_ref, win_out, back_out, logs_ref,
    hold_ref, win_ref, back_ref, probs_ref, w_ref, sems,
):
    groups, span = part_ref.shape[0], part_ref.shape[2]
    blocks = [slice(b * span, (b + 1) * span) for b in range(groups)]
    fetches = [
        pltpu.make_async_copy(w_hbm.at[:, x], w_ref.at[:, x], sems.at[groups + b])
        for b, x in enumerate(blocks)
    ]
    for c in fetches:
        c.start()
    rows = own_ref.shape[1]
    width = own_ref.shape[2] // 3
    hd = width // heads
    keys = win_ref.shape[0]
    slab = where_ref[0]
    take_window(lax.rem(slab, 2), own_ref, far_ref, rows, win_ref)
    copies = [pltpu.make_async_copy(win_ref, win_out, sems.at[2 * groups])]
    copies[0].start()
    mine = slice(2 * rows, 3 * rows)
    first = slab * rows
    row_idx = lax.broadcasted_iota(jnp.int32, (1, keys), 1) + (first - 2 * rows)
    col_idx = lax.broadcasted_iota(jnp.int32, (rows, 1), 0) + first
    row_pos, col_pos = row_idx.astype(F32), col_idx.astype(F32)
    row_doc, col_doc = document_codes(lens_ref[...].astype(F32), row_pos, col_pos)
    inside = (row_pos >= 0.0) & (row_pos < float(total))
    distance = jnp.abs(col_pos - row_pos)
    for h in range(heads):
        stride = dil_ref[h].astype(F32)

        def residue(pos, doc):
            steps = jnp.floor((pos + 0.5) / jnp.full(pos.shape, stride))
            return doc * 8.0 + (pos - steps * stride)

        row_code = jnp.where(inside, residue(row_pos, row_doc), -1.0)
        col_code = residue(col_pos, col_doc)
        mask = (row_code == col_code) & (distance <= stride * float(HALF))
        cols = slice(h * hd, (h + 1) * hd)
        vcols = slice(width + h * hd, width + (h + 1) * hd)
        qcols = slice(2 * width + h * hd, 2 * width + (h + 1) * hd)
        s = dot(win_ref[mine, qcols], win_ref[:, cols], ((1,), (1,))) * (hd**-0.5)
        s = jnp.where(mask, s, -jnp.inf)
        top = jnp.max(s, axis=1, keepdims=True)
        e = jnp.exp(s - top)
        norm = jnp.sum(e, axis=1, keepdims=True)
        probs = (e * (1.0 / norm)).astype(BF)
        probs_ref[h] = probs
        logs_ref[h] = as_row(top + jnp.log(norm))
        attn_ref[:, cols] = dot(probs, win_ref[:, vcols], ((1,), (0,))).astype(BF)
        back = dot(win_ref[mine, cols], win_ref[:, qcols], ((1,), (1,))) * (hd**-0.5)
        back_ref[h] = jnp.where(mask, back, -jnp.inf)
    copies.append(pltpu.make_async_copy(back_ref, back_out, sems.at[2 * groups + 1]))
    copies.append(pltpu.make_async_copy(probs_ref, probs_out, sems.at[2 * groups + 2]))
    copies[1].start()
    copies[2].start()
    attn = attn_ref[...]
    for b in range(groups):
        fetches[b].wait()
        hold_ref[b] = dot(attn, w_ref[:, blocks[b]], ((1,), (0,))).astype(BF)
        copies.append(pltpu.make_async_copy(hold_ref.at[b], part_ref.at[b], sems.at[b]))
        copies[-1].start()
    for c in copies:
        c.wait()


def cotangent_kernel(heads, mg_ref, w_ref, attn_ref, logs_ref, out_ref, delta_ref):
    span = mg_ref.shape[2]
    rows, width = attn_ref.shape
    hd = width // heads
    total = jnp.zeros((rows, width), F32)
    for b in range(mg_ref.shape[0]):
        total = total + dot(mg_ref[b], w_ref[:, b * span : (b + 1) * span], ((1,), (1,)))
    grad = total.astype(BF)
    out_ref[:rows, :] = grad
    product = grad.astype(F32) * attn_ref[...].astype(F32)
    extra = out_ref.shape[0] - rows
    place = lax.broadcasted_iota(jnp.int32, (extra, hd), 0)
    for h in range(heads):
        cols = slice(h * hd, (h + 1) * hd)
        delta = jnp.sum(product[:, cols], axis=1, keepdims=True)
        delta_ref[h] = delta
        stats = jnp.zeros((extra, hd), F32)
        for i, piece in enumerate(in_pieces(logs_ref[h]) + in_pieces(as_row(delta))):
            stats = jnp.where(place == i, piece, stats)
        out_ref[rows:, cols] = stats.astype(BF)


def query_kernel(heads, win_ref, probs_ref, ga_ref, delta_ref, dq_ref):
    rows, width = dq_ref.shape
    hd = width // heads
    for h in range(heads):
        cols = slice(h * hd, (h + 1) * hd)
        vcols = slice(width + h * hd, width + (h + 1) * hd)
        grad_prob = dot(ga_ref[:rows, cols], win_ref[:, vcols], ((1,), (1,)))
        slopes = (probs_ref[h].astype(F32) * (grad_prob - delta_ref[h])).astype(BF)
        dq_ref[:, cols] = (dot(slopes, win_ref[:, cols], ((1,), (0,))) * (hd**-0.5)).astype(BF)


def key_kernel(heads, where_ref, win_ref, back_ref, own_ref, far_ref, dk_ref, dv_ref, ga_ref):
    rows, width = dk_ref.shape
    hd = width // heads
    mine = slice(2 * rows, 3 * rows)
    core = lax.rem(where_ref[0], 2)
    take_window(core, own_ref, far_ref, rows, ga_ref)
    tails = [x[i, rows:, :].astype(F32) for x in (far_ref.at[0], own_ref, far_ref.at[1]) for i in range(2)]
    tails = [jnp.where(core == 0, tails[i], tails[i + 1]) for i in range(5)]
    stats = jnp.concatenate([jnp.stack([t[:, h * hd : (h + 1) * hd] for h in range(heads)]) for t in tails], axis=2)
    for h in range(heads):
        cols = slice(h * hd, (h + 1) * hd)
        vcols = slice(width + h * hd, width + (h + 1) * hd)
        qcols = slice(2 * width + h * hd, 2 * width + (h + 1) * hd)
        log_total = stats[h, 0:1] + stats[h, 1:2] + stats[h, 2:3]
        delta = stats[h, 3:4] + stats[h, 4:5] + stats[h, 5:6]
        weight = jnp.exp(back_ref[h] - log_total)
        grad_prob = dot(win_ref[mine, vcols], ga_ref[:, cols], ((1,), (1,)))
        slopes = (weight * (grad_prob - delta)).astype(BF)
        dk_ref[:, cols] = (dot(slopes, win_ref[:, qcols], ((1,), (0,))) * (hd**-0.5)).astype(BF)
        dv_ref[:, cols] = dot(weight.astype(BF), ga_ref[:, cols], ((1,), (0,))).astype(BF)


def mixed_kernel(x_ref, o_ref):
    total = x_ref[0].astype(F32)
    for c in range(1, x_ref.shape[0]):
        total = total + x_ref[c].astype(F32)
    o_ref[...] = total.astype(BF)


def to_neighbours(x):
    count = lax.axis_size("ctx")
    ahead = [(i, i + 2) for i in range(0, count - 2, 2)]
    back = [(i, i - 2) for i in range(3, count, 2)]
    return lax.ppermute(x, "ctx", ahead + back)


def in_chip(x):
    pairs = [[i, i + 1] for i in range(0, lax.axis_size("ctx"), 2)]
    return lax.all_gather(x, "ctx", axis=0, axis_index_groups=pairs)


def per_device(queries, keys, values, out_weight, mixed_grad, lengths, dilation):
    rows, width = queries.shape
    heads = dilation.shape[0]
    groups = lax.axis_size("head")
    span = mixed_grad.shape[1]
    total = rows * lax.axis_size("ctx")
    where = lax.axis_index("ctx").astype(jnp.int32).reshape(1)
    lens = lengths.reshape(1, -1)

    kvq, mgv = call(
        pack_kernel,
        [shape((rows, 3 * width), BF), shape((rows, span), BF)],
        [keys, values, queries, mixed_grad],
        "pack",
        scratch=[pltpu.SemaphoreType.DMA((4,))],
        hbm_in=(0, 1, 2, 3),
    )
    own2 = in_chip(kvq)
    near = to_neighbours(own2)
    (spread,) = call(
        spread_kernel,
        [shape((groups, rows, span), BF)],
        [mgv, own2],
        "spread",
        scratch=[pltpu.SemaphoreType.DMA((groups,))],
        hbm_out=(0,),
    )
    gathered = lax.all_to_all(spread, "head", 0, 0, tiled=True)
    far = in_chip(near)
    part, probs, attn, window, back, logs = call(
        functools.partial(forward_kernel, heads, total),
        [
            shape((groups, rows, span), BF),
            shape((heads, rows, 5 * rows), BF),
            shape((rows, width), BF),
            shape((5 * rows, 3 * width), BF),
            shape((heads, rows, 5 * rows), F32),
            shape((heads, 1, rows), F32),
        ],
        [where, dilation, lens, own2, far, out_weight],
        "forward",
        flops=80 * 2 * rows * width * (groups * span + 15 * rows),
        scratch=[
            pltpu.VMEM((groups, rows, span), BF),
            pltpu.VMEM((5 * rows, 3 * width), BF),
            pltpu.VMEM((heads, rows, 5 * rows), F32),
            pltpu.VMEM((heads, rows, 5 * rows), BF),
            pltpu.VMEM(out_weight.shape, BF),
            pltpu.SemaphoreType.DMA((2 * groups + 3,)),
        ],
        hbm_in=(5,),
        hbm_out=(0, 1, 3, 4),
    )
    ga, delta = call(
        functools.partial(cotangent_kernel, heads),
        [shape((rows + 16, width), BF), shape((heads, rows, 1), F32)],
        [gathered, out_weight, attn, logs],
        "cotangent",
        flops=2 * rows * width * groups * span,
    )
    ga, part = lax.optimization_barrier((ga, part))
    summed = lax.all_to_all(part, "head", 0, 0, tiled=True)
    ga2 = in_chip(ga)
    ga_near = to_neighbours(ga2)
    (dq,) = call(
        functools.partial(query_kernel, heads),
        [shape((rows, width), BF)],
        [window, probs, ga, delta],
        "query",
        flops=2 * rows * width * 10 * rows,
    )
    (mixed,) = call(mixed_kernel, [shape((rows, span), BF)], [summed], "mixed")
    dk, dv = call(
        functools.partial(key_kernel, heads),
        [shape((rows, width), BF), shape((rows, width), BF)],
        [where, window, back, ga2, in_chip(ga_near)],
        "key",
        flops=2 * rows * width * 15 * rows,
        scratch=[pltpu.VMEM((5 * rows, width), BF)],
    )
    return mixed, dq, dk, dv


def solution(mesh):
    placed = (
        P("ctx", "head"),
        P("ctx", "head"),
        P("ctx", "head"),
        P("head", None),
        P("ctx", "head"),
        P(),
        P("head"),
    )
    return jax.shard_map(
        per_device,
        mesh=mesh,
        in_specs=placed,
        out_specs=(P("ctx", "head"), P("ctx", "head"), P("ctx", "head"), P("ctx", "head")),
        check_vma=False,
    )
```

```python
import functools

import jax
import jax.numpy as jnp
from jax import lax
from jax.experimental import pallas as pl
from jax.experimental.pallas import tpu as pltpu
from jax.sharding import PartitionSpec as P

HALF = 32
BF = jnp.bfloat16
F32 = jnp.float32
VMEM = pl.BlockSpec(memory_space=pltpu.VMEM)
SMEM = pl.BlockSpec(memory_space=pltpu.SMEM)
HBM = pl.BlockSpec(memory_space=pltpu.HBM)


def dot(a, b, dims):
    return lax.dot_general(a, b, (dims, ((), ())), preferred_element_type=F32)


def call(body, outs, ins, name, flops=0, scratch=(), hbm_in=(), hbm_out=()):
    moved = sum(x.size * x.dtype.itemsize for x in (*ins, *outs))
    held = [
        pltpu.with_memory_space_constraint(x, pltpu.HBM) if i in hbm_in else x
        for i, x in enumerate(ins)
    ]
    return pl.pallas_call(
        body,
        out_shape=[pltpu.HBM(x.shape, x.dtype) if i in hbm_out else x for i, x in enumerate(outs)],
        in_specs=[SMEM if x.ndim == 1 else HBM if i in hbm_in else VMEM for i, x in enumerate(ins)],
        out_specs=[HBM if i in hbm_out else VMEM for i in range(len(outs))],
        scratch_shapes=scratch,
        compiler_params=pltpu.CompilerParams(vmem_limit_bytes=24 << 20),
        cost_estimate=pl.CostEstimate(flops=flops, bytes_accessed=moved, transcendentals=0),
        name=name,
    )(*held)


def shape(dims, dtype):
    return jax.ShapeDtypeStruct(dims, dtype)


def pack_kernel(k_ref, v_ref, q_ref, mg_ref, kvq_ref, mgv_ref, sems):
    w = k_ref.shape[1]
    copies = [pltpu.make_async_copy(mg_ref, mgv_ref, sems.at[3])]
    for i, x_ref in enumerate((k_ref, v_ref, q_ref)):
        part = kvq_ref.at[:, i * w : (i + 1) * w]
        copies.append(pltpu.make_async_copy(x_ref, part, sems.at[i]))
    for c in copies:
        c.start()
    for c in copies:
        c.wait()


def spread_kernel(mg_ref, after_ref, all_ref, sems):
    copies = [
        pltpu.make_async_copy(mg_ref, all_ref.at[b], sems.at[b]) for b in range(all_ref.shape[0])
    ]
    for c in copies:
        c.start()
    for c in copies:
        c.wait()


def as_row(col):
    n = col.shape[0]
    down = lax.broadcasted_iota(jnp.int32, (n, n), 0)
    across = lax.broadcasted_iota(jnp.int32, (n, n), 1)
    return jnp.sum(jnp.where(down == across, col, 0.0), axis=0, keepdims=True)


def in_pieces(x):
    pieces = []
    for _ in range(3):
        piece = x.astype(BF).astype(F32)
        pieces.append(piece)
        x = x - piece
    return pieces


def document_codes(lens, row_pos, col_pos):
    n = lens.shape[1]
    down = lax.broadcasted_iota(jnp.int32, (n, n), 0)
    across = lax.broadcasted_iota(jnp.int32, (n, n), 1)
    wide = jnp.broadcast_to(lens, (n, n))
    ends_col = jnp.sum(jnp.where(across <= down, wide, 0.0), axis=1, keepdims=True)
    lens_col = jnp.sum(jnp.where(across == down, wide, 0.0), axis=1, keepdims=True)
    ends_row = jnp.sum(jnp.where(down <= across, lens_col, 0.0), axis=0, keepdims=True)
    row_doc = jnp.sum(jnp.where(row_pos >= ends_col, 1.0, 0.0), axis=0, keepdims=True)
    col_doc = jnp.sum(jnp.where(col_pos >= ends_row, 1.0, 0.0), axis=1, keepdims=True)
    return row_doc, col_doc


def take_window(core, own_ref, far_ref, rows, window_ref):
    six = [x.at[i] for x in (far_ref.at[0], own_ref, far_ref.at[1]) for i in range(2)]
    for value in range(2):

        @pl.when(core == value)
        def _(value=value):
            for i in range(5):
                window_ref[i * rows : (i + 1) * rows, :] = six[i + value][:rows, :]


def forward_kernel(
    heads, total, where_ref, dil_ref, lens_ref, own_ref, far_ref, w_ref,
    part_ref, probs_out, attn_out, win_out, back_out, logs_ref,
    hold_ref, win_ref, back_ref, probs_ref, attn_ref, sems,
):
    groups, span = part_ref.shape[0], part_ref.shape[2]
    blocks = [slice(b * span, (b + 1) * span) for b in range(groups)]
    rows = own_ref.shape[1]
    width = own_ref.shape[2] // 3
    hd = width // heads
    keys = win_ref.shape[0]
    slab = where_ref[0]
    take_window(lax.rem(slab, 2), own_ref, far_ref, rows, win_ref)
    copies = [pltpu.make_async_copy(win_ref, win_out, sems.at[groups])]
    copies[0].start()
    mine = slice(2 * rows, 3 * rows)
    first = slab * rows
    row_idx = lax.broadcasted_iota(jnp.int32, (1, keys), 1) + (first - 2 * rows)
    col_idx = lax.broadcasted_iota(jnp.int32, (rows, 1), 0) + first
    row_pos, col_pos = row_idx.astype(F32), col_idx.astype(F32)
    row_doc, col_doc = document_codes(lens_ref[...].astype(F32), row_pos, col_pos)
    inside = (row_pos >= 0.0) & (row_pos < float(total))
    distance = jnp.abs(col_pos - row_pos)
    for h in range(heads):
        stride = dil_ref[h].astype(F32)

        def residue(pos, doc):
            steps = jnp.floor((pos + 0.5) / jnp.full(pos.shape, stride))
            return doc * 8.0 + (pos - steps * stride)

        row_code = jnp.where(inside, residue(row_pos, row_doc), -1.0)
        col_code = residue(col_pos, col_doc)
        mask = (row_code == col_code) & (distance <= stride * float(HALF))
        cols = slice(h * hd, (h + 1) * hd)
        vcols = slice(width + h * hd, width + (h + 1) * hd)
        qcols = slice(2 * width + h * hd, 2 * width + (h + 1) * hd)
        s = dot(win_ref[mine, qcols], win_ref[:, cols], ((1,), (1,))) * (hd**-0.5)
        s = jnp.where(mask, s, -jnp.inf)
        top = jnp.max(s, axis=1, keepdims=True)
        e = jnp.exp(s - top)
        norm = jnp.sum(e, axis=1, keepdims=True)
        probs = (e * (1.0 / norm)).astype(BF)
        probs_ref[h] = probs
        logs_ref[h] = as_row(top + jnp.log(norm))
        attn_ref[:, cols] = dot(probs, win_ref[:, vcols], ((1,), (0,))).astype(BF)
        back = dot(win_ref[mine, cols], win_ref[:, qcols], ((1,), (1,))) * (hd**-0.5)
        back_ref[h] = jnp.where(mask, back, -jnp.inf)
    copies.append(pltpu.make_async_copy(back_ref, back_out, sems.at[groups + 1]))
    copies.append(pltpu.make_async_copy(probs_ref, probs_out, sems.at[groups + 2]))
    copies.append(pltpu.make_async_copy(attn_ref, attn_out, sems.at[groups + 3]))
    for c in copies[1:]:
        c.start()
    attn = attn_ref[...]
    for b in range(groups):
        hold_ref[b] = dot(attn, w_ref[:, blocks[b]], ((1,), (0,))).astype(BF)
        copies.append(pltpu.make_async_copy(hold_ref.at[b], part_ref.at[b], sems.at[b]))
        copies[-1].start()
    for c in copies:
        c.wait()


def cotangent_kernel(heads, mg_ref, w_ref, attn_hbm, logs_ref, out_ref, delta_ref, attn_ref, sem):
    span = mg_ref.shape[2]
    fetch = pltpu.make_async_copy(attn_hbm, attn_ref, sem)
    fetch.start()
    rows, width = attn_ref.shape
    hd = width // heads
    total = jnp.zeros((rows, width), F32)
    for b in range(mg_ref.shape[0]):
        total = total + dot(mg_ref[b], w_ref[:, b * span : (b + 1) * span], ((1,), (1,)))
    grad = total.astype(BF)
    out_ref[:rows, :] = grad
    fetch.wait()
    product = grad.astype(F32) * attn_ref[...].astype(F32)
    extra = out_ref.shape[0] - rows
    place = lax.broadcasted_iota(jnp.int32, (extra, hd), 0)
    for h in range(heads):
        cols = slice(h * hd, (h + 1) * hd)
        delta = jnp.sum(product[:, cols], axis=1, keepdims=True)
        delta_ref[h] = delta
        stats = jnp.zeros((extra, hd), F32)
        for i, piece in enumerate(in_pieces(logs_ref[h]) + in_pieces(as_row(delta))):
            stats = jnp.where(place == i, piece, stats)
        out_ref[rows:, cols] = stats.astype(BF)


def query_kernel(heads, win_hbm, probs_hbm, ga_ref, delta_ref, dq_ref, win_ref, probs_ref, sems):
    rows, width = dq_ref.shape
    copies = [
        pltpu.make_async_copy(win_hbm.at[:, : 2 * width], win_ref, sems.at[0]),
        pltpu.make_async_copy(probs_hbm, probs_ref, sems.at[1]),
    ]
    for c in copies:
        c.start()
    for c in copies:
        c.wait()
    hd = width // heads
    for h in range(heads):
        cols = slice(h * hd, (h + 1) * hd)
        vcols = slice(width + h * hd, width + (h + 1) * hd)
        grad_prob = dot(ga_ref[:rows, cols], win_ref[:, vcols], ((1,), (1,)))
        slopes = (probs_ref[h].astype(F32) * (grad_prob - delta_ref[h])).astype(BF)
        dq_ref[:, cols] = (dot(slopes, win_ref[:, cols], ((1,), (0,))) * (hd**-0.5)).astype(BF)


def key_kernel(heads, where_ref, win_ref, back_ref, own_ref, far_ref, dk_ref, dv_ref, ga_ref):
    rows, width = dk_ref.shape
    hd = width // heads
    mine = slice(2 * rows, 3 * rows)
    core = lax.rem(where_ref[0], 2)
    take_window(core, own_ref, far_ref, rows, ga_ref)
    tails = [x[i, rows:, :].astype(F32) for x in (far_ref.at[0], own_ref, far_ref.at[1]) for i in range(2)]
    tails = [jnp.where(core == 0, tails[i], tails[i + 1]) for i in range(5)]
    stats = jnp.concatenate([jnp.stack([t[:, h * hd : (h + 1) * hd] for h in range(heads)]) for t in tails], axis=2)
    for h in range(heads):
        cols = slice(h * hd, (h + 1) * hd)
        vcols = slice(width + h * hd, width + (h + 1) * hd)
        qcols = slice(2 * width + h * hd, 2 * width + (h + 1) * hd)
        log_total = stats[h, 0:1] + stats[h, 1:2] + stats[h, 2:3]
        delta = stats[h, 3:4] + stats[h, 4:5] + stats[h, 5:6]
        weight = jnp.exp(back_ref[h] - log_total)
        grad_prob = dot(win_ref[mine, vcols], ga_ref[:, cols], ((1,), (1,)))
        slopes = (weight * (grad_prob - delta)).astype(BF)
        dk_ref[:, cols] = (dot(slopes, win_ref[:, qcols], ((1,), (0,))) * (hd**-0.5)).astype(BF)
        dv_ref[:, cols] = dot(weight.astype(BF), ga_ref[:, cols], ((1,), (0,))).astype(BF)


def mixed_kernel(x_ref, o_ref):
    total = x_ref[0].astype(F32)
    for c in range(1, x_ref.shape[0]):
        total = total + x_ref[c].astype(F32)
    o_ref[...] = total.astype(BF)


def to_neighbours(x):
    count = lax.axis_size("ctx")
    ahead = [(i, i + 2) for i in range(0, count - 2, 2)]
    back = [(i, i - 2) for i in range(3, count, 2)]
    return lax.ppermute(x, "ctx", ahead + back)


def in_chip(x):
    pairs = [[i, i + 1] for i in range(0, lax.axis_size("ctx"), 2)]
    return lax.all_gather(x, "ctx", axis=0, axis_index_groups=pairs)


def per_device(queries, keys, values, out_weight, mixed_grad, lengths, dilation):
    rows, width = queries.shape
    heads = dilation.shape[0]
    groups = lax.axis_size("head")
    span = mixed_grad.shape[1]
    total = rows * lax.axis_size("ctx")
    where = lax.axis_index("ctx").astype(jnp.int32).reshape(1)
    lens = lengths.reshape(1, -1)

    kvq, mgv = call(
        pack_kernel,
        [shape((rows, 3 * width), BF), shape((rows, span), BF)],
        [keys, values, queries, mixed_grad],
        "pack",
        scratch=[pltpu.SemaphoreType.DMA((4,))],
        hbm_in=(0, 1, 2, 3),
    )
    own2 = in_chip(kvq)
    near = to_neighbours(own2)
    (spread,) = call(
        spread_kernel,
        [shape((groups, rows, span), BF)],
        [mgv, own2],
        "spread",
        scratch=[pltpu.SemaphoreType.DMA((groups,))],
        hbm_out=(0,),
    )
    gathered = lax.all_to_all(spread, "head", 0, 0, tiled=True)
    far = in_chip(near)
    part, probs, attn, window, back, logs = call(
        functools.partial(forward_kernel, heads, total),
        [
            shape((groups, rows, span), BF),
            shape((heads, rows, 5 * rows), BF),
            shape((rows, width), BF),
            shape((5 * rows, 3 * width), BF),
            shape((heads, rows, 5 * rows), F32),
            shape((heads, 1, rows), F32),
        ],
        [where, dilation, lens, own2, far, out_weight],
        "forward",
        flops=80 * 2 * rows * width * (groups * span + 15 * rows),
        scratch=[
            pltpu.VMEM((groups, rows, span), BF),
            pltpu.VMEM((5 * rows, 3 * width), BF),
            pltpu.VMEM((heads, rows, 5 * rows), F32),
            pltpu.VMEM((heads, rows, 5 * rows), BF),
            pltpu.VMEM((rows, width), BF),
            pltpu.SemaphoreType.DMA((groups + 4,)),
        ],
        hbm_out=(0, 1, 2, 3, 4),
    )
    ga, delta = call(
        functools.partial(cotangent_kernel, heads),
        [shape((rows + 16, width), BF), shape((heads, rows, 1), F32)],
        [gathered, out_weight, attn, logs],
        "cotangent",
        flops=2 * rows * width * groups * span,
        scratch=[pltpu.VMEM((rows, width), BF), pltpu.SemaphoreType.DMA],
        hbm_in=(2,),
    )
    ga2, ga, part = lax.optimization_barrier((in_chip(ga), ga, part))
    ga_near = to_neighbours(ga2)
    (dq,) = call(
        functools.partial(query_kernel, heads),
        [shape((rows, width), BF)],
        [window, probs, ga, delta],
        "query",
        flops=2 * rows * width * 10 * rows,
        scratch=[
            pltpu.VMEM((5 * rows, 2 * width), BF),
            pltpu.VMEM((heads, rows, 5 * rows), BF),
            pltpu.SemaphoreType.DMA((2,)),
        ],
        hbm_in=(0, 1),
    )
    summed = lax.all_to_all(part, "head", 0, 0, tiled=True)
    (mixed,) = call(mixed_kernel, [shape((rows, span), BF)], [summed], "mixed")
    dk, dv = call(
        functools.partial(key_kernel, heads),
        [shape((rows, width), BF), shape((rows, width), BF)],
        [where, window, back, ga2, in_chip(ga_near)],
        "key",
        flops=30 * 10**9,
        scratch=[pltpu.VMEM((5 * rows, width), BF)],
    )
    return mixed, dq, dk, dv


def solution(mesh):
    placed = (
        P("ctx", "head"),
        P("ctx", "head"),
        P("ctx", "head"),
        P("head", None),
        P("ctx", "head"),
        P(),
        P("head"),
    )
    return jax.shard_map(
        per_device,
        mesh=mesh,
        in_specs=placed,
        out_specs=(P("ctx", "head"), P("ctx", "head"), P("ctx", "head"), P("ctx", "head")),
        check_vma=False,
    )
```

```python
import functools

import jax
import jax.numpy as jnp
from jax import lax
from jax.experimental import pallas as pl
from jax.experimental.pallas import tpu as pltpu
from jax.sharding import PartitionSpec as P

HALF = 32
BF = jnp.bfloat16
F32 = jnp.float32
VMEM = pl.BlockSpec(memory_space=pltpu.VMEM)
SMEM = pl.BlockSpec(memory_space=pltpu.SMEM)
HBM = pl.BlockSpec(memory_space=pltpu.HBM)


def dot(a, b, dims):
    return lax.dot_general(a, b, (dims, ((), ())), preferred_element_type=F32)


def call(body, outs, ins, name, flops=0, scratch=(), hbm_in=(), hbm_out=()):
    moved = sum(x.size * x.dtype.itemsize for x in (*ins, *outs))
    held = [
        pltpu.with_memory_space_constraint(x, pltpu.HBM) if i in hbm_in else x
        for i, x in enumerate(ins)
    ]
    return pl.pallas_call(
        body,
        out_shape=[pltpu.HBM(x.shape, x.dtype) if i in hbm_out else x for i, x in enumerate(outs)],
        in_specs=[SMEM if x.ndim == 1 else HBM if i in hbm_in else VMEM for i, x in enumerate(ins)],
        out_specs=[HBM if i in hbm_out else VMEM for i in range(len(outs))],
        scratch_shapes=scratch,
        compiler_params=pltpu.CompilerParams(vmem_limit_bytes=24 << 20),
        cost_estimate=pl.CostEstimate(flops=flops, bytes_accessed=moved, transcendentals=0),
        name=name,
    )(*held)


def shape(dims, dtype):
    return jax.ShapeDtypeStruct(dims, dtype)


def pack_kernel(k_ref, v_ref, q_ref, mg_ref, kvq_ref, mgv_ref, sems):
    w = k_ref.shape[1]
    copies = [pltpu.make_async_copy(mg_ref, mgv_ref, sems.at[3])]
    for i, x_ref in enumerate((k_ref, v_ref, q_ref)):
        part = kvq_ref.at[:, i * w : (i + 1) * w]
        copies.append(pltpu.make_async_copy(x_ref, part, sems.at[i]))
    for c in copies:
        c.start()
    for c in copies:
        c.wait()


def spread_kernel(mg_ref, after_ref, all_ref, sems):
    copies = [
        pltpu.make_async_copy(mg_ref, all_ref.at[b], sems.at[b]) for b in range(all_ref.shape[0])
    ]
    for c in copies:
        c.start()
    for c in copies:
        c.wait()


def as_row(col):
    n = col.shape[0]
    down = lax.broadcasted_iota(jnp.int32, (n, n), 0)
    across = lax.broadcasted_iota(jnp.int32, (n, n), 1)
    return jnp.sum(jnp.where(down == across, col, 0.0), axis=0, keepdims=True)


def in_pieces(x):
    pieces = []
    for _ in range(3):
        piece = x.astype(BF).astype(F32)
        pieces.append(piece)
        x = x - piece
    return pieces


def document_codes(lens, row_pos, col_pos):
    n = lens.shape[1]
    down = lax.broadcasted_iota(jnp.int32, (n, n), 0)
    across = lax.broadcasted_iota(jnp.int32, (n, n), 1)
    wide = jnp.broadcast_to(lens, (n, n))
    ends_col = jnp.sum(jnp.where(across <= down, wide, 0.0), axis=1, keepdims=True)
    lens_col = jnp.sum(jnp.where(across == down, wide, 0.0), axis=1, keepdims=True)
    ends_row = jnp.sum(jnp.where(down <= across, lens_col, 0.0), axis=0, keepdims=True)
    row_doc = jnp.sum(jnp.where(row_pos >= ends_col, 1.0, 0.0), axis=0, keepdims=True)
    col_doc = jnp.sum(jnp.where(col_pos >= ends_row, 1.0, 0.0), axis=1, keepdims=True)
    return row_doc, col_doc


def take_window(core, own_ref, far_ref, rows, window_ref):
    six = [x.at[i] for x in (far_ref.at[0], own_ref, far_ref.at[1]) for i in range(2)]
    for value in range(2):

        @pl.when(core == value)
        def _(value=value):
            for i in range(5):
                window_ref[i * rows : (i + 1) * rows, :] = six[i + value][:rows, :]


def forward_kernel(
    heads, total, where_ref, row_ref, dil_ref, lens_ref, own_ref, far_ref, w_ref,
    keep_out, give_out, probs_out, attn_out, win_out, back_out, logs_ref,
    hold_ref, win_ref, back_ref, probs_ref, attn_ref, sems,
):
    cols, span = keep_out.shape[0], keep_out.shape[2]
    rows = own_ref.shape[1]
    width = own_ref.shape[2] // 3
    hd = width // heads
    keys = win_ref.shape[0]
    slab = where_ref[0]
    take_window(lax.rem(slab, 2), own_ref, far_ref, rows, win_ref)
    copies = [pltpu.make_async_copy(win_ref, win_out, sems.at[2 * cols])]
    copies[0].start()
    mine = slice(2 * rows, 3 * rows)
    first = slab * rows
    row_idx = lax.broadcasted_iota(jnp.int32, (1, keys), 1) + (first - 2 * rows)
    col_idx = lax.broadcasted_iota(jnp.int32, (rows, 1), 0) + first
    row_pos, col_pos = row_idx.astype(F32), col_idx.astype(F32)
    row_doc, col_doc = document_codes(lens_ref[...].astype(F32), row_pos, col_pos)
    inside = (row_pos >= 0.0) & (row_pos < float(total))
    distance = jnp.abs(col_pos - row_pos)
    for h in range(heads):
        stride = dil_ref[h].astype(F32)

        def residue(pos, doc):
            steps = jnp.floor((pos + 0.5) / jnp.full(pos.shape, stride))
            return doc * 8.0 + (pos - steps * stride)

        row_code = jnp.where(inside, residue(row_pos, row_doc), -1.0)
        col_code = residue(col_pos, col_doc)
        mask = (row_code == col_code) & (distance <= stride * float(HALF))
        hcols = slice(h * hd, (h + 1) * hd)
        vcols = slice(width + h * hd, width + (h + 1) * hd)
        qcols = slice(2 * width + h * hd, 2 * width + (h + 1) * hd)
        s = dot(win_ref[mine, qcols], win_ref[:, hcols], ((1,), (1,))) * (hd**-0.5)
        s = jnp.where(mask, s, -jnp.inf)
        top = jnp.max(s, axis=1, keepdims=True)
        e = jnp.exp(s - top)
        norm = jnp.sum(e, axis=1, keepdims=True)
        probs = (e * (1.0 / norm)).astype(BF)
        probs_ref[h] = probs
        logs_ref[h] = as_row(top + jnp.log(norm))
        attn_ref[:, hcols] = dot(probs, win_ref[:, vcols], ((1,), (0,))).astype(BF)
        back = dot(win_ref[mine, hcols], win_ref[:, qcols], ((1,), (1,))) * (hd**-0.5)
        back_ref[h] = jnp.where(mask, back, -jnp.inf)
    copies.append(pltpu.make_async_copy(back_ref, back_out, sems.at[2 * cols + 1]))
    copies.append(pltpu.make_async_copy(probs_ref, probs_out, sems.at[2 * cols + 2]))
    copies.append(pltpu.make_async_copy(attn_ref, attn_out, sems.at[2 * cols + 3]))
    for c in copies[1:]:
        c.start()
    attn = attn_ref[...]
    for half, (r, out) in enumerate(((1 - row_ref[0], give_out), (row_ref[0], keep_out))):
        for c in range(cols):
            i = half * cols + c
            block = pl.ds(pl.multiple_of((r * cols + c) * span, span), span)
            hold_ref[i] = dot(attn, w_ref[:, block], ((1,), (0,))).astype(BF)
            copies.append(pltpu.make_async_copy(hold_ref.at[i], out.at[c], sems.at[i]))
            copies[-1].start()
    for c in copies:
        c.wait()


def cotangent_kernel(heads, mg_ref, w_ref, attn_hbm, logs_ref, out_ref, delta_ref, attn_ref, sem):
    span = mg_ref.shape[2]
    fetch = pltpu.make_async_copy(attn_hbm, attn_ref, sem)
    fetch.start()
    rows, width = attn_ref.shape
    hd = width // heads
    total = jnp.zeros((rows, width), F32)
    for b in range(mg_ref.shape[0]):
        total = total + dot(mg_ref[b], w_ref[:, b * span : (b + 1) * span], ((1,), (1,)))
    grad = total.astype(BF)
    out_ref[:rows, :] = grad
    fetch.wait()
    product = grad.astype(F32) * attn_ref[...].astype(F32)
    extra = out_ref.shape[0] - rows
    place = lax.broadcasted_iota(jnp.int32, (extra, hd), 0)
    for h in range(heads):
        cols = slice(h * hd, (h + 1) * hd)
        delta = jnp.sum(product[:, cols], axis=1, keepdims=True)
        delta_ref[h] = delta
        stats = jnp.zeros((extra, hd), F32)
        for i, piece in enumerate(in_pieces(logs_ref[h]) + in_pieces(as_row(delta))):
            stats = jnp.where(place == i, piece, stats)
        out_ref[rows:, cols] = stats.astype(BF)


def query_kernel(heads, win_hbm, probs_hbm, ga_ref, delta_ref, dq_ref, win_ref, probs_ref, sems):
    rows, width = dq_ref.shape
    copies = [
        pltpu.make_async_copy(win_hbm.at[:, : 2 * width], win_ref, sems.at[0]),
        pltpu.make_async_copy(probs_hbm, probs_ref, sems.at[1]),
    ]
    for c in copies:
        c.start()
    for c in copies:
        c.wait()
    hd = width // heads
    for h in range(heads):
        cols = slice(h * hd, (h + 1) * hd)
        vcols = slice(width + h * hd, width + (h + 1) * hd)
        grad_prob = dot(ga_ref[:rows, cols], win_ref[:, vcols], ((1,), (1,)))
        slopes = (probs_ref[h].astype(F32) * (grad_prob - delta_ref[h])).astype(BF)
        dq_ref[:, cols] = (dot(slopes, win_ref[:, cols], ((1,), (0,))) * (hd**-0.5)).astype(BF)


def key_kernel(heads, where_ref, win_ref, back_ref, own_ref, far_ref, dk_ref, dv_ref, ga_ref):
    rows, width = dk_ref.shape
    hd = width // heads
    mine = slice(2 * rows, 3 * rows)
    core = lax.rem(where_ref[0], 2)
    take_window(core, own_ref, far_ref, rows, ga_ref)
    tails = [x[i, rows:, :].astype(F32) for x in (far_ref.at[0], own_ref, far_ref.at[1]) for i in range(2)]
    tails = [jnp.where(core == 0, tails[i], tails[i + 1]) for i in range(5)]
    stats = jnp.concatenate([jnp.stack([t[:, h * hd : (h + 1) * hd] for h in range(heads)]) for t in tails], axis=2)
    for h in range(heads):
        cols = slice(h * hd, (h + 1) * hd)
        vcols = slice(width + h * hd, width + (h + 1) * hd)
        qcols = slice(2 * width + h * hd, 2 * width + (h + 1) * hd)
        log_total = stats[h, 0:1] + stats[h, 1:2] + stats[h, 2:3]
        delta = stats[h, 3:4] + stats[h, 4:5] + stats[h, 5:6]
        weight = jnp.exp(back_ref[h] - log_total)
        grad_prob = dot(win_ref[mine, vcols], ga_ref[:, cols], ((1,), (1,)))
        slopes = (weight * (grad_prob - delta)).astype(BF)
        dk_ref[:, cols] = (dot(slopes, win_ref[:, qcols], ((1,), (0,))) * (hd**-0.5)).astype(BF)
        dv_ref[:, cols] = dot(weight.astype(BF), ga_ref[:, cols], ((1,), (0,))).astype(BF)


def rows_kernel(keep_ref, got_ref, out_ref, hold_ref, sems):
    copies = []
    for c in range(keep_ref.shape[0]):
        hold_ref[c] = (keep_ref[c].astype(F32) + got_ref[c].astype(F32)).astype(BF)
        copies.append(pltpu.make_async_copy(hold_ref.at[c], out_ref.at[c], sems.at[c]))
        copies[-1].start()
    for c in copies:
        c.wait()


def mixed_kernel(x_ref, o_ref):
    total = x_ref[0].astype(F32)
    for c in range(1, x_ref.shape[0]):
        total = total + x_ref[c].astype(F32)
    o_ref[...] = total.astype(BF)


def to_neighbours(x):
    count = lax.axis_size("ctx")
    ahead = [(i, i + 2) for i in range(0, count - 2, 2)]
    back = [(i, i - 2) for i in range(3, count, 2)]
    return lax.ppermute(x, "ctx", ahead + back)


def in_chip(x):
    pairs = [[i, i + 1] for i in range(0, lax.axis_size("ctx"), 2)]
    return lax.all_gather(x, "ctx", axis=0, axis_index_groups=pairs)


def per_device(queries, keys, values, out_weight, mixed_grad, lengths, dilation):
    rows, width = queries.shape
    heads = dilation.shape[0]
    groups = lax.axis_size("head")
    span = mixed_grad.shape[1]
    total = rows * lax.axis_size("ctx")
    cols = groups // 2
    along_row = [[r * cols + c for c in range(cols)] for r in range(2)]
    other_row = [(i, (i + cols) % groups) for i in range(groups)]
    where = lax.axis_index("ctx").astype(jnp.int32).reshape(1)
    row = (lax.axis_index("head").astype(jnp.int32) // cols).reshape(1)
    lens = lengths.reshape(1, -1)

    kvq, mgv = call(
        pack_kernel,
        [shape((rows, 3 * width), BF), shape((rows, span), BF)],
        [keys, values, queries, mixed_grad],
        "pack",
        scratch=[pltpu.SemaphoreType.DMA((4,))],
        hbm_in=(0, 1, 2, 3),
    )
    own2 = in_chip(kvq)
    near = to_neighbours(own2)
    (spread,) = call(
        spread_kernel,
        [shape((groups, rows, span), BF)],
        [mgv, own2],
        "spread",
        scratch=[pltpu.SemaphoreType.DMA((groups,))],
        hbm_out=(0,),
    )
    gathered = lax.all_to_all(spread, "head", 0, 0, tiled=True)
    far = in_chip(near)
    keep, give, probs, attn, window, back, logs = call(
        functools.partial(forward_kernel, heads, total),
        [
            shape((cols, rows, span), BF),
            shape((cols, rows, span), BF),
            shape((heads, rows, 5 * rows), BF),
            shape((rows, width), BF),
            shape((5 * rows, 3 * width), BF),
            shape((heads, rows, 5 * rows), F32),
            shape((heads, 1, rows), F32),
        ],
        [where, row, dilation, lens, own2, far, out_weight],
        "forward",
        flops=80 * 2 * rows * width * (groups * span + 15 * rows),
        scratch=[
            pltpu.VMEM((groups, rows, span), BF),
            pltpu.VMEM((5 * rows, 3 * width), BF),
            pltpu.VMEM((heads, rows, 5 * rows), F32),
            pltpu.VMEM((heads, rows, 5 * rows), BF),
            pltpu.VMEM((rows, width), BF),
            pltpu.SemaphoreType.DMA((groups + 4,)),
        ],
        hbm_out=(0, 1, 2, 3, 4, 5),
    )
    got_half = lax.ppermute(give, "head", other_row)
    ga, delta = call(
        functools.partial(cotangent_kernel, heads),
        [shape((rows + 16, width), BF), shape((heads, rows, 1), F32)],
        [gathered, out_weight, attn, logs],
        "cotangent",
        flops=2 * rows * width * groups * span,
        scratch=[pltpu.VMEM((rows, width), BF), pltpu.SemaphoreType.DMA],
        hbm_in=(2,),
    )
    ga2, ga, keep = lax.optimization_barrier((in_chip(ga), ga, keep))
    ga_near = to_neighbours(ga2)
    (dq,) = call(
        functools.partial(query_kernel, heads),
        [shape((rows, width), BF)],
        [window, probs, ga, delta],
        "query",
        flops=2 * rows * width * 10 * rows,
        scratch=[
            pltpu.VMEM((5 * rows, 2 * width), BF),
            pltpu.VMEM((heads, rows, 5 * rows), BF),
            pltpu.SemaphoreType.DMA((2,)),
        ],
        hbm_in=(0, 1),
    )
    (half,) = call(
        rows_kernel,
        [shape((cols, rows, span), BF)],
        [keep, got_half],
        "rows",
        scratch=[pltpu.VMEM((cols, rows, span), BF), pltpu.SemaphoreType.DMA((cols,))],
        hbm_out=(0,),
    )
    summed = lax.all_to_all(half, "head", 0, 0, tiled=True, axis_index_groups=along_row)
    (mixed,) = call(mixed_kernel, [shape((rows, span), BF)], [summed], "mixed")
    dk, dv = call(
        functools.partial(key_kernel, heads),
        [shape((rows, width), BF), shape((rows, width), BF)],
        [where, window, back, ga2, in_chip(ga_near)],
        "key",
        flops=30 * 10**9,
        scratch=[pltpu.VMEM((5 * rows, width), BF)],
    )
    return mixed, dq, dk, dv


def solution(mesh):
    placed = (
        P("ctx", "head"),
        P("ctx", "head"),
        P("ctx", "head"),
        P("head", None),
        P("ctx", "head"),
        P(),
        P("head"),
    )
    return jax.shard_map(
        per_device,
        mesh=mesh,
        in_specs=placed,
        out_specs=(P("ctx", "head"), P("ctx", "head"), P("ctx", "head"), P("ctx", "head")),
        check_vma=False,
    )
```

```python
import functools

import jax
import jax.numpy as jnp
from jax import lax
from jax.experimental import pallas as pl
from jax.experimental.pallas import tpu as pltpu
from jax.sharding import PartitionSpec as P

HALF = 32
BF = jnp.bfloat16
F32 = jnp.float32
VMEM = pl.BlockSpec(memory_space=pltpu.VMEM)
SMEM = pl.BlockSpec(memory_space=pltpu.SMEM)
HBM = pl.BlockSpec(memory_space=pltpu.HBM)


def dot(a, b, dims):
    return lax.dot_general(a, b, (dims, ((), ())), preferred_element_type=F32)


def call(body, outs, ins, name, flops=0, scratch=(), hbm_in=(), hbm_out=()):
    moved = sum(x.size * x.dtype.itemsize for x in (*ins, *outs))
    held = [
        pltpu.with_memory_space_constraint(x, pltpu.HBM) if i in hbm_in else x
        for i, x in enumerate(ins)
    ]
    return pl.pallas_call(
        body,
        out_shape=[pltpu.HBM(x.shape, x.dtype) if i in hbm_out else x for i, x in enumerate(outs)],
        in_specs=[SMEM if x.ndim == 1 else HBM if i in hbm_in else VMEM for i, x in enumerate(ins)],
        out_specs=[HBM if i in hbm_out else VMEM for i in range(len(outs))],
        scratch_shapes=scratch,
        compiler_params=pltpu.CompilerParams(vmem_limit_bytes=24 << 20),
        cost_estimate=pl.CostEstimate(flops=flops, bytes_accessed=moved, transcendentals=0),
        name=name,
    )(*held)


def shape(dims, dtype):
    return jax.ShapeDtypeStruct(dims, dtype)


def pack_kernel(k_ref, v_ref, q_ref, mg_ref, kvq_ref, mgv_ref, sems):
    w = k_ref.shape[1]
    copies = [pltpu.make_async_copy(mg_ref, mgv_ref, sems.at[3])]
    for i, x_ref in enumerate((k_ref, v_ref, q_ref)):
        part = kvq_ref.at[:, i * w : (i + 1) * w]
        copies.append(pltpu.make_async_copy(x_ref, part, sems.at[i]))
    for c in copies:
        c.start()
    for c in copies:
        c.wait()


def spread_kernel(mg_ref, after_ref, all_ref, sems):
    copies = [
        pltpu.make_async_copy(mg_ref, all_ref.at[b], sems.at[b]) for b in range(all_ref.shape[0])
    ]
    for c in copies:
        c.start()
    for c in copies:
        c.wait()


def as_row(col):
    n = col.shape[0]
    down = lax.broadcasted_iota(jnp.int32, (n, n), 0)
    across = lax.broadcasted_iota(jnp.int32, (n, n), 1)
    return jnp.sum(jnp.where(down == across, col, 0.0), axis=0, keepdims=True)


def in_pieces(x):
    pieces = []
    for _ in range(3):
        piece = x.astype(BF).astype(F32)
        pieces.append(piece)
        x = x - piece
    return pieces


def document_codes(lens, row_pos, col_pos):
    n = lens.shape[1]
    down = lax.broadcasted_iota(jnp.int32, (n, n), 0)
    across = lax.broadcasted_iota(jnp.int32, (n, n), 1)
    wide = jnp.broadcast_to(lens, (n, n))
    ends_col = jnp.sum(jnp.where(across <= down, wide, 0.0), axis=1, keepdims=True)
    lens_col = jnp.sum(jnp.where(across == down, wide, 0.0), axis=1, keepdims=True)
    ends_row = jnp.sum(jnp.where(down <= across, lens_col, 0.0), axis=0, keepdims=True)
    row_doc = jnp.sum(jnp.where(row_pos >= ends_col, 1.0, 0.0), axis=0, keepdims=True)
    col_doc = jnp.sum(jnp.where(col_pos >= ends_row, 1.0, 0.0), axis=1, keepdims=True)
    return row_doc, col_doc


def take_window(core, own_ref, far_ref, rows, window_ref):
    six = [x.at[i] for x in (far_ref.at[0], own_ref, far_ref.at[1]) for i in range(2)]
    for value in range(2):

        @pl.when(core == value)
        def _(value=value):
            for i in range(5):
                window_ref[i * rows : (i + 1) * rows, :] = six[i + value][:rows, :]


def forward_kernel(
    heads, total, where_ref, dil_ref, lens_ref, own_ref, far_ref, w_ref,
    part_ref, probs_out, attn_out, win_out, back_out, logs_ref,
    hold_ref, win_ref, back_ref, probs_ref, attn_ref, sems,
):
    groups, span = part_ref.shape[0], part_ref.shape[2]
    blocks = [slice(b * span, (b + 1) * span) for b in range(groups)]
    rows = own_ref.shape[1]
    width = own_ref.shape[2] // 3
    hd = width // heads
    keys = win_ref.shape[0]
    slab = where_ref[0]
    take_window(lax.rem(slab, 2), own_ref, far_ref, rows, win_ref)
    copies = [pltpu.make_async_copy(win_ref, win_out, sems.at[groups])]
    copies[0].start()
    mine = slice(2 * rows, 3 * rows)
    first = slab * rows
    row_idx = lax.broadcasted_iota(jnp.int32, (1, keys), 1) + (first - 2 * rows)
    col_idx = lax.broadcasted_iota(jnp.int32, (rows, 1), 0) + first
    row_pos, col_pos = row_idx.astype(F32), col_idx.astype(F32)
    row_doc, col_doc = document_codes(lens_ref[...].astype(F32), row_pos, col_pos)
    inside = (row_pos >= 0.0) & (row_pos < float(total))
    distance = jnp.abs(col_pos - row_pos)
    for h in range(heads):
        stride = dil_ref[h].astype(F32)

        def residue(pos, doc):
            steps = jnp.floor((pos + 0.5) / jnp.full(pos.shape, stride))
            return doc * 8.0 + (pos - steps * stride)

        row_code = jnp.where(inside, residue(row_pos, row_doc), -1.0)
        col_code = residue(col_pos, col_doc)
        mask = (row_code == col_code) & (distance <= stride * float(HALF))
        cols = slice(h * hd, (h + 1) * hd)
        vcols = slice(width + h * hd, width + (h + 1) * hd)
        qcols = slice(2 * width + h * hd, 2 * width + (h + 1) * hd)
        s = dot(win_ref[mine, qcols], win_ref[:, cols], ((1,), (1,))) * (hd**-0.5)
        s = jnp.where(mask, s, -jnp.inf)
        top = jnp.max(s, axis=1, keepdims=True)
        e = jnp.exp(s - top)
        norm = jnp.sum(e, axis=1, keepdims=True)
        probs = (e * (1.0 / norm)).astype(BF)
        probs_ref[h] = probs
        logs_ref[h] = as_row(top + jnp.log(norm))
        attn_ref[:, cols] = dot(probs, win_ref[:, vcols], ((1,), (0,))).astype(BF)
        back = dot(win_ref[mine, cols], win_ref[:, qcols], ((1,), (1,))) * (hd**-0.5)
        back_ref[h] = jnp.where(mask, back, -jnp.inf)
    copies.append(pltpu.make_async_copy(back_ref, back_out, sems.at[groups + 1]))
    copies.append(pltpu.make_async_copy(probs_ref, probs_out, sems.at[groups + 2]))
    copies.append(pltpu.make_async_copy(attn_ref, attn_out, sems.at[groups + 3]))
    for c in copies[1:]:
        c.start()
    attn = attn_ref[...]
    for b in range(groups):
        hold_ref[b] = dot(attn, w_ref[:, blocks[b]], ((1,), (0,))).astype(BF)
        copies.append(pltpu.make_async_copy(hold_ref.at[b], part_ref.at[b], sems.at[b]))
        copies[-1].start()
    for c in copies:
        c.wait()


def cotangent_kernel(heads, mg_ref, w_ref, attn_hbm, logs_ref, out_ref, delta_ref, attn_ref, sem):
    span = mg_ref.shape[2]
    fetch = pltpu.make_async_copy(attn_hbm, attn_ref, sem)
    fetch.start()
    rows, width = attn_ref.shape
    hd = width // heads
    total = jnp.zeros((rows, width), F32)
    for b in range(mg_ref.shape[0]):
        total = total + dot(mg_ref[b], w_ref[:, b * span : (b + 1) * span], ((1,), (1,)))
    grad = total.astype(BF)
    out_ref[:rows, :] = grad
    fetch.wait()
    product = grad.astype(F32) * attn_ref[...].astype(F32)
    extra = out_ref.shape[0] - rows
    place = lax.broadcasted_iota(jnp.int32, (extra, hd), 0)
    for h in range(heads):
        cols = slice(h * hd, (h + 1) * hd)
        delta = jnp.sum(product[:, cols], axis=1, keepdims=True)
        delta_ref[h] = delta
        stats = jnp.zeros((extra, hd), F32)
        for i, piece in enumerate(in_pieces(logs_ref[h]) + in_pieces(as_row(delta))):
            stats = jnp.where(place == i, piece, stats)
        out_ref[rows:, cols] = stats.astype(BF)


def query_kernel(heads, win_hbm, probs_hbm, ga_ref, delta_ref, dq_ref, win_ref, probs_ref, sems):
    rows, width = dq_ref.shape
    copies = [
        pltpu.make_async_copy(win_hbm.at[:, : 2 * width], win_ref, sems.at[0]),
        pltpu.make_async_copy(probs_hbm, probs_ref, sems.at[1]),
    ]
    for c in copies:
        c.start()
    for c in copies:
        c.wait()
    hd = width // heads
    for h in range(heads):
        cols = slice(h * hd, (h + 1) * hd)
        vcols = slice(width + h * hd, width + (h + 1) * hd)
        grad_prob = dot(ga_ref[:rows, cols], win_ref[:, vcols], ((1,), (1,)))
        slopes = (probs_ref[h].astype(F32) * (grad_prob - delta_ref[h])).astype(BF)
        dq_ref[:, cols] = (dot(slopes, win_ref[:, cols], ((1,), (0,))) * (hd**-0.5)).astype(BF)


def key_kernel(heads, where_ref, win_ref, back_ref, own_ref, far_ref, dk_ref, dv_ref, ga_ref):
    rows, width = dk_ref.shape
    hd = width // heads
    mine = slice(2 * rows, 3 * rows)
    core = lax.rem(where_ref[0], 2)
    take_window(core, own_ref, far_ref, rows, ga_ref)
    tails = [x[i, rows:, :].astype(F32) for x in (far_ref.at[0], own_ref, far_ref.at[1]) for i in range(2)]
    tails = [jnp.where(core == 0, tails[i], tails[i + 1]) for i in range(5)]
    stats = jnp.concatenate([jnp.stack([t[:, h * hd : (h + 1) * hd] for h in range(heads)]) for t in tails], axis=2)
    for h in range(heads):
        cols = slice(h * hd, (h + 1) * hd)
        vcols = slice(width + h * hd, width + (h + 1) * hd)
        qcols = slice(2 * width + h * hd, 2 * width + (h + 1) * hd)
        log_total = stats[h, 0:1] + stats[h, 1:2] + stats[h, 2:3]
        delta = stats[h, 3:4] + stats[h, 4:5] + stats[h, 5:6]
        weight = jnp.exp(back_ref[h] - log_total)
        grad_prob = dot(win_ref[mine, vcols], ga_ref[:, cols], ((1,), (1,)))
        slopes = (weight * (grad_prob - delta)).astype(BF)
        dk_ref[:, cols] = (dot(slopes, win_ref[:, qcols], ((1,), (0,))) * (hd**-0.5)).astype(BF)
        dv_ref[:, cols] = dot(weight.astype(BF), ga_ref[:, cols], ((1,), (0,))).astype(BF)


def mixed_kernel(x_ref, o_ref):
    total = x_ref[0].astype(F32)
    for c in range(1, x_ref.shape[0]):
        total = total + x_ref[c].astype(F32)
    o_ref[...] = total.astype(BF)


def to_neighbours(x):
    count = lax.axis_size("ctx")
    ahead = [(i, i + 2) for i in range(0, count - 2, 2)]
    back = [(i, i - 2) for i in range(3, count, 2)]
    return lax.ppermute(x, "ctx", ahead + back)


def in_chip(x):
    pairs = [[i, i + 1] for i in range(0, lax.axis_size("ctx"), 2)]
    return lax.all_gather(x, "ctx", axis=0, axis_index_groups=pairs)


def per_device(queries, keys, values, out_weight, mixed_grad, lengths, dilation):
    rows, width = queries.shape
    heads = dilation.shape[0]
    groups = lax.axis_size("head")
    span = mixed_grad.shape[1]
    total = rows * lax.axis_size("ctx")
    where = lax.axis_index("ctx").astype(jnp.int32).reshape(1)
    lens = lengths.reshape(1, -1)

    kvq, mgv = call(
        pack_kernel,
        [shape((rows, 3 * width), BF), shape((rows, span), BF)],
        [keys, values, queries, mixed_grad],
        "pack",
        scratch=[pltpu.SemaphoreType.DMA((4,))],
        hbm_in=(0, 1, 2, 3),
    )
    own2 = in_chip(kvq)
    near = to_neighbours(own2)
    (spread,) = call(
        spread_kernel,
        [shape((groups, rows, span), BF)],
        [mgv, own2],
        "spread",
        scratch=[pltpu.SemaphoreType.DMA((groups,))],
        hbm_out=(0,),
    )
    gathered = lax.all_to_all(spread, "head", 0, 0, tiled=True)
    far = in_chip(near)
    part, probs, attn, window, back, logs = call(
        functools.partial(forward_kernel, heads, total),
        [
            shape((groups, rows, span), BF),
            shape((heads, rows, 5 * rows), BF),
            shape((rows, width), BF),
            shape((5 * rows, 3 * width), BF),
            shape((heads, rows, 5 * rows), F32),
            shape((heads, 1, rows), F32),
        ],
        [where, dilation, lens, own2, far, out_weight],
        "forward",
        flops=80 * 2 * rows * width * (groups * span + 15 * rows),
        scratch=[
            pltpu.VMEM((groups, rows, span), BF),
            pltpu.VMEM((5 * rows, 3 * width), BF),
            pltpu.VMEM((heads, rows, 5 * rows), F32),
            pltpu.VMEM((heads, rows, 5 * rows), BF),
            pltpu.VMEM((rows, width), BF),
            pltpu.SemaphoreType.DMA((groups + 4,)),
        ],
        hbm_out=(0, 1, 2, 3, 4),
    )
    ga, delta = call(
        functools.partial(cotangent_kernel, heads),
        [shape((rows + 16, width), BF), shape((heads, rows, 1), F32)],
        [gathered, out_weight, attn, logs],
        "cotangent",
        flops=2 * rows * width * groups * span,
        scratch=[pltpu.VMEM((rows, width), BF), pltpu.SemaphoreType.DMA],
        hbm_in=(2,),
    )
    ga, part = lax.optimization_barrier((ga, part))
    ga2, ga = lax.optimization_barrier((in_chip(ga), ga))
    ga_near = to_neighbours(ga2)
    (dq,) = call(
        functools.partial(query_kernel, heads),
        [shape((rows, width), BF)],
        [window, probs, ga, delta],
        "query",
        flops=2 * rows * width * 10 * rows,
        scratch=[
            pltpu.VMEM((5 * rows, 2 * width), BF),
            pltpu.VMEM((heads, rows, 5 * rows), BF),
            pltpu.SemaphoreType.DMA((2,)),
        ],
        hbm_in=(0, 1),
    )
    summed = lax.all_to_all(part, "head", 0, 0, tiled=True)
    (mixed,) = call(mixed_kernel, [shape((rows, span), BF)], [summed], "mixed")
    arrived, mixed = lax.optimization_barrier((ga_near, mixed))
    dk, dv = call(
        functools.partial(key_kernel, heads),
        [shape((rows, width), BF), shape((rows, width), BF)],
        [where, window, back, ga2, in_chip(arrived)],
        "key",
        flops=2 * rows * width * 15 * rows,
        scratch=[pltpu.VMEM((5 * rows, width), BF)],
    )
    return mixed, dq, dk, dv


def solution(mesh):
    placed = (
        P("ctx", "head"),
        P("ctx", "head"),
        P("ctx", "head"),
        P("head", None),
        P("ctx", "head"),
        P(),
        P("head"),
    )
    return jax.shard_map(
        per_device,
        mesh=mesh,
        in_specs=placed,
        out_specs=(P("ctx", "head"), P("ctx", "head"), P("ctx", "head"), P("ctx", "head")),
        check_vma=False,
    )
```

```python
import functools

import jax
import jax.numpy as jnp
from jax import lax
from jax.experimental import pallas as pl
from jax.experimental.pallas import tpu as pltpu
from jax.sharding import PartitionSpec as P

HALF = 32
BF = jnp.bfloat16
F32 = jnp.float32
VMEM = pl.BlockSpec(memory_space=pltpu.VMEM)
SMEM = pl.BlockSpec(memory_space=pltpu.SMEM)
HBM = pl.BlockSpec(memory_space=pltpu.HBM)


def dot(a, b, dims):
    return lax.dot_general(a, b, (dims, ((), ())), preferred_element_type=F32)


def call(body, outs, ins, name, flops=0, scratch=(), hbm_in=(), hbm_out=()):
    moved = sum(x.size * x.dtype.itemsize for x in (*ins, *outs))
    held = [
        pltpu.with_memory_space_constraint(x, pltpu.HBM) if i in hbm_in else x
        for i, x in enumerate(ins)
    ]
    return pl.pallas_call(
        body,
        out_shape=[pltpu.HBM(x.shape, x.dtype) if i in hbm_out else x for i, x in enumerate(outs)],
        in_specs=[SMEM if x.ndim == 1 else HBM if i in hbm_in else VMEM for i, x in enumerate(ins)],
        out_specs=[HBM if i in hbm_out else VMEM for i in range(len(outs))],
        scratch_shapes=scratch,
        compiler_params=pltpu.CompilerParams(vmem_limit_bytes=24 << 20),
        cost_estimate=pl.CostEstimate(flops=flops, bytes_accessed=moved, transcendentals=0),
        name=name,
    )(*held)


def shape(dims, dtype):
    return jax.ShapeDtypeStruct(dims, dtype)


def pack_kernel(k_ref, v_ref, q_ref, mg_ref, kvq_ref, mgv_ref, sems):
    w = k_ref.shape[1]
    copies = [pltpu.make_async_copy(mg_ref, mgv_ref, sems.at[3])]
    for i, x_ref in enumerate((k_ref, v_ref, q_ref)):
        part = kvq_ref.at[:, i * w : (i + 1) * w]
        copies.append(pltpu.make_async_copy(x_ref, part, sems.at[i]))
    for c in copies:
        c.start()
    for c in copies:
        c.wait()


def spread_kernel(mg_ref, after_ref, all_ref, sems):
    copies = [
        pltpu.make_async_copy(mg_ref, all_ref.at[b], sems.at[b]) for b in range(all_ref.shape[0])
    ]
    for c in copies:
        c.start()
    for c in copies:
        c.wait()


def as_row(col):
    n = col.shape[0]
    down = lax.broadcasted_iota(jnp.int32, (n, n), 0)
    across = lax.broadcasted_iota(jnp.int32, (n, n), 1)
    return jnp.sum(jnp.where(down == across, col, 0.0), axis=0, keepdims=True)


def in_pieces(x):
    pieces = []
    for _ in range(3):
        piece = x.astype(BF).astype(F32)
        pieces.append(piece)
        x = x - piece
    return pieces


def document_codes(lens, row_pos, col_pos):
    n = lens.shape[1]
    down = lax.broadcasted_iota(jnp.int32, (n, n), 0)
    across = lax.broadcasted_iota(jnp.int32, (n, n), 1)
    wide = jnp.broadcast_to(lens, (n, n))
    ends_col = jnp.sum(jnp.where(across <= down, wide, 0.0), axis=1, keepdims=True)
    lens_col = jnp.sum(jnp.where(across == down, wide, 0.0), axis=1, keepdims=True)
    ends_row = jnp.sum(jnp.where(down <= across, lens_col, 0.0), axis=0, keepdims=True)
    row_doc = jnp.sum(jnp.where(row_pos >= ends_col, 1.0, 0.0), axis=0, keepdims=True)
    col_doc = jnp.sum(jnp.where(col_pos >= ends_row, 1.0, 0.0), axis=1, keepdims=True)
    return row_doc, col_doc


def take_window(core, own_ref, far_ref, rows, window_ref):
    six = [x.at[i] for x in (far_ref.at[0], own_ref, far_ref.at[1]) for i in range(2)]
    for value in range(2):

        @pl.when(core == value)
        def _(value=value):
            for i in range(5):
                window_ref[i * rows : (i + 1) * rows, :] = six[i + value][:rows, :]


def forward_kernel(
    heads, total, where_ref, dil_ref, lens_ref, own_ref, far_ref, w_ref,
    part_ref, probs_out, attn_out, win_out, back_out, logs_ref,
    hold_ref, win_ref, back_ref, probs_ref, attn_ref, sems,
):
    groups, span = part_ref.shape[0], part_ref.shape[2]
    blocks = [slice(b * span, (b + 1) * span) for b in range(groups)]
    rows = own_ref.shape[1]
    width = own_ref.shape[2] // 3
    hd = width // heads
    keys = win_ref.shape[0]
    slab = where_ref[0]
    take_window(lax.rem(slab, 2), own_ref, far_ref, rows, win_ref)
    copies = [pltpu.make_async_copy(win_ref, win_out, sems.at[groups])]
    copies[0].start()
    mine = slice(2 * rows, 3 * rows)
    first = slab * rows
    row_idx = lax.broadcasted_iota(jnp.int32, (1, keys), 1) + (first - 2 * rows)
    col_idx = lax.broadcasted_iota(jnp.int32, (rows, 1), 0) + first
    row_pos, col_pos = row_idx.astype(F32), col_idx.astype(F32)
    row_doc, col_doc = document_codes(lens_ref[...].astype(F32), row_pos, col_pos)
    inside = (row_pos >= 0.0) & (row_pos < float(total))
    distance = jnp.abs(col_pos - row_pos)
    for h in range(heads):
        stride = dil_ref[h].astype(F32)

        def residue(pos, doc):
            steps = jnp.floor((pos + 0.5) / jnp.full(pos.shape, stride))
            return doc * 8.0 + (pos - steps * stride)

        row_code = jnp.where(inside, residue(row_pos, row_doc), -1.0)
        col_code = residue(col_pos, col_doc)
        mask = (row_code == col_code) & (distance <= stride * float(HALF))
        cols = slice(h * hd, (h + 1) * hd)
        vcols = slice(width + h * hd, width + (h + 1) * hd)
        qcols = slice(2 * width + h * hd, 2 * width + (h + 1) * hd)
        s = dot(win_ref[mine, qcols], win_ref[:, cols], ((1,), (1,))) * (hd**-0.5)
        s = jnp.where(mask, s, -jnp.inf)
        top = jnp.max(s, axis=1, keepdims=True)
        e = jnp.exp(s - top)
        norm = jnp.sum(e, axis=1, keepdims=True)
        probs = (e * (1.0 / norm)).astype(BF)
        probs_ref[h] = probs
        logs_ref[h] = as_row(top + jnp.log(norm))
        attn_ref[:, cols] = dot(probs, win_ref[:, vcols], ((1,), (0,))).astype(BF)
        back = dot(win_ref[mine, cols], win_ref[:, qcols], ((1,), (1,))) * (hd**-0.5)
        back_ref[h] = jnp.where(mask, back, -jnp.inf)
    copies.append(pltpu.make_async_copy(back_ref, back_out, sems.at[groups + 1]))
    copies.append(pltpu.make_async_copy(probs_ref, probs_out, sems.at[groups + 2]))
    copies.append(pltpu.make_async_copy(attn_ref, attn_out, sems.at[groups + 3]))
    for c in copies[1:]:
        c.start()
    attn = attn_ref[...]
    for b in range(groups):
        hold_ref[b] = dot(attn, w_ref[:, blocks[b]], ((1,), (0,))).astype(BF)
        copies.append(pltpu.make_async_copy(hold_ref.at[b], part_ref.at[b], sems.at[b]))
        copies[-1].start()
    for c in copies:
        c.wait()


def cotangent_kernel(heads, mg_ref, w_ref, attn_hbm, logs_ref, out_ref, delta_ref, attn_ref, sem):
    span = mg_ref.shape[2]
    fetch = pltpu.make_async_copy(attn_hbm, attn_ref, sem)
    fetch.start()
    rows, width = attn_ref.shape
    hd = width // heads
    total = jnp.zeros((rows, width), F32)
    for b in range(mg_ref.shape[0]):
        total = total + dot(mg_ref[b], w_ref[:, b * span : (b + 1) * span], ((1,), (1,)))
    grad = total.astype(BF)
    out_ref[:rows, :] = grad
    fetch.wait()
    product = grad.astype(F32) * attn_ref[...].astype(F32)
    extra = out_ref.shape[0] - rows
    place = lax.broadcasted_iota(jnp.int32, (extra, hd), 0)
    for h in range(heads):
        cols = slice(h * hd, (h + 1) * hd)
        delta = jnp.sum(product[:, cols], axis=1, keepdims=True)
        delta_ref[h] = delta
        stats = jnp.zeros((extra, hd), F32)
        for i, piece in enumerate(in_pieces(logs_ref[h]) + in_pieces(as_row(delta))):
            stats = jnp.where(place == i, piece, stats)
        out_ref[rows:, cols] = stats.astype(BF)


def query_kernel(heads, win_hbm, probs_hbm, ga_ref, delta_ref, dq_ref, win_ref, probs_ref, sems):
    rows, width = dq_ref.shape
    copies = [
        pltpu.make_async_copy(win_hbm.at[:, : 2 * width], win_ref, sems.at[0]),
        pltpu.make_async_copy(probs_hbm, probs_ref, sems.at[1]),
    ]
    for c in copies:
        c.start()
    for c in copies:
        c.wait()
    hd = width // heads
    for h in range(heads):
        cols = slice(h * hd, (h + 1) * hd)
        vcols = slice(width + h * hd, width + (h + 1) * hd)
        grad_prob = dot(ga_ref[:rows, cols], win_ref[:, vcols], ((1,), (1,)))
        slopes = (probs_ref[h].astype(F32) * (grad_prob - delta_ref[h])).astype(BF)
        dq_ref[:, cols] = (dot(slopes, win_ref[:, cols], ((1,), (0,))) * (hd**-0.5)).astype(BF)


def key_kernel(
    heads, where_ref, win_ref, back_ref, pair_ref, prev_ref, cross_ref, next_ref,
    dk_ref, dv_ref, ga_ref, tail_ref,
):
    rows, width = dk_ref.shape
    hd = width // heads
    mine = slice(2 * rows, 3 * rows)
    core = lax.rem(where_ref[0], 2)
    pair = [pair_ref.at[0], pair_ref.at[1]]
    orders = (
        (prev_ref, cross_ref, pair[0], pair[1], next_ref),
        (prev_ref, pair[0], pair[1], cross_ref, next_ref),
    )
    for value in range(2):

        @pl.when(core == value)
        def _(value=value):
            for i, x in enumerate(orders[value]):
                ga_ref[i * rows : (i + 1) * rows, :] = x[:rows, :]
                tail_ref[i] = x[rows:, :]

    tails = [tail_ref[i].astype(F32) for i in range(5)]
    stats = jnp.concatenate([jnp.stack([t[:, h * hd : (h + 1) * hd] for h in range(heads)]) for t in tails], axis=2)
    for h in range(heads):
        cols = slice(h * hd, (h + 1) * hd)
        vcols = slice(width + h * hd, width + (h + 1) * hd)
        qcols = slice(2 * width + h * hd, 2 * width + (h + 1) * hd)
        log_total = stats[h, 0:1] + stats[h, 1:2] + stats[h, 2:3]
        delta = stats[h, 3:4] + stats[h, 4:5] + stats[h, 5:6]
        weight = jnp.exp(back_ref[h] - log_total)
        grad_prob = dot(win_ref[mine, vcols], ga_ref[:, cols], ((1,), (1,)))
        slopes = (weight * (grad_prob - delta)).astype(BF)
        dk_ref[:, cols] = (dot(slopes, win_ref[:, qcols], ((1,), (0,))) * (hd**-0.5)).astype(BF)
        dv_ref[:, cols] = dot(weight.astype(BF), ga_ref[:, cols], ((1,), (0,))).astype(BF)


def mixed_kernel(x_ref, o_ref):
    total = x_ref[0].astype(F32)
    for c in range(1, x_ref.shape[0]):
        total = total + x_ref[c].astype(F32)
    o_ref[...] = total.astype(BF)


def to_neighbours(x):
    count = lax.axis_size("ctx")
    ahead = [(i, i + 2) for i in range(0, count - 2, 2)]
    back = [(i, i - 2) for i in range(3, count, 2)]
    return lax.ppermute(x, "ctx", ahead + back)


def in_chip(x):
    pairs = [[i, i + 1] for i in range(0, lax.axis_size("ctx"), 2)]
    return lax.all_gather(x, "ctx", axis=0, axis_index_groups=pairs)


def per_device(queries, keys, values, out_weight, mixed_grad, lengths, dilation):
    rows, width = queries.shape
    heads = dilation.shape[0]
    groups = lax.axis_size("head")
    span = mixed_grad.shape[1]
    total = rows * lax.axis_size("ctx")
    where = lax.axis_index("ctx").astype(jnp.int32).reshape(1)
    lens = lengths.reshape(1, -1)

    kvq, mgv = call(
        pack_kernel,
        [shape((rows, 3 * width), BF), shape((rows, span), BF)],
        [keys, values, queries, mixed_grad],
        "pack",
        scratch=[pltpu.SemaphoreType.DMA((4,))],
        hbm_in=(0, 1, 2, 3),
    )
    own2 = in_chip(kvq)
    near = to_neighbours(own2)
    (spread,) = call(
        spread_kernel,
        [shape((groups, rows, span), BF)],
        [mgv, own2],
        "spread",
        scratch=[pltpu.SemaphoreType.DMA((groups,))],
        hbm_out=(0,),
    )
    gathered = lax.all_to_all(spread, "head", 0, 0, tiled=True)
    far = in_chip(near)
    part, probs, attn, window, back, logs = call(
        functools.partial(forward_kernel, heads, total),
        [
            shape((groups, rows, span), BF),
            shape((heads, rows, 5 * rows), BF),
            shape((rows, width), BF),
            shape((5 * rows, 3 * width), BF),
            shape((heads, rows, 5 * rows), F32),
            shape((heads, 1, rows), F32),
        ],
        [where, dilation, lens, own2, far, out_weight],
        "forward",
        flops=80 * 2 * rows * width * (groups * span + 15 * rows),
        scratch=[
            pltpu.VMEM((groups, rows, span), BF),
            pltpu.VMEM((5 * rows, 3 * width), BF),
            pltpu.VMEM((heads, rows, 5 * rows), F32),
            pltpu.VMEM((heads, rows, 5 * rows), BF),
            pltpu.VMEM((rows, width), BF),
            pltpu.SemaphoreType.DMA((groups + 4,)),
        ],
        hbm_out=(0, 1, 2, 3, 4),
    )
    ga, delta = call(
        functools.partial(cotangent_kernel, heads),
        [shape((rows + 16, width), BF), shape((heads, rows, 1), F32)],
        [gathered, out_weight, attn, logs],
        "cotangent",
        flops=2 * rows * width * groups * span,
        scratch=[pltpu.VMEM((rows, width), BF), pltpu.SemaphoreType.DMA],
        hbm_in=(2,),
    )
    ga, part = lax.optimization_barrier((ga, part))
    ga2, ga = lax.optimization_barrier((in_chip(ga), ga))
    count = lax.axis_size("ctx")
    swaps = [(i, i + 1) for i in range(1, count - 1, 2)]
    prev_ga = lax.ppermute(ga, "ctx", [(i, i + 2) for i in range(count - 2)])
    next_ga = lax.ppermute(ga, "ctx", [(i + 2, i) for i in range(count - 2)])
    cross_ga = lax.ppermute(ga, "ctx", swaps + [(b, a) for a, b in swaps])
    (dq,) = call(
        functools.partial(query_kernel, heads),
        [shape((rows, width), BF)],
        [window, probs, ga, delta],
        "query",
        flops=2 * rows * width * 10 * rows,
        scratch=[
            pltpu.VMEM((5 * rows, 2 * width), BF),
            pltpu.VMEM((heads, rows, 5 * rows), BF),
            pltpu.SemaphoreType.DMA((2,)),
        ],
        hbm_in=(0, 1),
    )
    summed = lax.all_to_all(part, "head", 0, 0, tiled=True)
    (mixed,) = call(mixed_kernel, [shape((rows, span), BF)], [summed], "mixed")
    next_ga, mixed = lax.optimization_barrier((next_ga, mixed))
    dk, dv = call(
        functools.partial(key_kernel, heads),
        [shape((rows, width), BF), shape((rows, width), BF)],
        [where, window, back, ga2, prev_ga, cross_ga, next_ga],
        "key",
        flops=2 * rows * width * 15 * rows,
        scratch=[pltpu.VMEM((5 * rows, width), BF), pltpu.VMEM((5, 16, width), BF)],
    )
    return mixed, dq, dk, dv


def solution(mesh):
    placed = (
        P("ctx", "head"),
        P("ctx", "head"),
        P("ctx", "head"),
        P("head", None),
        P("ctx", "head"),
        P(),
        P("head"),
    )
    return jax.shard_map(
        per_device,
        mesh=mesh,
        in_specs=placed,
        out_specs=(P("ctx", "head"), P("ctx", "head"), P("ctx", "head"), P("ctx", "head")),
        check_vma=False,
    )
```

```python
import functools

import jax
import jax.numpy as jnp
from jax import lax
from jax.experimental import pallas as pl
from jax.experimental.pallas import tpu as pltpu
from jax.sharding import PartitionSpec as P

HALF = 32
BF = jnp.bfloat16
F32 = jnp.float32
VMEM = pl.BlockSpec(memory_space=pltpu.VMEM)
SMEM = pl.BlockSpec(memory_space=pltpu.SMEM)
HBM = pl.BlockSpec(memory_space=pltpu.HBM)


def dot(a, b, dims):
    return lax.dot_general(a, b, (dims, ((), ())), preferred_element_type=F32)


def call(body, outs, ins, name, flops=0, scratch=(), hbm_in=(), hbm_out=()):
    moved = sum(x.size * x.dtype.itemsize for x in (*ins, *outs))
    held = [
        pltpu.with_memory_space_constraint(x, pltpu.HBM) if i in hbm_in else x
        for i, x in enumerate(ins)
    ]
    return pl.pallas_call(
        body,
        out_shape=[pltpu.HBM(x.shape, x.dtype) if i in hbm_out else x for i, x in enumerate(outs)],
        in_specs=[SMEM if x.ndim == 1 else HBM if i in hbm_in else VMEM for i, x in enumerate(ins)],
        out_specs=[HBM if i in hbm_out else VMEM for i in range(len(outs))],
        scratch_shapes=scratch,
        compiler_params=pltpu.CompilerParams(vmem_limit_bytes=24 << 20),
        cost_estimate=pl.CostEstimate(flops=flops, bytes_accessed=moved, transcendentals=0),
        name=name,
    )(*held)


def shape(dims, dtype):
    return jax.ShapeDtypeStruct(dims, dtype)


def pack_kernel(k_ref, v_ref, q_ref, mg_ref, kvq_ref, mgv_ref, sems):
    w = k_ref.shape[1]
    copies = [pltpu.make_async_copy(mg_ref, mgv_ref, sems.at[3])]
    for i, x_ref in enumerate((k_ref, v_ref, q_ref)):
        part = kvq_ref.at[:, i * w : (i + 1) * w]
        copies.append(pltpu.make_async_copy(x_ref, part, sems.at[i]))
    for c in copies:
        c.start()
    for c in copies:
        c.wait()


def spread_kernel(mg_ref, after_ref, all_ref, sems):
    copies = [
        pltpu.make_async_copy(mg_ref, all_ref.at[b], sems.at[b]) for b in range(all_ref.shape[0])
    ]
    for c in copies:
        c.start()
    for c in copies:
        c.wait()


def as_row(col):
    n = col.shape[0]
    down = lax.broadcasted_iota(jnp.int32, (n, n), 0)
    across = lax.broadcasted_iota(jnp.int32, (n, n), 1)
    return jnp.sum(jnp.where(down == across, col, 0.0), axis=0, keepdims=True)


def in_pieces(x):
    pieces = []
    for _ in range(3):
        piece = x.astype(BF).astype(F32)
        pieces.append(piece)
        x = x - piece
    return pieces


def document_codes(lens, row_pos, col_pos):
    n = lens.shape[1]
    down = lax.broadcasted_iota(jnp.int32, (n, n), 0)
    across = lax.broadcasted_iota(jnp.int32, (n, n), 1)
    wide = jnp.broadcast_to(lens, (n, n))
    ends_col = jnp.sum(jnp.where(across <= down, wide, 0.0), axis=1, keepdims=True)
    lens_col = jnp.sum(jnp.where(across == down, wide, 0.0), axis=1, keepdims=True)
    ends_row = jnp.sum(jnp.where(down <= across, lens_col, 0.0), axis=0, keepdims=True)
    row_doc = jnp.sum(jnp.where(row_pos >= ends_col, 1.0, 0.0), axis=0, keepdims=True)
    col_doc = jnp.sum(jnp.where(col_pos >= ends_row, 1.0, 0.0), axis=1, keepdims=True)
    return row_doc, col_doc


def take_window(core, own_ref, far_ref, rows, window_ref):
    six = [x.at[i] for x in (far_ref.at[0], own_ref, far_ref.at[1]) for i in range(2)]
    for value in range(2):

        @pl.when(core == value)
        def _(value=value):
            for i in range(5):
                window_ref[i * rows : (i + 1) * rows, :] = six[i + value][:rows, :]


def forward_kernel(
    heads, total, where_ref, dil_ref, lens_ref, own_ref, far_ref, w_ref,
    part_ref, probs_out, attn_out, win_out, back_out, logs_ref,
    hold_ref, win_ref, back_ref, probs_ref, attn_ref, sems,
):
    groups, span = part_ref.shape[0], part_ref.shape[2]
    blocks = [slice(b * span, (b + 1) * span) for b in range(groups)]
    rows = own_ref.shape[1]
    width = own_ref.shape[2] // 3
    hd = width // heads
    keys = win_ref.shape[0]
    slab = where_ref[0]
    take_window(lax.rem(slab, 2), own_ref, far_ref, rows, win_ref)
    copies = [pltpu.make_async_copy(win_ref, win_out, sems.at[groups])]
    copies[0].start()
    mine = slice(2 * rows, 3 * rows)
    first = slab * rows
    row_idx = lax.broadcasted_iota(jnp.int32, (1, keys), 1) + (first - 2 * rows)
    col_idx = lax.broadcasted_iota(jnp.int32, (rows, 1), 0) + first
    row_pos, col_pos = row_idx.astype(F32), col_idx.astype(F32)
    row_doc, col_doc = document_codes(lens_ref[...].astype(F32), row_pos, col_pos)
    inside = (row_pos >= 0.0) & (row_pos < float(total))
    distance = jnp.abs(col_pos - row_pos)
    for h in range(heads):
        stride = dil_ref[h].astype(F32)

        def residue(pos, doc):
            steps = jnp.floor((pos + 0.5) / jnp.full(pos.shape, stride))
            return doc * 8.0 + (pos - steps * stride)

        row_code = jnp.where(inside, residue(row_pos, row_doc), -1.0)
        col_code = residue(col_pos, col_doc)
        mask = (row_code == col_code) & (distance <= stride * float(HALF))
        cols = slice(h * hd, (h + 1) * hd)
        vcols = slice(width + h * hd, width + (h + 1) * hd)
        qcols = slice(2 * width + h * hd, 2 * width + (h + 1) * hd)
        s = dot(win_ref[mine, qcols], win_ref[:, cols], ((1,), (1,))) * (hd**-0.5)
        s = jnp.where(mask, s, -jnp.inf)
        top = jnp.max(s, axis=1, keepdims=True)
        e = jnp.exp(s - top)
        norm = jnp.sum(e, axis=1, keepdims=True)
        probs = (e * (1.0 / norm)).astype(BF)
        probs_ref[h] = probs
        logs_ref[h] = as_row(top + jnp.log(norm))
        attn_ref[:, cols] = dot(probs, win_ref[:, vcols], ((1,), (0,))).astype(BF)
        back = dot(win_ref[mine, cols], win_ref[:, qcols], ((1,), (1,))) * (hd**-0.5)
        back_ref[h] = jnp.where(mask, back, -jnp.inf)
    copies.append(pltpu.make_async_copy(back_ref, back_out, sems.at[groups + 1]))
    copies.append(pltpu.make_async_copy(probs_ref, probs_out, sems.at[groups + 2]))
    copies.append(pltpu.make_async_copy(attn_ref, attn_out, sems.at[groups + 3]))
    for c in copies[1:]:
        c.start()
    attn = attn_ref[...]
    for b in range(groups):
        hold_ref[b] = dot(attn, w_ref[:, blocks[b]], ((1,), (0,))).astype(BF)
        copies.append(pltpu.make_async_copy(hold_ref.at[b], part_ref.at[b], sems.at[b]))
        copies[-1].start()
    for c in copies:
        c.wait()


def cotangent_kernel(heads, mg_ref, w_ref, attn_hbm, logs_ref, out_ref, delta_ref, attn_ref, sem):
    span = mg_ref.shape[2]
    fetch = pltpu.make_async_copy(attn_hbm, attn_ref, sem)
    fetch.start()
    rows, width = attn_ref.shape
    hd = width // heads
    total = jnp.zeros((rows, width), F32)
    for b in range(mg_ref.shape[0]):
        total = total + dot(mg_ref[b], w_ref[:, b * span : (b + 1) * span], ((1,), (1,)))
    grad = total.astype(BF)
    out_ref[:rows, :] = grad
    fetch.wait()
    product = grad.astype(F32) * attn_ref[...].astype(F32)
    extra = out_ref.shape[0] - rows
    place = lax.broadcasted_iota(jnp.int32, (extra, hd), 0)
    for h in range(heads):
        cols = slice(h * hd, (h + 1) * hd)
        delta = jnp.sum(product[:, cols], axis=1, keepdims=True)
        delta_ref[h] = delta
        stats = jnp.zeros((extra, hd), F32)
        for i, piece in enumerate(in_pieces(logs_ref[h]) + in_pieces(as_row(delta))):
            stats = jnp.where(place == i, piece, stats)
        out_ref[rows:, cols] = stats.astype(BF)


def query_kernel(heads, win_hbm, probs_hbm, ga_ref, delta_ref, dq_ref, win_ref, probs_ref, sems):
    rows, width = dq_ref.shape
    copies = [
        pltpu.make_async_copy(win_hbm.at[:, : 2 * width], win_ref, sems.at[0]),
        pltpu.make_async_copy(probs_hbm, probs_ref, sems.at[1]),
    ]
    for c in copies:
        c.start()
    for c in copies:
        c.wait()
    hd = width // heads
    for h in range(heads):
        cols = slice(h * hd, (h + 1) * hd)
        vcols = slice(width + h * hd, width + (h + 1) * hd)
        grad_prob = dot(ga_ref[:rows, cols], win_ref[:, vcols], ((1,), (1,)))
        slopes = (probs_ref[h].astype(F32) * (grad_prob - delta_ref[h])).astype(BF)
        dq_ref[:, cols] = (dot(slopes, win_ref[:, cols], ((1,), (0,))) * (hd**-0.5)).astype(BF)


def key_kernel(heads, where_ref, win_ref, back_ref, own_ref, far_ref, dk_ref, dv_ref, ga_ref):
    rows, width = dk_ref.shape
    hd = width // heads
    mine = slice(2 * rows, 3 * rows)
    core = lax.rem(where_ref[0], 2)
    take_window(core, own_ref, far_ref, rows, ga_ref)
    tails = [x[i, rows:, :].astype(F32) for x in (far_ref.at[0], own_ref, far_ref.at[1]) for i in range(2)]
    tails = [jnp.where(core == 0, tails[i], tails[i + 1]) for i in range(5)]
    stats = jnp.concatenate([jnp.stack([t[:, h * hd : (h + 1) * hd] for h in range(heads)]) for t in tails], axis=2)
    for h in range(heads):
        cols = slice(h * hd, (h + 1) * hd)
        vcols = slice(width + h * hd, width + (h + 1) * hd)
        qcols = slice(2 * width + h * hd, 2 * width + (h + 1) * hd)
        log_total = stats[h, 0:1] + stats[h, 1:2] + stats[h, 2:3]
        delta = stats[h, 3:4] + stats[h, 4:5] + stats[h, 5:6]
        weight = jnp.exp(back_ref[h] - log_total)
        grad_prob = dot(win_ref[mine, vcols], ga_ref[:, cols], ((1,), (1,)))
        slopes = (weight * (grad_prob - delta)).astype(BF)
        dk_ref[:, cols] = (dot(slopes, win_ref[:, qcols], ((1,), (0,))) * (hd**-0.5)).astype(BF)
        dv_ref[:, cols] = dot(weight.astype(BF), ga_ref[:, cols], ((1,), (0,))).astype(BF)


def mixed_kernel(x_ref, o_ref):
    total = x_ref[0].astype(F32)
    for c in range(1, x_ref.shape[0]):
        total = total + x_ref[c].astype(F32)
    o_ref[...] = total.astype(BF)


def to_neighbours(x):
    count = lax.axis_size("ctx")
    ahead = [(i, i + 2) for i in range(0, count - 2, 2)]
    back = [(i, i - 2) for i in range(3, count, 2)]
    return lax.ppermute(x, "ctx", ahead + back)


def in_chip(x):
    pairs = [[i, i + 1] for i in range(0, lax.axis_size("ctx"), 2)]
    return lax.all_gather(x, "ctx", axis=0, axis_index_groups=pairs)


def per_device(queries, keys, values, out_weight, mixed_grad, lengths, dilation):
    rows, width = queries.shape
    heads = dilation.shape[0]
    groups = lax.axis_size("head")
    span = mixed_grad.shape[1]
    total = rows * lax.axis_size("ctx")
    where = lax.axis_index("ctx").astype(jnp.int32).reshape(1)
    lens = lengths.reshape(1, -1)

    kvq, mgv = call(
        pack_kernel,
        [shape((rows, 3 * width), BF), shape((rows, span), BF)],
        [keys, values, queries, mixed_grad],
        "pack",
        scratch=[pltpu.SemaphoreType.DMA((4,))],
        hbm_in=(0, 1, 2, 3),
    )
    own2 = in_chip(kvq)
    near = to_neighbours(own2)
    (spread,) = call(
        spread_kernel,
        [shape((groups, rows, span), BF)],
        [mgv, own2],
        "spread",
        scratch=[pltpu.SemaphoreType.DMA((groups,))],
        hbm_out=(0,),
    )
    gathered = lax.all_to_all(spread, "head", 0, 0, tiled=True)
    far = in_chip(near)
    part, probs, attn, window, back, logs = call(
        functools.partial(forward_kernel, heads, total),
        [
            shape((groups, rows, span), BF),
            shape((heads, rows, 5 * rows), BF),
            shape((rows, width), BF),
            shape((5 * rows, 3 * width), BF),
            shape((heads, rows, 5 * rows), F32),
            shape((heads, 1, rows), F32),
        ],
        [where, dilation, lens, own2, far, out_weight],
        "forward",
        flops=2 * rows * width * (groups * span + 15 * rows),
        scratch=[
            pltpu.VMEM((groups, rows, span), BF),
            pltpu.VMEM((5 * rows, 3 * width), BF),
            pltpu.VMEM((heads, rows, 5 * rows), F32),
            pltpu.VMEM((heads, rows, 5 * rows), BF),
            pltpu.VMEM((rows, width), BF),
            pltpu.SemaphoreType.DMA((groups + 4,)),
        ],
        hbm_out=(0, 1, 2, 3, 4),
    )
    ga, delta = call(
        functools.partial(cotangent_kernel, heads),
        [shape((rows + 16, width), BF), shape((heads, rows, 1), F32)],
        [gathered, out_weight, attn, logs],
        "cotangent",
        flops=2 * rows * width * groups * span,
        scratch=[pltpu.VMEM((rows, width), BF), pltpu.SemaphoreType.DMA],
        hbm_in=(2,),
    )
    ga, part = lax.optimization_barrier((ga, part))
    ga2, ga = lax.optimization_barrier((in_chip(ga), ga))
    ga_near = to_neighbours(ga2)
    (dq,) = call(
        functools.partial(query_kernel, heads),
        [shape((rows, width), BF)],
        [window, probs, ga, delta],
        "query",
        flops=2 * rows * width * 10 * rows,
        scratch=[
            pltpu.VMEM((5 * rows, 2 * width), BF),
            pltpu.VMEM((heads, rows, 5 * rows), BF),
            pltpu.SemaphoreType.DMA((2,)),
        ],
        hbm_in=(0, 1),
    )
    summed = lax.all_to_all(part, "head", 0, 0, tiled=True)
    (mixed,) = call(mixed_kernel, [shape((rows, span), BF)], [summed], "mixed")
    arrived, mixed = lax.optimization_barrier((ga_near, mixed))
    dk, dv = call(
        functools.partial(key_kernel, heads),
        [shape((rows, width), BF), shape((rows, width), BF)],
        [where, window, back, ga2, in_chip(arrived)],
        "key",
        flops=2 * rows * width * 15 * rows,
        scratch=[pltpu.VMEM((5 * rows, width), BF)],
    )
    return mixed, dq, dk, dv


def solution(mesh):
    placed = (
        P("ctx", "head"),
        P("ctx", "head"),
        P("ctx", "head"),
        P("head", None),
        P("ctx", "head"),
        P(),
        P("head"),
    )
    return jax.shard_map(
        per_device,
        mesh=mesh,
        in_specs=placed,
        out_specs=(P("ctx", "head"), P("ctx", "head"), P("ctx", "head"), P("ctx", "head")),
        check_vma=False,
    )
```
